32 devices in a mesh: req: 8 (over z, core), mlp: 4 (over y, x).
Axes of the slice: x: 2, y: 2, z: 4, core: 2. Of those that a mesh axis runs over, the one named last changes fastest.
Arguments:
- hidden_input: bfloat16 [3072, 4096], P('req', 'mlp'), may hold values from -6 to 6
- input_norm_gain: bfloat16 [4096], replicated, may hold values from 0.099609375 to 1.8984375
- query_norm_gain: bfloat16 [128], replicated, may hold values from 0.099609375 to 1.8984375
- key_norm_gain: bfloat16 [128], replicated, may hold values from 0.099609375 to 1.8984375
- query_weight: bfloat16 [4096, 4096], P('req', 'mlp'), may hold values from -0.09375 to 0.09375
- key_value_weight: bfloat16 [4096, 2, 1024], P('req'), may hold values from -0.09375 to 0.09375
- output_weight: bfloat16 [4096, 4, 1024], P('mlp', None, 'req'), may hold values from -0.09375 to 0.09375
- adapter_down_qkv: bfloat16 [16, 48, 4096], P('req', None, 'mlp'), may hold values from -0.09375 to 0.09375
- adapter_down_output: bfloat16 [16, 16, 4096], P('req', None, 'mlp'), may hold values from -0.09375 to 0.09375
- adapter_up_query: bfloat16 [16, 16, 4096], P('req', None, 'mlp'), may hold values from -1.5 to 1.5
- adapter_up_key_value: bfloat16 [16, 16, 2, 1024], P('req'), may hold values from -1.5 to 1.5
- adapter_up_output: bfloat16 [16, 16, 4096], P('req', None, 'mlp'), may hold values from -1.5 to 1.5
- pool: bfloat16 [4096, 2, 1024], P('req'), may hold values from -6 to 6
- lengths: int32 [8, 4], P('req'), may hold values from 1 to 192, 384 in all within a row
- cached_prefix_pages: int32 [8, 4], P('req'), may hold values from 0 to 8
- prefix_page_table: int32 [8, 4, 8], P('req'), may hold values from 0 to 7, each once within a row
- adapter_of_request: int32 [8, 4, 1], P('req'), may hold values from 0 to 15
- adapter_storage: int32 [16], replicated, may hold values from 0 to 15, each once
Outputs:
- attention_update: bfloat16 [3072, 4096], P('req', 'mlp')
- new_cache: bfloat16 [3072, 2, 1024], P('req', None, 'mlp')
The draws below stay inside these ranges and needn't reach their ends.
Inputs may be any that keep to these rules, and one draw needn't show every extreme that they name: The lengths of one index of req sum to 384, and the longest of them is 192. `prefix_page_table`: each row lists every page of its pool once. `adapter_of_request`: every adapter is used by some request. `adapter_storage`: each slot holds one adapter.
All inputs are finite; a program needn't handle non-finite values.
Results may differ from the reference program's by a relative error of at most 0.035.
Values may be sent and summed in bfloat16 or wider, within the bound.
No kernel may reach another device: no remote copies, remote signals or barrier semaphores. Data moves between devices by JAX's collectives and lax.ppermute only.
A program may use at most 128 MiB of HBM per device.

```python
import math
import jax
import jax.numpy as jnp
import numpy as np
from jax import lax

MODEL_WIDTH = 4096
QUERY_HEADS = 32
KEY_VALUE_HEADS = 8
HEAD_SIZE = 128
ADAPTER_RANK = 16
REQ_GRP = 4
GROUP_TOKENS = 384
PAGE = 64
POOL_PAGES = 8
ADAPTER_COUNT = 16
TOKENS = 3072
CACHED_TOKENS = 4096
N_REQ = 8
N_MLP = 4


def with_ends(drawn, rng, low, high):
    spot = [jax.random.randint(jax.random.fold_in(rng, axis), (), 0, length) for axis, length in enumerate(drawn.shape)]
    main_axis = drawn.shape.index(max(drawn.shape))
    next_to = spot[:main_axis] + [(spot[main_axis] + 1) % drawn.shape[main_axis]] + spot[main_axis + 1:]
    return drawn.at[tuple(spot)].set(low).at[tuple(next_to)].set(high)


def shard_levels(own_key, extent, pieces, low, top_value):
    loudness = 1.0
    for position, blocks in pieces:
        steps = jax.random.uniform(jax.random.fold_in(jax.random.fold_in(own_key, 6), position), (blocks,), jnp.float32, low / len(pieces), top_value / len(pieces))
        loudness = loudness * jnp.repeat(jnp.exp(steps), extent[position] // blocks).reshape((-1,) + (1,) * (len(extent) - 1 - position))
    return loudness


def different_ones(own_key, rows, amount, top, lift):
    order = jax.random.permutation(jax.random.fold_in(own_key, 1), amount)
    pull = order
    for power in range(3):
        pull = pull * pull // amount
    pull = pull * lift // amount
    lots = jax.random.randint(jax.random.fold_in(own_key, 2), (rows, amount), 0, 4096) + pull
    fixed_rows = jax.random.permutation(jax.random.fold_in(own_key, 3), rows)[jnp.arange(amount) % rows]
    lots = jnp.where(jnp.arange(rows)[:, None] == fixed_rows[None, :], 1 << 14, lots)
    priority = lots * amount + jnp.arange(amount)
    return lax.top_k(priority.astype(jnp.int32), top)[1].astype(jnp.int32)


def length_profile(amount, total, reach, skew):
    portions = [(1 << 20) // math.isqrt(grade ** skew) + 1 for grade in range(2, amount + 1)]
    surplus, holding = total - reach - (amount - 1), [1] * (amount - 1)
    while surplus > 0:
        candidates = [i for i in range(amount - 1) if holding[i] < reach]
        whole, remaining = sum([portions[i] for i in candidates]), surplus
        for i in candidates:
            extra = min(reach - holding[i], max(1, remaining * portions[i] // whole), surplus)
            holding[i] = holding[i] + extra
            surplus = surplus - extra
    return np.array([reach] + holding)


def uneven(stream_key, number_of, total, reach, lean):
    if number_of == 2:
        one = jax.random.randint(stream_key, (), max(1, total - reach), min(reach, total - 1) + 1)
        return jnp.stack([one, total - one])
    tallies = jnp.asarray(length_profile(number_of, total, reach, lean), jnp.int32)
    pairs = (number_of - 1) // 2
    donor, receiver = tallies[1:1 + 2 * pairs:2], tallies[2:2 + 2 * pairs:2]
    margin = jnp.minimum(donor - 1, reach - receiver)
    passed = jax.random.randint(jax.random.fold_in(stream_key, 1), (pairs,), 0, 1 << 20) % (margin + 1)
    tallies = tallies.at[1:1 + 2 * pairs:2].set(donor - passed).at[2:2 + 2 * pairs:2].set(receiver + passed)
    return tallies[jax.random.permutation(jax.random.fold_in(stream_key, 2), number_of)]


def centred(own_key, extent, deviation, most, split=(), kind=jnp.bfloat16):
    entries = jax.random.normal(own_key, extent, jnp.float32) * deviation
    if len(split) > 0:
        entries = shard_levels(own_key, extent, split, -0.22, 0.18) * entries
    return jnp.clip(entries, min=-most, max=most).astype(kind)


def setup_inputs(seed: int = 0) -> dict:
    seeds = jax.random.split(jax.random.key(seed), 19)
    return {
        "hidden_input": centred(seeds[0], (TOKENS, MODEL_WIDTH), 1.0, 6.0, ((0, 8), (1, 4))),
        "input_norm_gain": jnp.clip(1.0 + 0.18 * jax.random.normal(seeds[1], (MODEL_WIDTH,), jnp.float32), 0.099609375, 1.8984375).astype(jnp.bfloat16),
        "query_norm_gain": jnp.clip(1.0 + 0.18 * jax.random.normal(seeds[2], (HEAD_SIZE,), jnp.float32), 0.099609375, 1.8984375).astype(jnp.bfloat16),
        "key_norm_gain": jnp.clip(1.0 + 0.18 * jax.random.normal(seeds[3], (HEAD_SIZE,), jnp.float32), 0.099609375, 1.8984375).astype(jnp.bfloat16),
        "query_weight": centred(seeds[4], (MODEL_WIDTH, QUERY_HEADS * HEAD_SIZE), MODEL_WIDTH ** -0.5, 0.09375, ((0, 8), (1, 4))),
        "key_value_weight": centred(seeds[5], (MODEL_WIDTH, 2, KEY_VALUE_HEADS * HEAD_SIZE), MODEL_WIDTH ** -0.5, 0.09375, ((0, 8),)),
        "output_weight": centred(seeds[6], (QUERY_HEADS * HEAD_SIZE, N_MLP, MODEL_WIDTH // N_MLP), (QUERY_HEADS * HEAD_SIZE) ** -0.5, 0.09375, ((0, 4), (2, 8))),
        "adapter_down_qkv": centred(seeds[7], (ADAPTER_COUNT, 3 * ADAPTER_RANK, MODEL_WIDTH), MODEL_WIDTH ** -0.5, 0.09375, ((0, 8), (2, 4))),
        "adapter_down_output": centred(seeds[8], (ADAPTER_COUNT, ADAPTER_RANK, QUERY_HEADS * HEAD_SIZE), (QUERY_HEADS * HEAD_SIZE) ** -0.5, 0.09375, ((0, 8), (2, 4))),
        "adapter_up_query": centred(seeds[9], (ADAPTER_COUNT, ADAPTER_RANK, QUERY_HEADS * HEAD_SIZE), ADAPTER_RANK ** -0.5, 1.5, ((0, 8), (2, 4))),
        "adapter_up_key_value": centred(seeds[10], (ADAPTER_COUNT, ADAPTER_RANK, 2, KEY_VALUE_HEADS * HEAD_SIZE), ADAPTER_RANK ** -0.5, 1.5, ((0, 8),)),
        "adapter_up_output": centred(seeds[11], (ADAPTER_COUNT, ADAPTER_RANK, MODEL_WIDTH), ADAPTER_RANK ** -0.5, 1.5, ((0, 8), (2, 4))),
        "pool": centred(seeds[12], (CACHED_TOKENS, 2, KEY_VALUE_HEADS * HEAD_SIZE), 1.0, 6.0, ((0, 8),)),
        "lengths": jax.vmap(lambda own: uneven(own, REQ_GRP, GROUP_TOKENS, GROUP_TOKENS // 2, 2))(jax.random.split(seeds[13], N_REQ)).reshape((N_REQ, REQ_GRP)).astype(jnp.int32),
        "cached_prefix_pages": with_ends(jax.random.randint(seeds[14], (N_REQ, REQ_GRP), 0, POOL_PAGES + 1), jax.random.fold_in(seeds[14], 1), 0, POOL_PAGES).astype(jnp.int32),
        "prefix_page_table": jax.vmap(lambda own: jax.random.permutation(own, POOL_PAGES))(jax.random.split(seeds[15], N_REQ * REQ_GRP)).reshape((N_REQ, REQ_GRP, POOL_PAGES)).astype(jnp.int32),
        "adapter_of_request": different_ones(seeds[16], N_REQ * REQ_GRP, ADAPTER_COUNT, 1, 512).reshape((N_REQ, REQ_GRP, 1)),
        "adapter_storage": jax.random.permutation(seeds[17], ADAPTER_COUNT).astype(jnp.int32),
    }


epsilon = 1e-06
rope_base = 1000000.0

def root_mean_scale(values, gain_vec):
    mean_sq = lax.optimization_barrier(jnp.mean(values * values, axis=-1, keepdims=True))
    return values * lax.rsqrt(mean_sq + epsilon) * gain_vec.astype(jnp.float32)

def rotary_embed(values, token_positions):
    half_width = values.shape[-1] // 2
    inverse_freq = jnp.exp(jnp.arange(half_width, dtype=jnp.float32) * (-2.0 / values.shape[-1]) * math.log(rope_base))
    angles = token_positions.astype(jnp.float32)[:, None] * inverse_freq[None, :]
    cosine = jnp.cos(angles)[:, None, :]
    sine_part = jnp.sin(angles)[:, None, :]
    front = values[..., :half_width]
    back = values[..., half_width:]
    return jnp.concatenate([front * cosine - back * sine_part, back * cosine + front * sine_part], axis=-1)

def row_tables(lengths_row, prefix_row, page_rows, row_count):
    ends_at = jnp.cumsum(lengths_row).astype(jnp.int32)
    starts_at = (ends_at - lengths_row).astype(jnp.int32)
    row_ids = jnp.arange(row_count, dtype=jnp.int32)
    owners = lax.optimization_barrier(jnp.sum((row_ids[:, None] >= ends_at[None, :]).astype(jnp.int32), axis=1)).astype(jnp.int32)
    group_members = owners[:, None] == jnp.arange(lengths_row.shape[0], dtype=jnp.int32)[None, :]
    offsets = PAGE * prefix_row[None, :] + row_ids[:, None] - starts_at[None, :]
    token_positions = lax.optimization_barrier(jnp.sum(jnp.where(group_members, offsets, 0), axis=1)).astype(jnp.int32)
    page_ids = jnp.arange(page_rows.shape[1], dtype=jnp.int32)
    listed = (page_rows[:, :, None] == page_ids[None, None, :]) & (page_ids[None, :, None] < prefix_row[:, None, None])
    page_used = lax.optimization_barrier(jnp.sum(listed.astype(jnp.float32), axis=1))
    return (owners, group_members, token_positions, page_used)

def apply_adapter(lowrank_inner, group_members, chosen_up):
    masked = lowrank_inner.astype(jnp.float32)[:, None, :] * group_members.astype(jnp.float32)[:, :, None]
    return jnp.einsum('gjr,jrc->gc', masked, chosen_up.astype(jnp.float32))

def reference(hidden_input, input_norm_gain, query_norm_gain, key_norm_gain, query_weight, key_value_weight, output_weight, adapter_down_qkv, adapter_down_output, adapter_up_query, adapter_up_key_value, adapter_up_output, pool, lengths, cached_prefix_pages, prefix_page_table, adapter_of_request, adapter_storage):
    key_value_width = KEY_VALUE_HEADS * HEAD_SIZE
    block_rows = QUERY_HEADS * HEAD_SIZE // N_MLP
    w_blocks = output_weight.reshape(QUERY_HEADS * HEAD_SIZE, MODEL_WIDTH).astype(jnp.float32).reshape(N_MLP, block_rows, MODEL_WIDTH)
    pool_token_rows = POOL_PAGES * PAGE

    def one_group(inputs_group):
        tokens, lengths_row, prefix_row, page_rows, chosen, pool_index_group = inputs_group
        owners, group_members, token_positions, page_used = row_tables(lengths_row, prefix_row, page_rows, GROUP_TOKENS)
        slot_indices = jnp.take(adapter_storage, chosen, axis=0)
        normalized_input = root_mean_scale(tokens.astype(jnp.float32), input_norm_gain).astype(jnp.bfloat16)
        chosen_down = jnp.take(adapter_down_qkv, slot_indices, axis=0).astype(jnp.float32)
        low_terms = jnp.einsum('gd,jkd->gjk', normalized_input.astype(jnp.float32), chosen_down)
        lowrank_inner = lax.optimization_barrier(jnp.sum(low_terms * group_members.astype(jnp.float32)[:, :, None], axis=1)).astype(jnp.bfloat16)
        query_plain = (jnp.dot(normalized_input, query_weight, preferred_element_type=jnp.float32) + apply_adapter(lowrank_inner[:, 0:ADAPTER_RANK], group_members, jnp.take(adapter_up_query, slot_indices, axis=0))).astype(jnp.bfloat16)
        key_value_chosen = jnp.take(adapter_up_key_value, slot_indices, axis=0)
        kv_base = jnp.dot(normalized_input, key_value_weight.reshape(MODEL_WIDTH, 2 * key_value_width), preferred_element_type=jnp.float32).reshape(GROUP_TOKENS, 2, key_value_width)
        key_lowrank_part = apply_adapter(lowrank_inner[:, ADAPTER_RANK:2 * ADAPTER_RANK], group_members, key_value_chosen[:, :, 0])
        value_lowrank_part = apply_adapter(lowrank_inner[:, 2 * ADAPTER_RANK:3 * ADAPTER_RANK], group_members, key_value_chosen[:, :, 1])
        key_value_plain = (kv_base + jnp.stack([key_lowrank_part, value_lowrank_part], axis=1)).astype(jnp.bfloat16)
        query_rotated = rotary_embed(root_mean_scale(query_plain.astype(jnp.float32).reshape(GROUP_TOKENS, QUERY_HEADS, HEAD_SIZE), query_norm_gain), token_positions).astype(jnp.bfloat16)
        key_rotated = rotary_embed(root_mean_scale(key_value_plain[:, 0].astype(jnp.float32).reshape(GROUP_TOKENS, KEY_VALUE_HEADS, HEAD_SIZE), key_norm_gain), token_positions).astype(jnp.bfloat16)
        cache_group = jnp.stack([key_rotated.reshape(GROUP_TOKENS, key_value_width), key_value_plain[:, 1]], axis=1)
        key_matrix = jnp.concatenate([pool_index_group[:, 0].reshape(pool_token_rows, KEY_VALUE_HEADS, HEAD_SIZE), key_rotated], axis=0)
        value_matrix = jnp.concatenate([pool_index_group[:, 1].reshape(pool_token_rows, KEY_VALUE_HEADS, HEAD_SIZE), key_value_plain[:, 1].reshape(GROUP_TOKENS, KEY_VALUE_HEADS, HEAD_SIZE)], axis=0)
        pool_ok = jnp.dot(group_members.astype(jnp.float32), page_used, precision=lax.Precision.HIGHEST)
        pool_ok = jnp.repeat(pool_ok, PAGE, axis=1) > 0.5
        row_ids = jnp.arange(GROUP_TOKENS, dtype=jnp.int32)
        causal = (owners[:, None] == owners[None, :]) & (row_ids[None, :] <= row_ids[:, None])
        allowed = jnp.concatenate([pool_ok, causal], axis=1)
        query_rows = query_rotated.astype(jnp.float32).reshape(GROUP_TOKENS, KEY_VALUE_HEADS, QUERY_HEADS // KEY_VALUE_HEADS, HEAD_SIZE)
        scores = jnp.einsum('gkhd,skd->khgs', query_rows, key_matrix.astype(jnp.float32)) / math.sqrt(HEAD_SIZE)
        exp_scores = jnp.where(allowed[None, None], jnp.exp(scores), 0.0)
        softmax = (exp_scores / lax.optimization_barrier(jnp.sum(exp_scores, axis=-1, keepdims=True))).astype(jnp.bfloat16)
        attended = jnp.einsum('khgs,skd->gkhd', softmax.astype(jnp.float32), value_matrix.astype(jnp.float32))
        attended = attended.astype(jnp.bfloat16).reshape(GROUP_TOKENS, QUERY_HEADS * HEAD_SIZE)
        output_down = jnp.take(adapter_down_output, slot_indices, axis=0).astype(jnp.float32)
        out_terms = jnp.einsum('gc,jrc->gjr', attended.astype(jnp.float32), output_down)
        lowrank_result = lax.optimization_barrier(jnp.sum(out_terms * group_members.astype(jnp.float32)[:, :, None], axis=1)).astype(jnp.bfloat16)
        parts = jnp.einsum('gmc,mcd->gmd', attended.astype(jnp.float32).reshape(GROUP_TOKENS, N_MLP, block_rows), w_blocks)
        parts = lax.optimization_barrier(parts.astype(jnp.bfloat16))
        head_count_all = lax.optimization_barrier(jnp.sum(parts.astype(jnp.float32), axis=1))
        output_update = (head_count_all + apply_adapter(lowrank_result, group_members, jnp.take(adapter_up_output, slot_indices, axis=0))).astype(jnp.bfloat16)
        return (output_update, cache_group)
    output_update, cache_all = lax.map(one_group, (hidden_input.reshape(N_REQ, GROUP_TOKENS, MODEL_WIDTH), lengths, cached_prefix_pages, prefix_page_table, adapter_of_request[:, :, 0], pool.reshape(N_REQ, pool_token_rows, 2, key_value_width)))
    return (output_update.reshape(TOKENS, MODEL_WIDTH), cache_all.reshape(TOKENS, 2, key_value_width))
```

```python
import math

import jax
import jax.numpy as jnp
from jax import lax
from jax.sharding import PartitionSpec as P

QUERY_HEADS = 32
KEY_VALUE_HEADS = 8
HEAD_SIZE = 128
ADAPTER_RANK = 16
PAGE = 64


epsilon = 1e-06
rope_base = 1000000.0


def root_mean_scale(values, gain_vec):
    mean_sq = jnp.mean(values * values, axis=-1, keepdims=True)
    return values * lax.rsqrt(mean_sq + epsilon) * gain_vec.astype(jnp.float32)


def rotary_embed(values, token_positions):
    half_width = values.shape[-1] // 2
    inverse_freq = jnp.exp(
        jnp.arange(half_width, dtype=jnp.float32) * (-2.0 / values.shape[-1]) * math.log(rope_base)
    )
    angles = token_positions.astype(jnp.float32)[:, None] * inverse_freq[None, :]
    cosine = jnp.cos(angles)[:, None, :]
    sine_part = jnp.sin(angles)[:, None, :]
    front = values[..., :half_width]
    back = values[..., half_width:]
    return jnp.concatenate(
        [front * cosine - back * sine_part, back * cosine + front * sine_part], axis=-1
    )


def row_tables(lengths_row, prefix_row, page_rows, row_count):
    ends_at = jnp.cumsum(lengths_row)
    starts_at = ends_at - lengths_row
    row_ids = jnp.arange(row_count, dtype=jnp.int32)
    owners = jnp.sum((row_ids[:, None] >= ends_at[None, :]).astype(jnp.int32), axis=1)
    group_members = owners[:, None] == jnp.arange(lengths_row.shape[0], dtype=jnp.int32)[None, :]
    offsets = PAGE * prefix_row[None, :] + row_ids[:, None] - starts_at[None, :]
    token_positions = jnp.sum(jnp.where(group_members, offsets, 0), axis=1)
    page_ids = jnp.arange(page_rows.shape[1], dtype=jnp.int32)
    listed = (page_rows[:, :, None] == page_ids[None, None, :]) & (
        page_ids[None, :, None] < prefix_row[:, None, None]
    )
    page_used = jnp.sum(listed.astype(jnp.float32), axis=1)
    return (owners, group_members, token_positions, page_used)


def apply_adapter(lowrank_inner, group_members, chosen_up):
    masked = lowrank_inner[:, None, :] * group_members.astype(lowrank_inner.dtype)[:, :, None]
    return jnp.einsum("gjr,jrc->gc", masked, chosen_up, preferred_element_type=jnp.float32)


def select_rows(terms, group_members):
    return jnp.sum(terms * group_members.astype(jnp.float32)[:, :, None], axis=1)


def shards(
    hidden_input,
    input_norm_gain,
    query_norm_gain,
    key_norm_gain,
    query_weight,
    key_value_weight,
    output_weight,
    adapter_down_qkv,
    adapter_down_output,
    adapter_up_query,
    adapter_up_key_value,
    adapter_up_output,
    pool,
    lengths,
    cached_prefix_pages,
    prefix_page_table,
    adapter_of_request,
    adapter_storage,
):
    feature_group_count = lax.axis_size("mlp")
    feature_group_index = lax.axis_index("mlp")
    whole = lax.all_gather(hidden_input, "mlp", axis=1, tiled=True)
    row_count, full_width = whole.shape
    normalized_input = root_mean_scale(whole.astype(jnp.float32), input_norm_gain).astype(
        jnp.bfloat16
    )
    owners, group_members, token_positions, page_used = row_tables(
        lengths[0], cached_prefix_pages[0], prefix_page_table[0], row_count
    )
    q_width = query_weight.shape[1]
    query_head_rows = q_width // HEAD_SIZE
    key_value_local = max(1, KEY_VALUE_HEADS // feature_group_count)
    key_value_width = key_value_local * HEAD_SIZE
    key_value_begin = (
        feature_group_index * query_head_rows // (QUERY_HEADS // KEY_VALUE_HEADS) * HEAD_SIZE
    )
    own_wkv = lax.dynamic_slice_in_dim(key_value_weight, key_value_begin, key_value_width, 2)
    request_key_value_up = lax.dynamic_slice_in_dim(
        adapter_up_key_value, key_value_begin, key_value_width, 3
    )
    gathered = (
        lax.all_gather(adapter_down_qkv, "req", axis=0, tiled=True),
        lax.all_gather(adapter_down_output, "req", axis=0, tiled=True),
        lax.all_gather(adapter_up_query, "req", axis=0, tiled=True),
        lax.all_gather(request_key_value_up, "req", axis=0, tiled=True),
        lax.all_gather(adapter_up_output, "req", axis=0, tiled=True),
    )
    slot_indices = jnp.take(adapter_storage, adapter_of_request[0, :, 0], axis=0)
    chosen_down = jnp.take(gathered[0], slot_indices, axis=0)
    output_down = jnp.take(gathered[1], slot_indices, axis=0)
    query_up_part = jnp.take(gathered[2], slot_indices, axis=0)
    key_value_up = jnp.take(gathered[3], slot_indices, axis=0)
    output_up = jnp.take(gathered[4], slot_indices, axis=0)
    feature_cols = full_width // feature_group_count
    own_normed = lax.dynamic_slice_in_dim(
        normalized_input, feature_group_index * feature_cols, feature_cols, 1
    )
    low_terms = jnp.einsum(
        "gd,jkd->gjk", own_normed, chosen_down, preferred_element_type=jnp.float32
    )
    lowrank_inner = lax.psum(select_rows(low_terms, group_members).astype(jnp.bfloat16), "mlp")
    q_part = lax.all_gather(query_weight, "req", axis=0, tiled=True)
    kv_part = lax.all_gather(own_wkv, "req", axis=0, tiled=True)
    query_width_total = jnp.dot(normalized_input, q_part, preferred_element_type=jnp.float32)
    kv_total = jnp.dot(
        normalized_input,
        kv_part.reshape(kv_part.shape[0], 2 * key_value_width),
        preferred_element_type=jnp.float32,
    )
    query_width_total, kv_total = (query_width_total, kv_total)
    query_plain = (
        query_width_total
        + apply_adapter(lowrank_inner[:, 0:ADAPTER_RANK], group_members, query_up_part)
    ).astype(jnp.bfloat16)
    key_lowrank_part = apply_adapter(
        lowrank_inner[:, ADAPTER_RANK : 2 * ADAPTER_RANK], group_members, key_value_up[:, :, 0]
    )
    value_lowrank_part = apply_adapter(
        lowrank_inner[:, 2 * ADAPTER_RANK : 3 * ADAPTER_RANK], group_members, key_value_up[:, :, 1]
    )
    key_value_plain = (
        kv_total.reshape(row_count, 2, key_value_width)
        + jnp.stack([key_lowrank_part, value_lowrank_part], axis=1)
    ).astype(jnp.bfloat16)
    cached = lax.dynamic_slice_in_dim(pool, key_value_begin, key_value_width, 2)
    pool_token_rows = cached.shape[0]
    query_rotated = rotary_embed(
        root_mean_scale(
            query_plain.astype(jnp.float32).reshape(row_count, query_head_rows, HEAD_SIZE),
            query_norm_gain,
        ),
        token_positions,
    ).astype(jnp.bfloat16)
    key_rotated = rotary_embed(
        root_mean_scale(
            key_value_plain[:, 0]
            .astype(jnp.float32)
            .reshape(row_count, key_value_local, HEAD_SIZE),
            key_norm_gain,
        ),
        token_positions,
    ).astype(jnp.bfloat16)
    cache_columns = KEY_VALUE_HEADS * HEAD_SIZE // feature_group_count
    own_offset = feature_group_index * cache_columns - key_value_begin
    local_cache = jnp.stack(
        [key_rotated.reshape(row_count, key_value_width), key_value_plain[:, 1]], axis=1
    )
    new_cache = lax.dynamic_slice_in_dim(local_cache, own_offset, cache_columns, 2)
    key_matrix = jnp.concatenate(
        [cached[:, 0].reshape(pool_token_rows, key_value_local, HEAD_SIZE), key_rotated], axis=0
    )
    value_matrix = jnp.concatenate(
        [
            cached[:, 1].reshape(pool_token_rows, key_value_local, HEAD_SIZE),
            key_value_plain[:, 1].reshape(row_count, key_value_local, HEAD_SIZE),
        ],
        axis=0,
    )
    pool_ok = jnp.dot(group_members.astype(jnp.float32), page_used, precision=lax.Precision.HIGHEST)
    pool_ok = jnp.repeat(pool_ok, PAGE, axis=1) > 0.5
    row_ids = jnp.arange(row_count, dtype=jnp.int32)
    causal = (owners[:, None] == owners[None, :]) & (row_ids[None, :] <= row_ids[:, None])
    allowed = jnp.concatenate([pool_ok, causal], axis=1)
    query_rows = query_rotated.reshape(
        row_count, key_value_local, query_head_rows // key_value_local, HEAD_SIZE
    )
    scores = jnp.einsum(
        "gkhd,skd->khgs", query_rows, key_matrix, preferred_element_type=jnp.float32
    ) / math.sqrt(HEAD_SIZE)
    exp_scores = jnp.where(allowed[None, None], jnp.exp(scores), 0.0)
    softmax = (exp_scores / jnp.sum(exp_scores, axis=-1, keepdims=True)).astype(jnp.bfloat16)
    attended = jnp.einsum(
        "khgs,skd->gkhd", softmax, value_matrix, preferred_element_type=jnp.float32
    )
    attended = attended.astype(jnp.bfloat16).reshape(row_count, q_width)
    out_terms = jnp.einsum("gc,jrc->gjr", attended, output_down, preferred_element_type=jnp.float32)
    lowrank_result = lax.psum(select_rows(out_terms, group_members), "mlp").astype(jnp.bfloat16)
    partial_value = jnp.einsum(
        "gc,cnk->gnk",
        attended,
        lax.all_gather(output_weight, "req", axis=2, tiled=True),
        preferred_element_type=jnp.float32,
    )
    summed_output = lax.psum_scatter(
        partial_value.reshape(row_count, full_width).astype(jnp.bfloat16),
        "mlp",
        scatter_dimension=1,
        tiled=True,
    ).astype(jnp.float32)
    attention_update = (
        summed_output + apply_adapter(lowrank_result, group_members, output_up)
    ).astype(jnp.bfloat16)
    return (attention_update, new_cache)


PLANES = 4
BLOCKS = 4


def planes_fit(mesh):
    return mesh.shape["req"] == 2 * PLANES and mesh.shape["mlp"] == BLOCKS


def plane_pairs(pairs):
    return [(2 * a + core, 2 * b + core) for a, b in pairs for core in range(2)]


INWARD = plane_pairs([(0, 1), (3, 2)])
MIDDLE = plane_pairs([(1, 2), (2, 1)])
OUTWARD = plane_pairs([(1, 0), (2, 3)])
CORES = [(r, r ^ 1) for r in range(2 * PLANES)]


def along(value, pairs):
    return lax.ppermute(value, "req", pairs)


def to_blocks(pieces):
    return [
        lax.ppermute(piece, "mlp", [(b, b ^ k) for b in range(BLOCKS)])
        for k, piece in enumerate(pieces)
        if k > 0
    ]


def after(value, *earlier):
    return lax.optimization_barrier((value,) + earlier)[0]


def spread(lowrank, column_slots, row_slots):
    rank = lowrank.shape[1]
    column = jnp.arange(column_slots.shape[0], dtype=jnp.int32)
    picks = (column[None, :] % rank == jnp.arange(rank, dtype=jnp.int32)[:, None]).astype(
        jnp.bfloat16
    )
    wide = jnp.dot(lowrank, picks, preferred_element_type=jnp.float32)
    return jnp.where(row_slots[:, None] == column_slots[None, :], wide, 0.0).astype(jnp.bfloat16)


def request_slots(lengths_row, slots, row_count):
    ends_at = jnp.cumsum(lengths_row)
    row_ids = jnp.arange(row_count, dtype=jnp.int32)
    owners = jnp.sum((row_ids[:, None] >= ends_at[None, :]).astype(jnp.int32), axis=1)
    members = owners[:, None] == jnp.arange(slots.shape[0], dtype=jnp.int32)[None, :]
    return jnp.sum(jnp.where(members, slots[None, :], 0), axis=1)


def shards_by_plane(
    hidden_input,
    input_norm_gain,
    query_norm_gain,
    key_norm_gain,
    query_weight,
    key_value_weight,
    output_weight,
    adapter_down_qkv,
    adapter_down_output,
    adapter_up_query,
    adapter_up_key_value,
    adapter_up_output,
    pool,
    lengths,
    cached_prefix_pages,
    prefix_page_table,
    adapter_of_request,
    adapter_storage,
):
    request_index = lax.axis_index("req")
    plane, core = request_index // 2, request_index % 2
    block = lax.axis_index("mlp")
    at_end = (plane == 0) | (plane == PLANES - 1)
    near_end = jnp.where(plane < 2, 0, PLANES - 1)
    inner_planes = [plane, near_end, 3 - plane, 3 - near_end]
    row_count, block_width = hidden_input.shape
    q_width = query_weight.shape[1]
    query_heads_here = q_width // HEAD_SIZE
    key_value_local = KEY_VALUE_HEADS // BLOCKS
    key_value_width = key_value_local * HEAD_SIZE
    key_value_begin = block * key_value_width

    slots = jnp.take(adapter_storage, adapter_of_request[0, :, 0], axis=0)
    tables = jnp.concatenate([lengths[0], slots])[None, :]
    own_wkv = lax.dynamic_slice_in_dim(key_value_weight, key_value_begin, key_value_width, 2)
    own_w = jnp.concatenate([query_weight, own_wkv.reshape(-1, 2 * key_value_width)], axis=1)
    own_up_kv = lax.dynamic_slice_in_dim(adapter_up_key_value, key_value_begin, key_value_width, 3)
    own_adapters = jnp.concatenate(
        [
            adapter_down_qkv,
            adapter_up_query,
            own_up_kv.reshape(own_up_kv.shape[0], -1, block_width),
            adapter_down_output,
            adapter_up_output,
        ],
        axis=1,
    )
    own_wo = jnp.transpose(output_weight, (1, 0, 2))

    end_hidden = along(hidden_input, INWARD)
    end_tables = along(tables, INWARD)[0]
    own_pieces = [hidden_input] + to_blocks([hidden_input] * BLOCKS)
    ad_1 = along(own_adapters, INWARD)
    ad_2 = along(own_adapters, MIDDLE)
    wo_out1 = along(own_wo, OUTWARD)
    w_1 = along(after(own_w, end_hidden, ad_1), INWARD)
    w_2 = along(after(own_w, ad_2), MIDDLE)
    ad_3 = along(after(ad_1, w_2), MIDDLE)
    w_3 = along(after(w_1, ad_3), MIDDLE)
    wo_in1 = along(after(own_wo, w_1), INWARD)
    wo_mid1 = along(after(own_wo, w_3), MIDDLE)
    wo_mid2 = along(after(wo_in1, wo_mid1), MIDDLE)
    end_pieces = [end_hidden] + to_blocks([after(end_hidden, *own_pieces)] * BLOCKS)

    gains = input_norm_gain.astype(jnp.float32).reshape(BLOCKS, block_width)
    rows = [jnp.concatenate([a, b], axis=0).astype(jnp.float32) for a, b in zip(own_pieces, end_pieces)]
    mean_sq = sum(jnp.sum(v * v, axis=1, keepdims=True) for v in rows) / (BLOCKS * block_width)
    scale = lax.rsqrt(mean_sq + epsilon)
    normed = [
        (v * scale * lax.dynamic_index_in_dim(gains, block ^ k, 0)).astype(jnp.bfloat16)
        for k, v in enumerate(rows)
    ]
    half = block_width // 2
    normed_core = jnp.stack([jnp.where(core == 0, v[:, :half], v[:, half:]) for v in normed])
    normed_other = jnp.stack([jnp.where(core == 0, v[:, half:], v[:, :half]) for v in normed])

    own_core_adapters = jnp.concatenate([own_adapters, ad_1, ad_2, ad_3], axis=0)
    adapters = jnp.concatenate([own_core_adapters, along(own_core_adapters, CORES)], axis=0)
    slot_ids = jnp.stack(
        [4 * p + 2 * c + i for c in (core, 1 - core) for p in inner_planes for i in range(2)]
    ).astype(jnp.int32)
    rank = ADAPTER_RANK
    row_slots = jnp.concatenate(
        [
            request_slots(lengths[0], slots, row_count),
            request_slots(end_tables[: lengths.shape[1]], end_tables[lengths.shape[1] :], row_count),
        ]
    )
    down = adapters[:, : 3 * rank].reshape(-1, block_width)
    low_terms = lax.dot_general(
        normed[0], down, (((1,), (1,)), ((), ())), preferred_element_type=jnp.float32
    )
    wide_slots = jnp.repeat(slot_ids, 3 * rank)
    low_terms = jnp.where(row_slots[:, None] == wide_slots[None, :], low_terms, 0.0).astype(jnp.bfloat16)
    gather_ranks = (
        jnp.arange(down.shape[0], dtype=jnp.int32)[:, None] % (3 * rank)
        == jnp.arange(3 * rank, dtype=jnp.int32)[None, :]
    ).astype(jnp.bfloat16)
    low_part = jnp.dot(low_terms, gather_ranks, preferred_element_type=jnp.float32).astype(jnp.bfloat16)
    low_parts = [low_part] + to_blocks([low_part] * BLOCKS)
    lowrank = sum(v.astype(jnp.float32) for v in low_parts).astype(jnp.bfloat16)
    column_slots = jnp.repeat(slot_ids, rank)
    up_query = adapters[:, 3 * rank : 4 * rank].reshape(-1, q_width)
    up_kv_rows = own_up_kv.shape[1] * 2 * key_value_width // block_width
    up_kv = adapters[:, 4 * rank : 4 * rank + up_kv_rows].reshape(-1, 2 * key_value_width)
    out_first = 4 * rank + up_kv_rows
    q_low = jnp.dot(
        spread(lowrank[:, :rank], column_slots, row_slots), up_query, preferred_element_type=jnp.float32
    )
    k_low = jnp.dot(
        spread(lowrank[:, rank : 2 * rank], column_slots, row_slots),
        up_kv[:, :key_value_width],
        preferred_element_type=jnp.float32,
    )
    v_low = jnp.dot(
        spread(lowrank[:, 2 * rank :], column_slots, row_slots),
        up_kv[:, key_value_width:],
        preferred_element_type=jnp.float32,
    )

    def chosen_out(wanted):
        places = jnp.sum(
            jnp.where(
                wanted[:, None] == slot_ids[None, :],
                jnp.arange(slot_ids.shape[0], dtype=jnp.int32)[None, :],
                0,
            ),
            axis=1,
        )
        return jnp.take(adapters[:, out_first:], places, axis=0)

    end_out = along(chosen_out(end_tables[lengths.shape[1] :]), OUTWARD)
    out_adapters = jnp.where(at_end, end_out, chosen_out(slots))

    sums = None
    for p, w in zip(inner_planes, (own_w, w_1, w_2, w_3)):
        k = p ^ block
        term = jnp.dot(
            lax.dynamic_index_in_dim(normed_core, k, 0, keepdims=False),
            w,
            preferred_element_type=jnp.float32,
        ) + jnp.dot(
            lax.dynamic_index_in_dim(normed_other, k, 0, keepdims=False),
            along(w, CORES),
            preferred_element_type=jnp.float32,
        )
        sums = term if sums is None else sums + term
    raw = (sums + jnp.concatenate([q_low, k_low, v_low], axis=1)).astype(jnp.bfloat16)
    back = along(raw[row_count:], OUTWARD)
    wo_out2 = along(after(wo_mid1, back), OUTWARD)
    wo_out3 = along(after(wo_mid2, wo_out2), OUTWARD)
    raw = jnp.where(at_end, back, raw[:row_count])
    query_plain = raw[:, :q_width]
    key_plain = raw[:, q_width : q_width + key_value_width]
    value_plain = raw[:, q_width + key_value_width :].reshape(row_count, key_value_local, HEAD_SIZE)

    owners, group_members, token_positions, page_used = row_tables(
        lengths[0], cached_prefix_pages[0], prefix_page_table[0], row_count
    )
    cached = lax.dynamic_slice_in_dim(pool, key_value_begin, key_value_width, 2)
    pool_token_rows = cached.shape[0]
    query_rotated = rotary_embed(
        root_mean_scale(
            query_plain.astype(jnp.float32).reshape(row_count, query_heads_here, HEAD_SIZE),
            query_norm_gain,
        ),
        token_positions,
    ).astype(jnp.bfloat16)
    key_rotated = rotary_embed(
        root_mean_scale(
            key_plain.astype(jnp.float32).reshape(row_count, key_value_local, HEAD_SIZE),
            key_norm_gain,
        ),
        token_positions,
    ).astype(jnp.bfloat16)
    new_cache = jnp.stack(
        [
            key_rotated.reshape(row_count, key_value_width),
            value_plain.reshape(row_count, key_value_width),
        ],
        axis=1,
    )
    key_matrix = jnp.concatenate(
        [cached[:, 0].reshape(pool_token_rows, key_value_local, HEAD_SIZE), key_rotated], axis=0
    )
    value_matrix = jnp.concatenate(
        [cached[:, 1].reshape(pool_token_rows, key_value_local, HEAD_SIZE), value_plain], axis=0
    )
    pool_ok = jnp.dot(group_members.astype(jnp.float32), page_used, precision=lax.Precision.HIGHEST)
    pool_ok = jnp.repeat(pool_ok, PAGE, axis=1) > 0.5
    row_ids = jnp.arange(row_count, dtype=jnp.int32)
    causal = (owners[:, None] == owners[None, :]) & (row_ids[None, :] <= row_ids[:, None])
    allowed = jnp.concatenate([pool_ok, causal], axis=1)
    query_rows = query_rotated.reshape(
        row_count, key_value_local, query_heads_here // key_value_local, HEAD_SIZE
    )
    scores = jnp.einsum(
        "gkhd,skd->khgs", query_rows, key_matrix, preferred_element_type=jnp.float32
    ) / math.sqrt(HEAD_SIZE)
    exp_scores = jnp.where(allowed[None, None], jnp.exp(scores), 0.0)
    softmax = (exp_scores / jnp.sum(exp_scores, axis=-1, keepdims=True)).astype(jnp.bfloat16)
    attended = jnp.einsum(
        "khgs,skd->gkhd", softmax, value_matrix, preferred_element_type=jnp.float32
    )
    attended = attended.astype(jnp.bfloat16).reshape(row_count, q_width)

    out_terms = jnp.einsum(
        "gc,jrc->gjr", attended, out_adapters[:, :rank], preferred_element_type=jnp.float32
    )
    out_part = select_rows(out_terms, group_members)
    lowrank_out = sum([out_part] + to_blocks([out_part] * BLOCKS)).astype(jnp.bfloat16)
    request_ids = jnp.arange(lengths.shape[1], dtype=jnp.int32)
    out_low = jnp.dot(
        spread(lowrank_out, jnp.repeat(request_ids, rank), owners),
        out_adapters[:, rank:].reshape(-1, block_width),
        preferred_element_type=jnp.float32,
    )

    step_weights = (
        own_wo,
        jnp.where(at_end, wo_out1, wo_in1),
        jnp.where(at_end, wo_out2, wo_mid1),
        jnp.where(at_end, wo_out3, wo_mid2),
    )
    near = jnp.where(at_end, jnp.where(plane == 0, 1, 2), near_end)
    other = jnp.where(at_end, jnp.where(plane == 0, 2, 1), 3 - plane)
    step_planes = [plane, near, other, 6 - plane - near - other]
    columns = []
    for w in step_weights:
        both = jnp.concatenate([w, along(w, CORES)], axis=2)
        parts = [
            jnp.dot(
                attended,
                lax.dynamic_index_in_dim(both, block ^ k, 0, keepdims=False),
                preferred_element_type=jnp.float32,
            ).astype(jnp.bfloat16)
            for k in range(BLOCKS)
        ]
        total = sum(v.astype(jnp.float32) for v in [parts[0]] + to_blocks(parts))
        columns += [total[:, :HEAD_SIZE], total[:, HEAD_SIZE:]]
    columns = jnp.stack(columns)
    ordered = []
    for p in range(PLANES):
        place = sum(i * (q == p).astype(jnp.int32) for i, q in enumerate(step_planes))
        for c in range(2):
            ordered.append(
                lax.dynamic_index_in_dim(columns, 2 * place + (core != c), 0, keepdims=False)
            )
    attention_update = (jnp.concatenate(ordered, axis=1) + out_low).astype(jnp.bfloat16)
    return (attention_update, new_cache)


def solution(mesh):
    return jax.shard_map(
        shards_by_plane if planes_fit(mesh) else shards,
        mesh=mesh,
        in_specs=(
            P("req", "mlp"),
            P(),
            P(),
            P(),
            P("req", "mlp"),
            P("req", None, None),
            P("mlp", None, "req"),
            P("req", None, "mlp"),
            P("req", None, "mlp"),
            P("req", None, "mlp"),
            P("req", None, None, None),
            P("req", None, "mlp"),
            P("req", None, None),
            P("req", None),
            P("req", None),
            P("req", None, None),
            P("req", None, None),
            P(),
        ),
        out_specs=(P("req", "mlp"), P("req", None, "mlp")),
        check_vma=False,
    )
```

```python
import functools
import math

import jax
import jax.numpy as jnp
from jax import lax
from jax.experimental import pallas as pl
from jax.experimental.pallas import tpu as pltpu
from jax.sharding import PartitionSpec as P

QUERY_HEADS = 32
KEY_VALUE_HEADS = 8
HEAD_SIZE = 128
ADAPTER_RANK = 16
PAGE = 64


epsilon = 1e-06
rope_base = 1000000.0


def root_mean_scale(values, gain_vec):
    mean_sq = jnp.mean(values * values, axis=-1, keepdims=True)
    return values * lax.rsqrt(mean_sq + epsilon) * gain_vec.astype(jnp.float32)


def rotary_embed(values, token_positions):
    half_width = values.shape[-1] // 2
    inverse_freq = jnp.exp(
        jnp.arange(half_width, dtype=jnp.float32) * (-2.0 / values.shape[-1]) * math.log(rope_base)
    )
    angles = token_positions.astype(jnp.float32)[:, None] * inverse_freq[None, :]
    cosine = jnp.cos(angles)[:, None, :]
    sine_part = jnp.sin(angles)[:, None, :]
    front = values[..., :half_width]
    back = values[..., half_width:]
    return jnp.concatenate(
        [front * cosine - back * sine_part, back * cosine + front * sine_part], axis=-1
    )


def row_tables(lengths_row, prefix_row, page_rows, row_count):
    ends_at = jnp.cumsum(lengths_row)
    starts_at = ends_at - lengths_row
    row_ids = jnp.arange(row_count, dtype=jnp.int32)
    owners = jnp.sum((row_ids[:, None] >= ends_at[None, :]).astype(jnp.int32), axis=1)
    group_members = owners[:, None] == jnp.arange(lengths_row.shape[0], dtype=jnp.int32)[None, :]
    offsets = PAGE * prefix_row[None, :] + row_ids[:, None] - starts_at[None, :]
    token_positions = jnp.sum(jnp.where(group_members, offsets, 0), axis=1)
    page_ids = jnp.arange(page_rows.shape[1], dtype=jnp.int32)
    listed = (page_rows[:, :, None] == page_ids[None, None, :]) & (
        page_ids[None, :, None] < prefix_row[:, None, None]
    )
    page_used = jnp.sum(listed.astype(jnp.float32), axis=1)
    return (owners, group_members, token_positions, page_used)


def apply_adapter(lowrank_inner, group_members, chosen_up):
    masked = lowrank_inner[:, None, :] * group_members.astype(lowrank_inner.dtype)[:, :, None]
    return jnp.einsum("gjr,jrc->gc", masked, chosen_up, preferred_element_type=jnp.float32)


def select_rows(terms, group_members):
    return jnp.sum(terms * group_members.astype(jnp.float32)[:, :, None], axis=1)


def shards(
    hidden_input,
    input_norm_gain,
    query_norm_gain,
    key_norm_gain,
    query_weight,
    key_value_weight,
    output_weight,
    adapter_down_qkv,
    adapter_down_output,
    adapter_up_query,
    adapter_up_key_value,
    adapter_up_output,
    pool,
    lengths,
    cached_prefix_pages,
    prefix_page_table,
    adapter_of_request,
    adapter_storage,
):
    feature_group_count = lax.axis_size("mlp")
    feature_group_index = lax.axis_index("mlp")
    whole = lax.all_gather(hidden_input, "mlp", axis=1, tiled=True)
    row_count, full_width = whole.shape
    normalized_input = root_mean_scale(whole.astype(jnp.float32), input_norm_gain).astype(
        jnp.bfloat16
    )
    owners, group_members, token_positions, page_used = row_tables(
        lengths[0], cached_prefix_pages[0], prefix_page_table[0], row_count
    )
    q_width = query_weight.shape[1]
    query_head_rows = q_width // HEAD_SIZE
    key_value_local = max(1, KEY_VALUE_HEADS // feature_group_count)
    key_value_width = key_value_local * HEAD_SIZE
    key_value_begin = (
        feature_group_index * query_head_rows // (QUERY_HEADS // KEY_VALUE_HEADS) * HEAD_SIZE
    )
    own_wkv = lax.dynamic_slice_in_dim(key_value_weight, key_value_begin, key_value_width, 2)
    request_key_value_up = lax.dynamic_slice_in_dim(
        adapter_up_key_value, key_value_begin, key_value_width, 3
    )
    gathered = (
        lax.all_gather(adapter_down_qkv, "req", axis=0, tiled=True),
        lax.all_gather(adapter_down_output, "req", axis=0, tiled=True),
        lax.all_gather(adapter_up_query, "req", axis=0, tiled=True),
        lax.all_gather(request_key_value_up, "req", axis=0, tiled=True),
        lax.all_gather(adapter_up_output, "req", axis=0, tiled=True),
    )
    slot_indices = jnp.take(adapter_storage, adapter_of_request[0, :, 0], axis=0)
    chosen_down = jnp.take(gathered[0], slot_indices, axis=0)
    output_down = jnp.take(gathered[1], slot_indices, axis=0)
    query_up_part = jnp.take(gathered[2], slot_indices, axis=0)
    key_value_up = jnp.take(gathered[3], slot_indices, axis=0)
    output_up = jnp.take(gathered[4], slot_indices, axis=0)
    feature_cols = full_width // feature_group_count
    own_normed = lax.dynamic_slice_in_dim(
        normalized_input, feature_group_index * feature_cols, feature_cols, 1
    )
    low_terms = jnp.einsum(
        "gd,jkd->gjk", own_normed, chosen_down, preferred_element_type=jnp.float32
    )
    lowrank_inner = lax.psum(select_rows(low_terms, group_members).astype(jnp.bfloat16), "mlp")
    q_part = lax.all_gather(query_weight, "req", axis=0, tiled=True)
    kv_part = lax.all_gather(own_wkv, "req", axis=0, tiled=True)
    query_width_total = jnp.dot(normalized_input, q_part, preferred_element_type=jnp.float32)
    kv_total = jnp.dot(
        normalized_input,
        kv_part.reshape(kv_part.shape[0], 2 * key_value_width),
        preferred_element_type=jnp.float32,
    )
    query_width_total, kv_total = (query_width_total, kv_total)
    query_plain = (
        query_width_total
        + apply_adapter(lowrank_inner[:, 0:ADAPTER_RANK], group_members, query_up_part)
    ).astype(jnp.bfloat16)
    key_lowrank_part = apply_adapter(
        lowrank_inner[:, ADAPTER_RANK : 2 * ADAPTER_RANK], group_members, key_value_up[:, :, 0]
    )
    value_lowrank_part = apply_adapter(
        lowrank_inner[:, 2 * ADAPTER_RANK : 3 * ADAPTER_RANK], group_members, key_value_up[:, :, 1]
    )
    key_value_plain = (
        kv_total.reshape(row_count, 2, key_value_width)
        + jnp.stack([key_lowrank_part, value_lowrank_part], axis=1)
    ).astype(jnp.bfloat16)
    cached = lax.dynamic_slice_in_dim(pool, key_value_begin, key_value_width, 2)
    pool_token_rows = cached.shape[0]
    query_rotated = rotary_embed(
        root_mean_scale(
            query_plain.astype(jnp.float32).reshape(row_count, query_head_rows, HEAD_SIZE),
            query_norm_gain,
        ),
        token_positions,
    ).astype(jnp.bfloat16)
    key_rotated = rotary_embed(
        root_mean_scale(
            key_value_plain[:, 0]
            .astype(jnp.float32)
            .reshape(row_count, key_value_local, HEAD_SIZE),
            key_norm_gain,
        ),
        token_positions,
    ).astype(jnp.bfloat16)
    cache_columns = KEY_VALUE_HEADS * HEAD_SIZE // feature_group_count
    own_offset = feature_group_index * cache_columns - key_value_begin
    local_cache = jnp.stack(
        [key_rotated.reshape(row_count, key_value_width), key_value_plain[:, 1]], axis=1
    )
    new_cache = lax.dynamic_slice_in_dim(local_cache, own_offset, cache_columns, 2)
    key_matrix = jnp.concatenate(
        [cached[:, 0].reshape(pool_token_rows, key_value_local, HEAD_SIZE), key_rotated], axis=0
    )
    value_matrix = jnp.concatenate(
        [
            cached[:, 1].reshape(pool_token_rows, key_value_local, HEAD_SIZE),
            key_value_plain[:, 1].reshape(row_count, key_value_local, HEAD_SIZE),
        ],
        axis=0,
    )
    pool_ok = jnp.dot(group_members.astype(jnp.float32), page_used, precision=lax.Precision.HIGHEST)
    pool_ok = jnp.repeat(pool_ok, PAGE, axis=1) > 0.5
    row_ids = jnp.arange(row_count, dtype=jnp.int32)
    causal = (owners[:, None] == owners[None, :]) & (row_ids[None, :] <= row_ids[:, None])
    allowed = jnp.concatenate([pool_ok, causal], axis=1)
    query_rows = query_rotated.reshape(
        row_count, key_value_local, query_head_rows // key_value_local, HEAD_SIZE
    )
    scores = jnp.einsum(
        "gkhd,skd->khgs", query_rows, key_matrix, preferred_element_type=jnp.float32
    ) / math.sqrt(HEAD_SIZE)
    exp_scores = jnp.where(allowed[None, None], jnp.exp(scores), 0.0)
    softmax = (exp_scores / jnp.sum(exp_scores, axis=-1, keepdims=True)).astype(jnp.bfloat16)
    attended = jnp.einsum(
        "khgs,skd->gkhd", softmax, value_matrix, preferred_element_type=jnp.float32
    )
    attended = attended.astype(jnp.bfloat16).reshape(row_count, q_width)
    out_terms = jnp.einsum("gc,jrc->gjr", attended, output_down, preferred_element_type=jnp.float32)
    lowrank_result = lax.psum(select_rows(out_terms, group_members), "mlp").astype(jnp.bfloat16)
    partial_value = jnp.einsum(
        "gc,cnk->gnk",
        attended,
        lax.all_gather(output_weight, "req", axis=2, tiled=True),
        preferred_element_type=jnp.float32,
    )
    summed_output = lax.psum_scatter(
        partial_value.reshape(row_count, full_width).astype(jnp.bfloat16),
        "mlp",
        scatter_dimension=1,
        tiled=True,
    ).astype(jnp.float32)
    attention_update = (
        summed_output + apply_adapter(lowrank_result, group_members, output_up)
    ).astype(jnp.bfloat16)
    return (attention_update, new_cache)


PLANES = 4
BLOCKS = 4
GROUPS = 2
WIDE = 256


def planes_fit(mesh):
    return mesh.shape["req"] == 2 * PLANES and mesh.shape["mlp"] == BLOCKS


def plane_pairs(pairs):
    return [(2 * a + core, 2 * b + core) for a, b in pairs for core in range(2)]


INWARD = plane_pairs([(0, 1), (3, 2)])
MIDDLE = plane_pairs([(1, 2), (2, 1)])
OUTWARD = plane_pairs([(1, 0), (2, 3)])
NEAR = plane_pairs([(0, 1), (1, 0), (2, 3), (3, 2)])
CORES = [(r, r ^ 1) for r in range(2 * PLANES)]


def along(value, pairs):
    return lax.ppermute(value, "req", pairs)


def swap_blocks(value, k):
    return lax.ppermute(value, "mlp", [(b, b ^ k) for b in range(BLOCKS)])


def to_blocks(pieces):
    return [
        lax.ppermute(piece, "mlp", [(b, b ^ k) for b in range(BLOCKS)])
        for k, piece in enumerate(pieces)
        if k > 0
    ]


def gate_kernel(*refs):
    del refs


def gate(values, earlier):
    return pl.pallas_call(
        gate_kernel,
        in_specs=[pl.BlockSpec(memory_space=pl.ANY)] * (len(values) + len(earlier)),
        out_specs=[pl.BlockSpec(memory_space=pl.ANY)] * len(values),
        out_shape=[jax.ShapeDtypeStruct(v.shape, v.dtype) for v in values],
        input_output_aliases={i: i for i in range(len(values))},
        name="gate",
    )(*values, *earlier)


def in_vmem():
    return pl.BlockSpec(memory_space=pltpu.VMEM)


def in_smem():
    return pl.BlockSpec(memory_space=pltpu.SMEM)


def cost(flops, bytes_accessed, transcendentals=0):
    return pl.CostEstimate(
        flops=flops, bytes_accessed=bytes_accessed, transcendentals=transcendentals
    )


def kernel_params():
    return pltpu.CompilerParams(vmem_limit_bytes=56 * 1024 * 1024)


def request_of_rows(table, shape, axis):
    row = lax.broadcasted_iota(jnp.int32, shape, axis)
    end, owner = table[0], jnp.zeros(shape, jnp.int32)
    for j in range(1, 4):
        owner = jnp.where(row >= end, j, owner)
        end = end + table[j]
    return owner


def slots_of_rows(table, storage, row_count):
    owner = request_of_rows(table, (1, row_count), 1)
    slots = jnp.zeros((1, row_count), jnp.int32) + storage[table[4]]
    for j in range(1, 4):
        slots = jnp.where(owner == j, storage[table[4 + j]], slots)
    return slots


def slot_list(place):
    core = place[0]
    return [4 * place[2 + i] + 2 * c + s for c in (core, 1 - core) for i in range(4) for s in range(2)]


def dot(a, b):
    return jnp.dot(a, b, preferred_element_type=jnp.float32)


def core_columns(c, half):
    return pl.ds(pl.multiple_of(c * half, half), half)


def norm_kernel(place, gain, p0, p1, p2, p3, p4, *refs):
    out, done = refs[-2:]
    pieces = [p[...].astype(jnp.float32) for p in (p0, p1, p2)]
    late = pl.program_id(0) >= pl.num_programs(0) // 2
    pieces.append(jnp.where(late, p4[...], p3[...]).astype(jnp.float32))
    total = sum(jnp.sum(v * v, axis=1, keepdims=True) for v in pieces)
    half = pieces[0].shape[1] // 2
    scale = lax.rsqrt(total / (BLOCKS * 2 * half) + epsilon)
    core = place[0]
    for k, v in enumerate(pieces):
        normed = (v * scale * gain[pl.ds(place[1] ^ k, 1), :]).astype(jnp.bfloat16)
        out[k, :, core_columns(core, half)] = normed[:, :half]
        out[k, :, core_columns(1 - core, half)] = normed[:, half:]
    done[...] = jnp.zeros(done.shape, jnp.float32)


def norm_rows(place, gain, pieces, group, given):
    rows, width = pieces[0].shape
    tiles = 4
    tile = rows // tiles
    more = [] if given is None else [given]
    whole = pl.BlockSpec((tile, width), lambda i, place: (i, 0))
    front = pl.BlockSpec((tile, width), lambda i, place: (jnp.minimum(i, tiles // 2 - 1), 0))
    back = pl.BlockSpec((tile, width), lambda i, place: (jnp.maximum(i - tiles // 2, 0), 0))
    return pl.pallas_call(
        norm_kernel,
        grid_spec=pltpu.PrefetchScalarGridSpec(
            num_scalar_prefetch=1,
            grid=(tiles,),
            in_specs=[pl.BlockSpec((BLOCKS, width), lambda i, place: (0, 0))]
            + [whole] * 3
            + [front, back]
            + [pl.BlockSpec(memory_space=pl.ANY)] * len(more),
            out_specs=[
                pl.BlockSpec((BLOCKS, tile, width), lambda i, place: (0, tiles * group + i, 0)),
                pl.BlockSpec((8, 128), lambda i, place: (0, 0)),
            ],
        ),
        out_shape=[
            jax.ShapeDtypeStruct((BLOCKS, GROUPS * rows, width), jnp.bfloat16),
            jax.ShapeDtypeStruct((8, 128), jnp.float32),
        ],
        input_output_aliases={7: 0} if more else {},
        compiler_params=kernel_params(),
        cost_estimate=cost(16 * rows * width, 4 * BLOCKS * rows * width),
        name="norm_rows",
    )(place, gain, *pieces, *more)


SLOT_ROWS = 128


def pack_kernel(table, kv, down_qkv, up_query, up_kv, down_out, up_out, out):
    depth, kv_columns = kv.shape
    rank = ADAPTER_RANK
    out[2 * SLOT_ROWS :, :kv_columns] = kv[: depth // 2]
    out[2 * SLOT_ROWS :, kv_columns:] = kv[depth // 2 :]
    for s in range(2):
        first = s * SLOT_ROWS
        out[first : first + 3 * rank] = down_qkv[s]
        out[first + 3 * rank : first + 4 * rank] = up_query[s]
        out[first + 4 * rank : first + 5 * rank, :kv_columns] = up_kv[s]
        out[first + 4 * rank : first + 5 * rank, kv_columns:] = jnp.zeros(
            (rank, out.shape[1] - kv_columns), jnp.bfloat16
        )
        out[first + 5 * rank : first + 6 * rank] = down_out[s]
        out[first + 6 * rank : first + 7 * rank] = up_out[s]
    shape = (rank, out.shape[1])
    lane = lax.broadcasted_iota(jnp.int32, shape, 1)
    numbers = jnp.zeros(shape, jnp.float32)
    for i in range(8):
        numbers = jnp.where(lane == i, table[i].astype(jnp.float32), numbers)
    for s in range(2):
        out[s * SLOT_ROWS + 7 * rank : (s + 1) * SLOT_ROWS] = numbers.astype(jnp.bfloat16)


def pack_rows(table, kv, *adapters):
    width = adapters[0].shape[2]
    return pl.pallas_call(
        pack_kernel,
        in_specs=[in_smem()] + [in_vmem()] * 6,
        out_specs=in_vmem(),
        out_shape=jax.ShapeDtypeStruct((2 * SLOT_ROWS + kv.shape[0] // 2, width), jnp.bfloat16),
        compiler_params=kernel_params(),
        cost_estimate=cost(0, 4 * width * (2 * SLOT_ROWS + kv.shape[0] // 2), 0),
        name="pack_rows",
    )(table, kv, *adapters)


def rank_kernel(place, own_table, end_table, storage, x, *refs):
    packed, (low, chosen_own, chosen_end, up, down) = refs[:8], refs[8:]
    slots = slot_list(place)
    rank, rows, q_width = ADAPTER_RANK, x.shape[1] // GROUPS, x.shape[2]
    kv_columns, half, core = up.shape[1] - q_width, q_width // 2, place[0]
    for t, ref in enumerate(packed):
        for s in range(2):
            i, first = 2 * t + s, s * SLOT_ROWS
            for c, columns in ((core, slice(0, half)), (1 - core, slice(half, q_width))):
                down[3 * rank * i : 3 * rank * (i + 1), columns] = ref[
                    first : first + 3 * rank, core_columns(c, half)
                ]
            up[rank * i : rank * (i + 1), :q_width] = ref[first + 3 * rank : first + 4 * rank, :]
            up[rank * i : rank * (i + 1), q_width:] = ref[
                first + 4 * rank : first + 5 * rank, :kv_columns
            ]
    for g, (table, chosen) in enumerate(((own_table, chosen_own), (end_table, chosen_end))):
        terms = lax.dot_general(
            down[...],
            x[0, g * rows : (g + 1) * rows, :],
            (((1,), (1,)), ((), ())),
            preferred_element_type=jnp.float32,
        )
        row_slots = slots_of_rows(table, storage, rows)
        total = jnp.zeros((3 * rank, rows), jnp.float32)
        for i, slot in enumerate(slots):
            total += jnp.where(row_slots == slot, terms[3 * rank * i : 3 * rank * (i + 1)], 0.0)
        low[:, g * rows : (g + 1) * rows] = total.astype(jnp.bfloat16)
        for j in range(4):
            wanted = storage[table[4 + j]]
            for i, slot in enumerate(slots):

                @pl.when(wanted == slot)
                def _(j=j, i=i, chosen=chosen):
                    first = (i % 2) * SLOT_ROWS
                    chosen[j] = packed[i // 2][first + 5 * rank : first + 7 * rank, :]


def rank_terms(place, own_table, end_table, storage, x, packed, kv_columns):
    _, rows, width = x.shape
    chosen = jax.ShapeDtypeStruct((4, 2 * ADAPTER_RANK, width), jnp.bfloat16)
    up = jax.ShapeDtypeStruct((16 * ADAPTER_RANK, width + kv_columns), jnp.bfloat16)
    low = jax.ShapeDtypeStruct((3 * ADAPTER_RANK, rows), jnp.bfloat16)
    first = pl.BlockSpec((1, rows, width), lambda i: (0, 0, 0))
    slots = pl.BlockSpec((2 * SLOT_ROWS, width), lambda i: (0, 0))
    whole = lambda shape: pl.BlockSpec(shape, lambda i: (0,) * len(shape))
    return pl.pallas_call(
        rank_kernel,
        grid=(1,),
        in_specs=[in_smem()] * 4 + [first] + [slots] * 8,
        out_specs=[whole(v.shape) for v in (low, chosen, chosen, up)],
        out_shape=[low, chosen, chosen, up],
        scratch_shapes=[pltpu.VMEM((16 * 3 * ADAPTER_RANK, width), jnp.bfloat16)],
        compiler_params=kernel_params(),
        cost_estimate=cost(2 * 16 * 3 * ADAPTER_RANK * rows * width, 2 * width * (rows + 18 * SLOT_ROWS + 256), 0),
        name="rank_terms",
    )(place, own_table, end_table, storage, x, *packed)


def first_kernel(place, x, *refs):
    weights, packed, (out, done) = refs[:6], refs[6:22], refs[22:]
    half, depth = x.shape[2] // 2, packed[0].shape[0]
    step = pl.program_id(0)

    @pl.when(step < 4)
    def _():
        total = None
        for i, w in enumerate(weights):
            k, c = place[2 + i // 2] ^ place[1], i % 2
            term = dot(x[k, :, c * half : (c + 1) * half], w[...])
            total = term if total is None else total + term
        out[...] = total

    @pl.when(step >= 4)
    def _():
        total = None
        for i, w in enumerate(packed):
            k, c = place[2 + i // 4] ^ place[1], i % 4
            term = dot(x[k, :, c * depth : (c + 1) * depth], w[...])
            total = term if total is None else total + term
        out[...] = total

    done[...] = jnp.zeros(done.shape, jnp.float32)


def project_first(place, x, queries, packed):
    _, rows, width = x.shape
    depth = queries[0].shape[0]
    tile = pl.BlockSpec((rows, WIDE), lambda n: (0, n))
    query = pl.BlockSpec((depth, WIDE), lambda n: (0, jnp.minimum(n, 3)))
    key_values = [
        pl.BlockSpec((depth // 2, WIDE), lambda n, b=b: (1, b + jnp.maximum(n - 4, 0)))
        for b in (0, 2)
    ]
    return pl.pallas_call(
        first_kernel,
        grid=(6,),
        in_specs=[in_smem(), pl.BlockSpec(x.shape, lambda n: (0, 0, 0))]
        + [query] * 6
        + key_values * 8,
        out_specs=[tile, pl.BlockSpec((8, 128), lambda n: (0, 0))],
        out_shape=[
            jax.ShapeDtypeStruct((rows, 6 * WIDE), jnp.float32),
            jax.ShapeDtypeStruct((8, 128), jnp.float32),
        ],
        compiler_params=kernel_params(),
        cost_estimate=cost(2 * rows * width * (3 * width + 2 * width), 8 * rows * width + 2 * width * (3 * width + 2 * width) + 24 * rows * WIDE, 0),
        name="project_first",
    )(place, x, *queries, *[p for p in packed for _ in range(2)])


def last_kernel(place, x, q_core, q_other, up, given, *refs):
    own_table, end_table, storage = refs[:3]
    lows, (own, end, spread) = refs[3:7], refs[7:]
    rank, rows, half = ADAPTER_RANK, x.shape[1] // GROUPS, x.shape[2] // 2
    step = pl.program_id(0)
    for part, at in enumerate((0, 4, 5)):

        @pl.when(step == at)
        def _(part=part):
            slots = slot_list(place)
            low = sum(v[part * rank : (part + 1) * rank].astype(jnp.float32) for v in lows)
            low = low.astype(jnp.bfloat16).astype(jnp.float32)
            for g, table in enumerate((own_table, end_table)):
                row_slots = slots_of_rows(table, storage, rows)
                mine = low[:, g * rows : (g + 1) * rows]
                wide = jnp.concatenate([jnp.where(row_slots == s, mine, 0.0) for s in slots], axis=0)
                spread[g * rows : (g + 1) * rows, :] = wide.T.astype(jnp.bfloat16)

    @pl.when(step < 4)
    def _():
        total = (
            given[...]
            + dot(spread[...], up[...])
            + dot(x[0, :, :half], q_core[...])
            + dot(x[0, :, half:], q_other[...])
        ).astype(jnp.bfloat16)
        own[...] = total[:rows]
        end[...] = total[rows:]

    @pl.when(step >= 4)
    def _():
        total = (given[...] + dot(spread[...], up[...])).astype(jnp.bfloat16)
        own[...] = total[:rows]
        end[...] = total[rows:]


def project_last(place, own_table, end_table, storage, x, queries, up, lows, sums):
    _, rows, width = x.shape
    depth = queries[0].shape[0]
    features = pl.BlockSpec((1, rows, width), lambda n, place: (place[5] ^ place[1], 0, 0))
    tile = pl.BlockSpec((rows // GROUPS, WIDE), lambda n, place: (0, n))
    query = pl.BlockSpec((depth, WIDE), lambda n, place: (0, jnp.minimum(n, 3)))
    low = pl.BlockSpec(lows[0].shape, lambda n, place: (0, 0))
    return pl.pallas_call(
        last_kernel,
        grid_spec=pltpu.PrefetchScalarGridSpec(
            num_scalar_prefetch=1,
            grid=(6,),
            in_specs=[features]
            + [query] * 2
            + [pl.BlockSpec((up.shape[0], WIDE), lambda n, place: (0, n))]
            + [pl.BlockSpec((rows, WIDE), lambda n, place: (0, n))]
            + [in_smem()] * 3
            + [low] * 4,
            out_specs=[tile, tile],
            scratch_shapes=[pltpu.VMEM((rows, 16 * ADAPTER_RANK), jnp.bfloat16)],
        ),
        out_shape=[jax.ShapeDtypeStruct((rows // GROUPS, 6 * WIDE), jnp.bfloat16)] * 2,
        compiler_params=kernel_params(),
        cost_estimate=cost(2 * rows * (width + 256) * 6 * WIDE, 2 * rows * width + 2 * width * width + 36 * rows * WIDE, 0),
        name="project_last",
    )(place, x, *queries, up, sums, own_table, end_table, storage, *lows)


def attention_kernel(
    place, table, prefix, pages, own, back, k_pool, v_pool, q_gain, k_gain, cosine, sine,
    chosen_own, chosen_back, out, cache, low, raw, keys, values, allowed, down,
):
    rows, pool_rows = own.shape[0], k_pool.shape[0]
    page_count = pool_rows // PAGE

    @pl.when(place[6] == 1)
    def _():
        raw[...] = back[...]
        down[...] = chosen_back[:, :ADAPTER_RANK, :].reshape(down.shape)

    @pl.when(place[6] == 0)
    def _():
        raw[...] = own[...]
        down[...] = chosen_own[:, :ADAPTER_RANK, :].reshape(down.shape)

    owner = request_of_rows(table, (rows, 1), 0)
    page = lax.broadcasted_iota(jnp.int32, (1, pool_rows), 1) // PAGE
    seen = jnp.zeros((rows, pool_rows), jnp.int32)
    for j in range(4):
        mine = jnp.zeros((1, pool_rows), jnp.int32)
        for i in range(page_count):
            mine = jnp.where((page == pages[8 * j + i]) & (i < prefix[j]), 1, mine)
        seen = jnp.where(owner == j, mine, seen)
    allowed[:, :pool_rows] = seen
    row = lax.broadcasted_iota(jnp.int32, (rows, rows), 0)
    column = lax.broadcasted_iota(jnp.int32, (rows, rows), 1)
    same = owner == request_of_rows(table, (1, rows), 1)
    allowed[:, pool_rows:] = (same & (column <= row)).astype(jnp.int32)

    def turned(value, gain):
        value = value.astype(jnp.float32)
        mean_sq = jnp.mean(value * value, axis=1, keepdims=True)
        value = value * lax.rsqrt(mean_sq + epsilon) * gain[...]
        other = pltpu.roll(value, HEAD_SIZE // 2, 1)
        return (value * cosine[...] + other * sine[...]).astype(jnp.bfloat16)

    kv_heads = k_pool.shape[1] // HEAD_SIZE
    q_width = out.shape[1]
    per_key = q_width // HEAD_SIZE // kv_heads
    kv_width = kv_heads * HEAD_SIZE
    cache[:, kv_width:] = raw[:, q_width + kv_width :]
    for h in range(kv_heads):
        head = slice(h * HEAD_SIZE, (h + 1) * HEAD_SIZE)
        keys[:pool_rows] = k_pool[:, head]
        values[:pool_rows] = v_pool[:, head]
        k_new = turned(raw[:, q_width + h * HEAD_SIZE : q_width + (h + 1) * HEAD_SIZE], k_gain)
        keys[pool_rows:] = k_new
        cache[:, head] = k_new
        values[pool_rows:] = raw[
            :, q_width + kv_width + h * HEAD_SIZE : q_width + kv_width + (h + 1) * HEAD_SIZE
        ]
        for g in range(per_key):
            place_q = slice((h * per_key + g) * HEAD_SIZE, (h * per_key + g + 1) * HEAD_SIZE)
            query = turned(raw[:, place_q], q_gain)
            scores = lax.dot_general(
                query, keys[...], (((1,), (1,)), ((), ())), preferred_element_type=jnp.float32
            ) * (1.0 / math.sqrt(HEAD_SIZE))
            grown = jnp.where(allowed[...] > 0, jnp.exp(scores), 0.0)
            weights = (grown / jnp.sum(grown, axis=1, keepdims=True)).astype(jnp.bfloat16)
            out[:, place_q] = jnp.dot(
                weights, values[...], preferred_element_type=jnp.float32
            ).astype(jnp.bfloat16)
    terms = lax.dot_general(
        down[...], out[...], (((1,), (1,)), ((), ())), preferred_element_type=jnp.float32
    )
    owner_lane = request_of_rows(table, (1, rows), 1)
    low[...] = sum(
        jnp.where(owner_lane == j, terms[j * ADAPTER_RANK : (j + 1) * ADAPTER_RANK], 0.0)
        for j in range(4)
    )


def attend(place, table, prefix, pages, own, back, k_pool, v_pool, q_gain, k_gain, cosine, sine,
           chosen_own, chosen_back):
    rows = own.shape[0]
    kv_width = k_pool.shape[1]
    q_width = own.shape[1] - 2 * kv_width
    keys = k_pool.shape[0] + rows
    return pl.pallas_call(
        attention_kernel,
        in_specs=[in_smem()] * 4 + [in_vmem()] * 10,
        out_specs=[in_vmem()] * 3,
        out_shape=[
            jax.ShapeDtypeStruct((rows, q_width), jnp.bfloat16),
            jax.ShapeDtypeStruct((rows, 2 * kv_width), jnp.bfloat16),
            jax.ShapeDtypeStruct((ADAPTER_RANK, rows), jnp.float32),
        ],
        scratch_shapes=[
            pltpu.VMEM(own.shape, jnp.bfloat16),
            pltpu.VMEM((keys, HEAD_SIZE), jnp.bfloat16),
            pltpu.VMEM((keys, HEAD_SIZE), jnp.bfloat16),
            pltpu.VMEM((rows, keys), jnp.int32),
            pltpu.VMEM((4 * ADAPTER_RANK, chosen_own.shape[2]), jnp.bfloat16),
        ],
        compiler_params=kernel_params(),
        cost_estimate=cost(4 * rows * keys * q_width, 6 * rows * q_width, rows * keys * (q_width // HEAD_SIZE)),
        name="attend",
    )(place, table, prefix, pages, own, back, k_pool, v_pool, q_gain, k_gain, cosine, sine,
      chosen_own, chosen_back)


def columns_kernel(count, place, attended, *refs):
    sources, outs, (held, sems) = refs[: 4 * count], refs[-2 - BLOCKS : -2], refs[-2:]
    rows = attended.shape[0]
    if len(refs) > 4 * count + BLOCKS + 2:
        low = refs[4 * count]
        for out in outs:
            out[rows:, :rows] = low[...].astype(jnp.bfloat16)
            out[rows:, rows:] = jnp.zeros((low.shape[0], out.shape[1] - rows), jnp.bfloat16)
    at_end = place[6] == 1

    def copies(chunk, end, k):
        pair = sources[4 * chunk + (0 if end else 2) :][:2]
        return [
            pltpu.make_async_copy(
                pair[c].at[place[1] ^ k],
                held.at[k, :, (2 * chunk + c) * HEAD_SIZE : (2 * chunk + c + 1) * HEAD_SIZE],
                sems.at[chunk, k, c],
            )
            for c in range(2)
        ]

    for end in (True, False):

        @pl.when(at_end if end else jnp.logical_not(at_end))
        def _(end=end):
            for k in range(BLOCKS):
                for chunk in range(count):
                    for copy in copies(chunk, end, k):
                        copy.start()

    for k in range(BLOCKS):
        for chunk in range(count):
            for copy in copies(chunk, False, k):
                copy.wait()
        outs[k][:rows] = dot(attended[...], held[k]).astype(jnp.bfloat16)


def project_columns(place, attended, chunks, low=None):
    more = [] if low is None else [low]
    rows = attended.shape[0] + (0 if low is None else low.shape[0])
    depth = chunks[0][0].shape[1]
    width = WIDE * len(chunks)
    return pl.pallas_call(
        functools.partial(columns_kernel, len(chunks)),
        in_specs=[in_smem(), in_vmem()]
        + [pl.BlockSpec(memory_space=pl.ANY)] * (4 * len(chunks))
        + [in_vmem()] * len(more),
        out_specs=[in_vmem()] * BLOCKS,
        out_shape=[jax.ShapeDtypeStruct((rows, width), jnp.bfloat16)] * BLOCKS,
        scratch_shapes=[
            pltpu.VMEM((BLOCKS, depth, width), jnp.bfloat16),
            pltpu.SemaphoreType.DMA((len(chunks), BLOCKS, 2)),
        ],
        compiler_params=kernel_params(),
        cost_estimate=cost(2 * rows * depth * BLOCKS * width, 2 * (rows * depth + depth * BLOCKS * width + rows * BLOCKS * width), 0),
        name="project_columns",
    )(place, attended, *[w for chunk in chunks for w in chunk], *more)


def sum_kernel(place, table, chosen_own, chosen_back, *refs):
    parts, (out, up) = refs[:12], refs[12:]
    rank, rows = ADAPTER_RANK, out.shape[0]

    @pl.when(place[6] == 1)
    def _():
        up[...] = chosen_back[:, rank:, :].reshape(up.shape)

    @pl.when(place[6] == 0)
    def _():
        up[...] = chosen_own[:, rank:, :].reshape(up.shape)

    low = sum(v[rows:, :rows].astype(jnp.float32) for v in parts[:4])
    low = low.astype(jnp.bfloat16).astype(jnp.float32)
    owner = request_of_rows(table, (1, rows), 1)
    wide = jnp.concatenate([jnp.where(owner == j, low, 0.0) for j in range(4)], axis=0)
    spread = wide.T.astype(jnp.bfloat16)
    core = place[0]
    for i in range(PLANES):
        first, at = (0, i * WIDE) if i < 2 else (4 * (i - 1), 0)
        total = sum(v[:rows, at : at + WIDE].astype(jnp.float32) for v in parts[first : first + 4])
        for c, mine in ((core, total[:, :HEAD_SIZE]), (1 - core, total[:, HEAD_SIZE:])):
            begin = pl.multiple_of((2 * place[7 + i] + c) * HEAD_SIZE, HEAD_SIZE)
            columns = pl.ds(begin, HEAD_SIZE)
            out[:, columns] = (
                mine + jnp.dot(spread, up[:, columns], preferred_element_type=jnp.float32)
            ).astype(jnp.bfloat16)


def sum_columns(place, table, chosen_own, chosen_back, parts):
    rows = parts[-1].shape[0]
    width = chosen_own.shape[2]
    return pl.pallas_call(
        sum_kernel,
        in_specs=[in_smem()] * 2 + [in_vmem()] * 14,
        out_specs=in_vmem(),
        out_shape=jax.ShapeDtypeStruct((rows, width), jnp.bfloat16),
        scratch_shapes=[pltpu.VMEM((4 * ADAPTER_RANK, width), jnp.bfloat16)],
        compiler_params=kernel_params(),
        cost_estimate=cost(2 * rows * width * (8 + 4 * ADAPTER_RANK), 12 * rows * width, 0),
        name="sum_columns",
    )(place, table, chosen_own, chosen_back, *parts)


def shards_by_plane(
    hidden_input,
    input_norm_gain,
    query_norm_gain,
    key_norm_gain,
    query_weight,
    key_value_weight,
    output_weight,
    adapter_down_qkv,
    adapter_down_output,
    adapter_up_query,
    adapter_up_key_value,
    adapter_up_output,
    pool,
    lengths,
    cached_prefix_pages,
    prefix_page_table,
    adapter_of_request,
    adapter_storage,
):
    request_index = lax.axis_index("req")
    plane, core = request_index // 2, request_index % 2
    block = lax.axis_index("mlp")
    at_end = (plane == 0) | (plane == PLANES - 1)
    near_end = jnp.where(plane < 2, 0, PLANES - 1)
    near = jnp.where(at_end, jnp.where(plane == 0, 1, 2), near_end)
    other = jnp.where(at_end, jnp.where(plane == 0, 2, 1), 3 - plane)
    place = jnp.stack(
        [core, block, plane, near_end, 3 - plane, 3 - near_end, at_end.astype(jnp.int32)]
        + [plane, near, other, 6 - plane - near - other]
    ).astype(jnp.int32)
    row_count, block_width = hidden_input.shape
    key_value_width = KEY_VALUE_HEADS // BLOCKS * HEAD_SIZE
    key_value_begin = block * key_value_width

    half_rows = row_count // 2
    table = jnp.concatenate([lengths[0], adapter_of_request[0, :, 0]])
    q_2 = along(query_weight, MIDDLE)
    end_hidden = along(hidden_input, INWARD)
    own_1, own_2 = swap_blocks(hidden_input, 1), swap_blocks(hidden_input, 2)
    kv_0 = lax.dynamic_slice_in_dim(key_value_weight, key_value_begin, key_value_width, 2)
    up_kv = lax.dynamic_slice_in_dim(adapter_up_key_value, key_value_begin, key_value_width, 3)
    rest_0 = pack_rows(
        table,
        kv_0.reshape(-1, 2 * key_value_width),
        adapter_down_qkv,
        adapter_up_query,
        up_kv.reshape(up_kv.shape[0], ADAPTER_RANK, 2 * key_value_width),
        adapter_down_output,
        adapter_up_output,
    )
    rest_0, end_hidden, q_2, own_1, own_2, query_later = gate(
        [rest_0, end_hidden, q_2, own_1, own_2, query_weight], []
    )
    rest_1 = along(rest_0, INWARD)
    rest_2 = along(rest_0, MIDDLE)
    own_3 = swap_blocks(own_1[:half_rows], 2)
    own_4 = swap_blocks(own_2[half_rows:], 1)
    end_1, end_2 = swap_blocks(end_hidden, 1), swap_blocks(end_hidden, 2)
    rest_1, rest_2, own_3, own_4, end_1, end_2, query_later = gate(
        [rest_1, rest_2, own_3, own_4, end_1, end_2, query_later], []
    )
    end_table = rest_1[7 * ADAPTER_RANK, :8].astype(jnp.int32)
    q_1 = along(query_later, INWARD)
    rest_3 = along(rest_1, MIDDLE)
    end_3 = swap_blocks(end_1[:half_rows], 2)
    end_4 = swap_blocks(end_2[half_rows:], 1)
    q_0x, q_2x = along(query_later, CORES), along(q_2, CORES)
    rest_0x, rest_1x, rest_2x = (along(v, CORES) for v in (rest_0, rest_1, rest_2))

    gain = input_norm_gain.astype(jnp.float32).reshape(BLOCKS, block_width)
    x, own_done = norm_rows(place, gain, [hidden_input, own_1, own_2, own_3, own_4], 0, None)
    x, end_done = norm_rows(place, gain, [end_hidden, end_1, end_2, end_3, end_4], 1, x)
    wo_0 = jnp.transpose(output_weight, (1, 0, 2))
    q_1, rest_3, wo_0 = gate(
        [q_1, rest_3, wo_0], [q_0x, q_2x, rest_0x, rest_1x, rest_2x, end_done]
    )
    q_3 = along(q_1, MIDDLE)
    wo_1 = along(wo_0, NEAR)
    q_1x = along(q_1, CORES)
    rest_3x = along(rest_3, CORES)

    packed = [rest_0, rest_1, rest_2, rest_3, rest_0x, rest_1x, rest_2x, rest_3x]
    low, chosen_own, chosen_end, up = rank_terms(
        place, table, end_table, adapter_storage, x, packed, 2 * key_value_width
    )
    lows = [low] + to_blocks([low] * BLOCKS)
    chosen_back = along(chosen_end, OUTWARD)

    sums, first_done = project_first(
        place,
        x,
        [query_weight, q_0x, q_1, q_1x, q_2, q_2x],
        [v for pair in zip(packed[:4], packed[4:]) for v in pair],
    )
    q_3x = along(q_3, CORES)
    wo_0, wo_1 = gate([wo_0, wo_1], [first_done, chosen_back] + lows)
    wo_mid1, wo_mid2 = along(wo_0, MIDDLE), along(wo_1, MIDDLE)
    raw_own, raw_end = project_last(
        place, table, end_table, adapter_storage, x, [q_3, q_3x], up, lows, sums
    )
    raw_back = along(raw_end, OUTWARD)
    wo_0x, wo_1x = along(wo_0, CORES), along(wo_1, CORES)
    (wo_mid1,) = gate([wo_mid1], [raw_back, wo_0x, wo_1x])
    wo_out2 = along(wo_mid1, OUTWARD)

    cached = lax.dynamic_slice_in_dim(pool, key_value_begin, key_value_width, 2)
    _, _, token_positions, _ = row_tables(
        lengths[0], cached_prefix_pages[0], prefix_page_table[0], row_count
    )
    half_width = HEAD_SIZE // 2
    inverse_freq = jnp.exp(
        jnp.arange(half_width, dtype=jnp.float32) * (-2.0 / HEAD_SIZE) * math.log(rope_base)
    )
    angles = token_positions.astype(jnp.float32)[:, None] * inverse_freq[None, :]
    cosine, sine = jnp.cos(angles), jnp.sin(angles)
    attended, cache, low_out = attend(
        place,
        table,
        cached_prefix_pages[0],
        prefix_page_table[0].reshape(-1),
        raw_own,
        raw_back,
        cached[:, 0],
        cached[:, 1],
        query_norm_gain.astype(jnp.float32)[None, :],
        key_norm_gain.astype(jnp.float32)[None, :],
        jnp.concatenate([cosine, cosine], axis=1),
        jnp.concatenate([-sine, sine], axis=1),
        chosen_own,
        chosen_back,
    )
    new_cache = cache.reshape(row_count, 2, key_value_width)

    near_parts = project_columns(
        place, attended, [(wo_0, wo_0x, wo_0, wo_0x), (wo_1, wo_1x, wo_1, wo_1x)], low_out
    )
    parts = [near_parts[0]] + to_blocks(near_parts)
    (wo_mid2,) = gate([wo_mid2], [attended])
    wo_out3 = along(wo_mid2, OUTWARD)
    (wo_out2,) = gate([wo_out2], near_parts[:1])
    mid_parts = project_columns(
        place, attended, [(wo_out2, along(wo_out2, CORES), wo_mid1, along(wo_mid1, CORES))]
    )
    parts += [mid_parts[0]] + to_blocks(mid_parts)
    (wo_out3,) = gate([wo_out3], parts)
    last_parts = project_columns(
        place, attended, [(wo_out3, along(wo_out3, CORES), wo_mid2, along(wo_mid2, CORES))]
    )
    parts += [last_parts[0]] + to_blocks(last_parts)
    attention_update = sum_columns(place, table, chosen_own, chosen_back, parts)
    return (attention_update, new_cache)


def solution(mesh):
    return jax.shard_map(
        shards_by_plane if planes_fit(mesh) else shards,
        mesh=mesh,
        in_specs=(
            P("req", "mlp"),
            P(),
            P(),
            P(),
            P("req", "mlp"),
            P("req", None, None),
            P("mlp", None, "req"),
            P("req", None, "mlp"),
            P("req", None, "mlp"),
            P("req", None, "mlp"),
            P("req", None, None, None),
            P("req", None, "mlp"),
            P("req", None, None),
            P("req", None),
            P("req", None),
            P("req", None, None),
            P("req", None, None),
            P(),
        ),
        out_specs=(P("req", "mlp"), P("req", None, "mlp")),
        check_vma=False,
    )
```

```python
import functools
import math

import jax
import jax.numpy as jnp
from jax import lax
from jax.experimental import pallas as pl
from jax.experimental.pallas import tpu as pltpu
from jax.sharding import PartitionSpec as P

QUERY_HEADS = 32
KEY_VALUE_HEADS = 8
HEAD_SIZE = 128
ADAPTER_RANK = 16
PAGE = 64


epsilon = 1e-06
rope_base = 1000000.0


def root_mean_scale(values, gain_vec):
    mean_sq = jnp.mean(values * values, axis=-1, keepdims=True)
    return values * lax.rsqrt(mean_sq + epsilon) * gain_vec.astype(jnp.float32)


def rotary_embed(values, token_positions):
    half_width = values.shape[-1] // 2
    inverse_freq = jnp.exp(
        jnp.arange(half_width, dtype=jnp.float32) * (-2.0 / values.shape[-1]) * math.log(rope_base)
    )
    angles = token_positions.astype(jnp.float32)[:, None] * inverse_freq[None, :]
    cosine = jnp.cos(angles)[:, None, :]
    sine_part = jnp.sin(angles)[:, None, :]
    front = values[..., :half_width]
    back = values[..., half_width:]
    return jnp.concatenate(
        [front * cosine - back * sine_part, back * cosine + front * sine_part], axis=-1
    )


def row_tables(lengths_row, prefix_row, page_rows, row_count):
    ends_at = jnp.cumsum(lengths_row)
    starts_at = ends_at - lengths_row
    row_ids = jnp.arange(row_count, dtype=jnp.int32)
    owners = jnp.sum((row_ids[:, None] >= ends_at[None, :]).astype(jnp.int32), axis=1)
    group_members = owners[:, None] == jnp.arange(lengths_row.shape[0], dtype=jnp.int32)[None, :]
    offsets = PAGE * prefix_row[None, :] + row_ids[:, None] - starts_at[None, :]
    token_positions = jnp.sum(jnp.where(group_members, offsets, 0), axis=1)
    page_ids = jnp.arange(page_rows.shape[1], dtype=jnp.int32)
    listed = (page_rows[:, :, None] == page_ids[None, None, :]) & (
        page_ids[None, :, None] < prefix_row[:, None, None]
    )
    page_used = jnp.sum(listed.astype(jnp.float32), axis=1)
    return (owners, group_members, token_positions, page_used)


def apply_adapter(lowrank_inner, group_members, chosen_up):
    masked = lowrank_inner[:, None, :] * group_members.astype(lowrank_inner.dtype)[:, :, None]
    return jnp.einsum("gjr,jrc->gc", masked, chosen_up, preferred_element_type=jnp.float32)


def select_rows(terms, group_members):
    return jnp.sum(terms * group_members.astype(jnp.float32)[:, :, None], axis=1)


def shards(
    hidden_input,
    input_norm_gain,
    query_norm_gain,
    key_norm_gain,
    query_weight,
    key_value_weight,
    output_weight,
    adapter_down_qkv,
    adapter_down_output,
    adapter_up_query,
    adapter_up_key_value,
    adapter_up_output,
    pool,
    lengths,
    cached_prefix_pages,
    prefix_page_table,
    adapter_of_request,
    adapter_storage,
):
    feature_group_count = lax.axis_size("mlp")
    feature_group_index = lax.axis_index("mlp")
    whole = lax.all_gather(hidden_input, "mlp", axis=1, tiled=True)
    row_count, full_width = whole.shape
    normalized_input = root_mean_scale(whole.astype(jnp.float32), input_norm_gain).astype(
        jnp.bfloat16
    )
    owners, group_members, token_positions, page_used = row_tables(
        lengths[0], cached_prefix_pages[0], prefix_page_table[0], row_count
    )
    q_width = query_weight.shape[1]
    query_head_rows = q_width // HEAD_SIZE
    key_value_local = max(1, KEY_VALUE_HEADS // feature_group_count)
    key_value_width = key_value_local * HEAD_SIZE
    key_value_begin = (
        feature_group_index * query_head_rows // (QUERY_HEADS // KEY_VALUE_HEADS) * HEAD_SIZE
    )
    own_wkv = lax.dynamic_slice_in_dim(key_value_weight, key_value_begin, key_value_width, 2)
    request_key_value_up = lax.dynamic_slice_in_dim(
        adapter_up_key_value, key_value_begin, key_value_width, 3
    )
    gathered = (
        lax.all_gather(adapter_down_qkv, "req", axis=0, tiled=True),
        lax.all_gather(adapter_down_output, "req", axis=0, tiled=True),
        lax.all_gather(adapter_up_query, "req", axis=0, tiled=True),
        lax.all_gather(request_key_value_up, "req", axis=0, tiled=True),
        lax.all_gather(adapter_up_output, "req", axis=0, tiled=True),
    )
    slot_indices = jnp.take(adapter_storage, adapter_of_request[0, :, 0], axis=0)
    chosen_down = jnp.take(gathered[0], slot_indices, axis=0)
    output_down = jnp.take(gathered[1], slot_indices, axis=0)
    query_up_part = jnp.take(gathered[2], slot_indices, axis=0)
    key_value_up = jnp.take(gathered[3], slot_indices, axis=0)
    output_up = jnp.take(gathered[4], slot_indices, axis=0)
    feature_cols = full_width // feature_group_count
    own_normed = lax.dynamic_slice_in_dim(
        normalized_input, feature_group_index * feature_cols, feature_cols, 1
    )
    low_terms = jnp.einsum(
        "gd,jkd->gjk", own_normed, chosen_down, preferred_element_type=jnp.float32
    )
    lowrank_inner = lax.psum(select_rows(low_terms, group_members).astype(jnp.bfloat16), "mlp")
    q_part = lax.all_gather(query_weight, "req", axis=0, tiled=True)
    kv_part = lax.all_gather(own_wkv, "req", axis=0, tiled=True)
    query_width_total = jnp.dot(normalized_input, q_part, preferred_element_type=jnp.float32)
    kv_total = jnp.dot(
        normalized_input,
        kv_part.reshape(kv_part.shape[0], 2 * key_value_width),
        preferred_element_type=jnp.float32,
    )
    query_width_total, kv_total = (query_width_total, kv_total)
    query_plain = (
        query_width_total
        + apply_adapter(lowrank_inner[:, 0:ADAPTER_RANK], group_members, query_up_part)
    ).astype(jnp.bfloat16)
    key_lowrank_part = apply_adapter(
        lowrank_inner[:, ADAPTER_RANK : 2 * ADAPTER_RANK], group_members, key_value_up[:, :, 0]
    )
    value_lowrank_part = apply_adapter(
        lowrank_inner[:, 2 * ADAPTER_RANK : 3 * ADAPTER_RANK], group_members, key_value_up[:, :, 1]
    )
    key_value_plain = (
        kv_total.reshape(row_count, 2, key_value_width)
        + jnp.stack([key_lowrank_part, value_lowrank_part], axis=1)
    ).astype(jnp.bfloat16)
    cached = lax.dynamic_slice_in_dim(pool, key_value_begin, key_value_width, 2)
    pool_token_rows = cached.shape[0]
    query_rotated = rotary_embed(
        root_mean_scale(
            query_plain.astype(jnp.float32).reshape(row_count, query_head_rows, HEAD_SIZE),
            query_norm_gain,
        ),
        token_positions,
    ).astype(jnp.bfloat16)
    key_rotated = rotary_embed(
        root_mean_scale(
            key_value_plain[:, 0]
            .astype(jnp.float32)
            .reshape(row_count, key_value_local, HEAD_SIZE),
            key_norm_gain,
        ),
        token_positions,
    ).astype(jnp.bfloat16)
    cache_columns = KEY_VALUE_HEADS * HEAD_SIZE // feature_group_count
    own_offset = feature_group_index * cache_columns - key_value_begin
    local_cache = jnp.stack(
        [key_rotated.reshape(row_count, key_value_width), key_value_plain[:, 1]], axis=1
    )
    new_cache = lax.dynamic_slice_in_dim(local_cache, own_offset, cache_columns, 2)
    key_matrix = jnp.concatenate(
        [cached[:, 0].reshape(pool_token_rows, key_value_local, HEAD_SIZE), key_rotated], axis=0
    )
    value_matrix = jnp.concatenate(
        [
            cached[:, 1].reshape(pool_token_rows, key_value_local, HEAD_SIZE),
            key_value_plain[:, 1].reshape(row_count, key_value_local, HEAD_SIZE),
        ],
        axis=0,
    )
    pool_ok = jnp.dot(group_members.astype(jnp.float32), page_used, precision=lax.Precision.HIGHEST)
    pool_ok = jnp.repeat(pool_ok, PAGE, axis=1) > 0.5
    row_ids = jnp.arange(row_count, dtype=jnp.int32)
    causal = (owners[:, None] == owners[None, :]) & (row_ids[None, :] <= row_ids[:, None])
    allowed = jnp.concatenate([pool_ok, causal], axis=1)
    query_rows = query_rotated.reshape(
        row_count, key_value_local, query_head_rows // key_value_local, HEAD_SIZE
    )
    scores = jnp.einsum(
        "gkhd,skd->khgs", query_rows, key_matrix, preferred_element_type=jnp.float32
    ) / math.sqrt(HEAD_SIZE)
    exp_scores = jnp.where(allowed[None, None], jnp.exp(scores), 0.0)
    softmax = (exp_scores / jnp.sum(exp_scores, axis=-1, keepdims=True)).astype(jnp.bfloat16)
    attended = jnp.einsum(
        "khgs,skd->gkhd", softmax, value_matrix, preferred_element_type=jnp.float32
    )
    attended = attended.astype(jnp.bfloat16).reshape(row_count, q_width)
    out_terms = jnp.einsum("gc,jrc->gjr", attended, output_down, preferred_element_type=jnp.float32)
    lowrank_result = lax.psum(select_rows(out_terms, group_members), "mlp").astype(jnp.bfloat16)
    partial_value = jnp.einsum(
        "gc,cnk->gnk",
        attended,
        lax.all_gather(output_weight, "req", axis=2, tiled=True),
        preferred_element_type=jnp.float32,
    )
    summed_output = lax.psum_scatter(
        partial_value.reshape(row_count, full_width).astype(jnp.bfloat16),
        "mlp",
        scatter_dimension=1,
        tiled=True,
    ).astype(jnp.float32)
    attention_update = (
        summed_output + apply_adapter(lowrank_result, group_members, output_up)
    ).astype(jnp.bfloat16)
    return (attention_update, new_cache)


PLANES = 4
BLOCKS = 4
GROUPS = 2
WIDE = 256


def planes_fit(mesh):
    return mesh.shape["req"] == 2 * PLANES and mesh.shape["mlp"] == BLOCKS


def plane_pairs(pairs):
    return [(2 * a + core, 2 * b + core) for a, b in pairs for core in range(2)]


INWARD = plane_pairs([(0, 1), (3, 2)])
MIDDLE = plane_pairs([(1, 2), (2, 1)])
OUTWARD = plane_pairs([(1, 0), (2, 3)])
NEAR = plane_pairs([(0, 1), (1, 0), (2, 3), (3, 2)])
CORES = [(r, r ^ 1) for r in range(2 * PLANES)]


def along(value, pairs):
    return lax.ppermute(value, "req", pairs)


def swap_blocks(value, k):
    return lax.ppermute(value, "mlp", [(b, b ^ k) for b in range(BLOCKS)])


def to_blocks(pieces):
    return [
        lax.ppermute(piece, "mlp", [(b, b ^ k) for b in range(BLOCKS)])
        for k, piece in enumerate(pieces)
        if k > 0
    ]


def gate_kernel(*refs):
    del refs


def gate(values, earlier, mebibytes=60):
    return pl.pallas_call(
        gate_kernel,
        in_specs=[pl.BlockSpec(memory_space=pl.ANY)] * (len(values) + len(earlier)),
        out_specs=[pl.BlockSpec(memory_space=pl.ANY)] * len(values),
        out_shape=[jax.ShapeDtypeStruct(v.shape, v.dtype) for v in values],
        input_output_aliases={i: i for i in range(len(values))},
        compiler_params=kernel_params(mebibytes),
        name="gate",
    )(*values, *earlier)


def in_vmem():
    return pl.BlockSpec(memory_space=pltpu.VMEM)


def in_smem():
    return pl.BlockSpec(memory_space=pltpu.SMEM)


def cost(flops, bytes_accessed, transcendentals=0):
    return pl.CostEstimate(
        flops=flops, bytes_accessed=bytes_accessed, transcendentals=transcendentals
    )


def kernel_params(mebibytes):
    return pltpu.CompilerParams(vmem_limit_bytes=mebibytes * 1024 * 1024)


def request_of_rows(table, shape, axis):
    row = lax.broadcasted_iota(jnp.int32, shape, axis)
    end, owner = table[0], jnp.zeros(shape, jnp.int32)
    for j in range(1, 4):
        owner = jnp.where(row >= end, j, owner)
        end = end + table[j]
    return owner


def slots_of_rows(table, storage, row_count):
    owner = request_of_rows(table, (1, row_count), 1)
    slots = jnp.zeros((1, row_count), jnp.int32) + storage[table[4]]
    for j in range(1, 4):
        slots = jnp.where(owner == j, storage[table[4 + j]], slots)
    return slots


def slot_list(place):
    core = place[0]
    return [4 * place[2 + i] + 2 * c + s for c in (core, 1 - core) for i in range(4) for s in range(2)]


def dot(a, b):
    return jnp.dot(a, b, preferred_element_type=jnp.float32)


def core_columns(c, half):
    return pl.ds(pl.multiple_of(c * half, half), half)


def norm_kernel(place, gain, p0, p1, p2, p3, p4, *refs):
    out, done = refs[-2:]
    pieces = [p[...].astype(jnp.float32) for p in (p0, p1, p2)]
    late = pl.program_id(0) >= pl.num_programs(0) // 2
    pieces.append(jnp.where(late, p4[...], p3[...]).astype(jnp.float32))
    total = sum(jnp.sum(v * v, axis=1, keepdims=True) for v in pieces)
    half = pieces[0].shape[1] // 2
    scale = lax.rsqrt(total / (BLOCKS * 2 * half) + epsilon)
    core = place[0]
    for k, v in enumerate(pieces):
        normed = (v * scale * gain[pl.ds(place[1] ^ k, 1), :]).astype(jnp.bfloat16)
        first = 2 * place[11 + k]
        out[:, core_columns(first + core, half)] = normed[:, :half]
        out[:, core_columns(first + 1 - core, half)] = normed[:, half:]
    done[...] = jnp.zeros(done.shape, jnp.float32)


def norm_rows(place, gain, pieces, group, given):
    tiles, width = 4, gain.shape[1]
    rows = pieces[0][0].shape[0]
    tile = rows // tiles
    more = [] if given is None else [given]
    index = [lambda i: i] * 3
    index += [lambda i: jnp.minimum(i, tiles // 2 - 1), lambda i: jnp.maximum(i - tiles // 2, 0)]
    return pl.pallas_call(
        norm_kernel,
        grid_spec=pltpu.PrefetchScalarGridSpec(
            num_scalar_prefetch=1,
            grid=(tiles,),
            in_specs=[pl.BlockSpec((BLOCKS, width), lambda i, place: (0, 0))]
            + [
                pl.BlockSpec((tile, width), lambda i, place, f=f, at=at: (f + at(i), 0))
                for (_, f), at in zip(pieces, index)
            ]
            + [pl.BlockSpec(memory_space=pl.ANY)] * len(more),
            out_specs=[
                pl.BlockSpec((tile, BLOCKS * width), lambda i, place: (tiles * group + i, 0)),
                pl.BlockSpec((8, 128), lambda i, place: (0, 0)),
            ],
        ),
        out_shape=[
            jax.ShapeDtypeStruct((GROUPS * rows, BLOCKS * width), jnp.bfloat16),
            jax.ShapeDtypeStruct((8, 128), jnp.float32),
        ],
        input_output_aliases={7: 0} if more else {},
        compiler_params=kernel_params(56),
        cost_estimate=cost(16 * rows * width, 4 * BLOCKS * rows * width),
        name="norm_rows",
    )(place, gain, *[p for p, _ in pieces], *more)


SLOT_ROWS = 128


def pack_kernel(table, kv, down_qkv, up_query, up_kv, down_out, up_out, out):
    depth, kv_columns = kv.shape
    rank = ADAPTER_RANK
    out[2 * SLOT_ROWS :, :kv_columns] = kv[: depth // 2]
    out[2 * SLOT_ROWS :, kv_columns:] = kv[depth // 2 :]
    for s in range(2):
        first = s * SLOT_ROWS
        out[first : first + 3 * rank] = down_qkv[s]
        out[first + 3 * rank : first + 4 * rank] = up_query[s]
        out[first + 4 * rank : first + 5 * rank, :kv_columns] = up_kv[s]
        out[first + 4 * rank : first + 5 * rank, kv_columns:] = jnp.zeros(
            (rank, out.shape[1] - kv_columns), jnp.bfloat16
        )
        out[first + 5 * rank : first + 6 * rank] = down_out[s]
        out[first + 6 * rank : first + 7 * rank] = up_out[s]
    shape = (rank, out.shape[1])
    lane = lax.broadcasted_iota(jnp.int32, shape, 1)
    numbers = jnp.zeros(shape, jnp.float32)
    for i in range(8):
        numbers = jnp.where(lane == i, table[i].astype(jnp.float32), numbers)
    for s in range(2):
        out[s * SLOT_ROWS + 7 * rank : (s + 1) * SLOT_ROWS] = numbers.astype(jnp.bfloat16)


def pack_rows(table, kv, *adapters):
    width = adapters[0].shape[2]
    return pl.pallas_call(
        pack_kernel,
        in_specs=[in_smem()] + [in_vmem()] * 6,
        out_specs=in_vmem(),
        out_shape=jax.ShapeDtypeStruct((2 * SLOT_ROWS + kv.shape[0] // 2, width), jnp.bfloat16),
        compiler_params=kernel_params(56),
        cost_estimate=cost(0, 4 * width * (2 * SLOT_ROWS + kv.shape[0] // 2), 0),
        name="pack_rows",
    )(table, kv, *adapters)


def rank_kernel(place, own_table, end_table, storage, x, *refs):
    packed, (low, chosen_own, chosen_end, up, up_kv, down) = refs[:8], refs[8:]
    slots = slot_list(place)
    rank, rows, q_width = ADAPTER_RANK, x.shape[0] // GROUPS, x.shape[1]
    kv_columns, half, core = up_kv.shape[1], q_width // 2, place[0]
    for t, ref in enumerate(packed):
        for s in range(2):
            i, first = 2 * t + s, s * SLOT_ROWS
            for c, columns in ((core, slice(0, half)), (1 - core, slice(half, q_width))):
                down[3 * rank * i : 3 * rank * (i + 1), columns] = ref[
                    first : first + 3 * rank, core_columns(c, half)
                ]
            up[rank * i : rank * (i + 1), :] = ref[first + 3 * rank : first + 4 * rank, :]
            up_kv[rank * i : rank * (i + 1), :] = ref[
                first + 4 * rank : first + 5 * rank, :kv_columns
            ]
    for g, (table, chosen) in enumerate(((own_table, chosen_own), (end_table, chosen_end))):
        terms = lax.dot_general(
            down[...],
            x[g * rows : (g + 1) * rows, :],
            (((1,), (1,)), ((), ())),
            preferred_element_type=jnp.float32,
        )
        row_slots = slots_of_rows(table, storage, rows)
        total = jnp.zeros((3 * rank, rows), jnp.float32)
        for i, slot in enumerate(slots):
            total += jnp.where(row_slots == slot, terms[3 * rank * i : 3 * rank * (i + 1)], 0.0)
        low[:, g * rows : (g + 1) * rows] = total.astype(jnp.bfloat16)
        for j in range(4):
            wanted = storage[table[4 + j]]
            for i, slot in enumerate(slots):

                @pl.when(wanted == slot)
                def _(j=j, i=i, chosen=chosen):
                    first = (i % 2) * SLOT_ROWS
                    chosen[j] = packed[i // 2][first + 5 * rank : first + 7 * rank, :]


def rank_terms(place, own_table, end_table, storage, x, packed, kv_columns):
    rows, width = x.shape[0], x.shape[1] // BLOCKS
    chosen = jax.ShapeDtypeStruct((4, 2 * ADAPTER_RANK, width), jnp.bfloat16)
    up = jax.ShapeDtypeStruct((16 * ADAPTER_RANK, width), jnp.bfloat16)
    up_kv = jax.ShapeDtypeStruct((16 * ADAPTER_RANK, kv_columns), jnp.bfloat16)
    low = jax.ShapeDtypeStruct((3 * ADAPTER_RANK, rows), jnp.bfloat16)
    slots = pl.BlockSpec((2 * SLOT_ROWS, width), lambda i, place: (0, 0))
    whole = lambda shape: pl.BlockSpec(shape, lambda i, place: (0,) * len(shape))
    return pl.pallas_call(
        rank_kernel,
        grid_spec=pltpu.PrefetchScalarGridSpec(
            num_scalar_prefetch=1,
            grid=(1,),
            in_specs=[in_smem()] * 3
            + [pl.BlockSpec((rows, width), lambda i, place: (0, place[11]))]
            + [slots] * 8,
            out_specs=[whole(v.shape) for v in (low, chosen, chosen, up, up_kv)],
            scratch_shapes=[pltpu.VMEM((16 * 3 * ADAPTER_RANK, width), jnp.bfloat16)],
        ),
        out_shape=[low, chosen, chosen, up, up_kv],
        compiler_params=kernel_params(56),
        cost_estimate=cost(
            2 * 16 * 3 * ADAPTER_RANK * rows * width, 2 * width * (rows + 18 * SLOT_ROWS + 256)
        ),
        name="rank_terms",
    )(place, own_table, end_table, storage, x, *packed)


def spread_ranks(place, tables, storage, lows, part, spread):
    rank = ADAPTER_RANK
    rows = spread.shape[0] // GROUPS
    slots = slot_list(place)
    low = sum(v[part * rank : (part + 1) * rank].astype(jnp.float32) for v in lows)
    low = low.astype(jnp.bfloat16).astype(jnp.float32)
    for g, table in enumerate(tables):
        row_slots = slots_of_rows(table, storage, rows)
        mine = low[:, g * rows : (g + 1) * rows]
        wide = jnp.concatenate([jnp.where(row_slots == s, mine, 0.0) for s in slots], axis=0)
        spread[g * rows : (g + 1) * rows, :] = wide.T.astype(jnp.bfloat16)


def project_kernel(is_q, place, own_table, end_table, storage, x, *refs):
    sources, lows, up = refs[:8], refs[8:12], refs[12]
    own, end, spread, held, x_held, sems = refs[13:]
    rows, width = own.shape[0], x.shape[1] // BLOCKS
    depth = held.shape[0] // 8

    def copies(chunk):
        block = slice(chunk * width, (chunk + 1) * width)
        first = 0 if is_q else 2 * SLOT_ROWS
        return [pltpu.make_async_copy(x.at[:, block], x_held.at[:, block], sems.at[chunk, 2])] + [
            pltpu.make_async_copy(
                sources[2 * chunk + c].at[first:, :],
                held.at[(2 * chunk + c) * depth : (2 * chunk + c + 1) * depth, :],
                sems.at[chunk, c],
            )
            for c in range(2)
        ]

    for chunk in range(BLOCKS):
        for copy in copies(chunk):
            copy.start()
    tables = (own_table, end_table)
    total = None
    if is_q:
        spread_ranks(place, tables, storage, lows, 0, spread)
        low = dot(spread[...], up[...])
    else:
        low = []
        for part in range(2):
            spread_ranks(place, tables, storage, lows, 1 + part, spread)
            low.append(dot(spread[...], up[:, part * WIDE : (part + 1) * WIDE]))
        low = jnp.concatenate(low, axis=1)
    for chunk in range(BLOCKS):
        for copy in copies(chunk):
            copy.wait()
        w = held[2 * chunk * depth : 2 * (chunk + 1) * depth, :]
        if not is_q:
            columns = own.shape[1]
            w = jnp.concatenate(
                [
                    w[c * depth : (c + 1) * depth, h * columns : (h + 1) * columns]
                    for c in range(2)
                    for h in range(2)
                ],
                axis=0,
            )
        term = dot(x_held[:, chunk * width : (chunk + 1) * width], w)
        total = low + term if total is None else total + term
    total = total.astype(jnp.bfloat16)
    own[...] = total[:rows]
    end[...] = total[rows:]


def project(place, own_table, end_table, storage, x, sources, lows, up, is_q):
    rows, width = x.shape[0], x.shape[1] // BLOCKS
    columns = up.shape[1]
    anywhere = pl.BlockSpec(memory_space=pl.ANY)
    return pl.pallas_call(
        functools.partial(project_kernel, is_q),
        in_specs=[in_smem()] * 4 + [anywhere] * 9 + [in_vmem()] * 5,
        out_specs=[in_vmem()] * 2,
        out_shape=[jax.ShapeDtypeStruct((rows // GROUPS, columns), jnp.bfloat16)] * 2,
        scratch_shapes=[
            pltpu.VMEM((rows, 16 * ADAPTER_RANK), jnp.bfloat16),
            pltpu.VMEM(((8 if is_q else 4) * sources[0].shape[0], width), jnp.bfloat16),
            pltpu.VMEM(x.shape, jnp.bfloat16),
            pltpu.SemaphoreType.DMA((BLOCKS, 3)),
        ],
        compiler_params=kernel_params(56),
        cost_estimate=cost(
            2 * rows * (BLOCKS * width + 256) * columns,
            2 * BLOCKS * width * (rows + columns) + 2 * rows * columns,
        ),
        name="project_query" if is_q else "project_key_value",
    )(place, own_table, end_table, storage, x, *sources, *lows, up)


def attention_kernel(
    place, table, prefix, pages, own, back, kv_own, kv_back, k_pool, v_pool, q_gain, k_gain,
    cosine, sine, chosen_own, chosen_back, out, cache, low, raw, raw_kv, keys, values, allowed, down,
):
    rows, pool_rows = own.shape[0], k_pool.shape[0]
    page_count = pool_rows // PAGE

    @pl.when(place[6] == 1)
    def _():
        raw[...] = back[...]
        raw_kv[...] = kv_back[...]
        down[...] = chosen_back[:, :ADAPTER_RANK, :].reshape(down.shape)

    @pl.when(place[6] == 0)
    def _():
        raw[...] = own[...]
        raw_kv[...] = kv_own[...]
        down[...] = chosen_own[:, :ADAPTER_RANK, :].reshape(down.shape)

    owner = request_of_rows(table, (rows, 1), 0)
    page = lax.broadcasted_iota(jnp.int32, (1, pool_rows), 1) // PAGE
    seen = jnp.zeros((rows, pool_rows), jnp.int32)
    for j in range(4):
        mine = jnp.zeros((1, pool_rows), jnp.int32)
        for i in range(page_count):
            mine = jnp.where((page == pages[8 * j + i]) & (i < prefix[j]), 1, mine)
        seen = jnp.where(owner == j, mine, seen)
    allowed[:, :pool_rows] = seen
    row = lax.broadcasted_iota(jnp.int32, (rows, rows), 0)
    column = lax.broadcasted_iota(jnp.int32, (rows, rows), 1)
    same = owner == request_of_rows(table, (1, rows), 1)
    allowed[:, pool_rows:] = (same & (column <= row)).astype(jnp.int32)

    def turned(value, gain):
        value = value.astype(jnp.float32)
        mean_sq = jnp.mean(value * value, axis=1, keepdims=True)
        value = value * lax.rsqrt(mean_sq + epsilon) * gain[...]
        other = pltpu.roll(value, HEAD_SIZE // 2, 1)
        return (value * cosine[...] + other * sine[...]).astype(jnp.bfloat16)

    kv_heads = k_pool.shape[1] // HEAD_SIZE
    q_width = out.shape[1]
    per_key = q_width // HEAD_SIZE // kv_heads
    kv_width = kv_heads * HEAD_SIZE
    cache[:, kv_width:] = raw_kv[:, kv_width:]
    for h in range(kv_heads):
        head = slice(h * HEAD_SIZE, (h + 1) * HEAD_SIZE)
        keys[:pool_rows] = k_pool[:, head]
        values[:pool_rows] = v_pool[:, head]
        k_new = turned(raw_kv[:, head], k_gain)
        keys[pool_rows:] = k_new
        cache[:, head] = k_new
        values[pool_rows:] = raw_kv[:, kv_width + h * HEAD_SIZE : kv_width + (h + 1) * HEAD_SIZE]
        for g in range(per_key):
            place_q = slice((h * per_key + g) * HEAD_SIZE, (h * per_key + g + 1) * HEAD_SIZE)
            query = turned(raw[:, place_q], q_gain)
            scores = lax.dot_general(
                query, keys[...], (((1,), (1,)), ((), ())), preferred_element_type=jnp.float32
            ) * (1.0 / math.sqrt(HEAD_SIZE))
            grown = jnp.where(allowed[...] > 0, jnp.exp(scores), 0.0)
            weights = (grown / jnp.sum(grown, axis=1, keepdims=True)).astype(jnp.bfloat16)
            out[:, place_q] = jnp.dot(
                weights, values[...], preferred_element_type=jnp.float32
            ).astype(jnp.bfloat16)
    terms = lax.dot_general(
        down[...], out[...], (((1,), (1,)), ((), ())), preferred_element_type=jnp.float32
    )
    owner_lane = request_of_rows(table, (1, rows), 1)
    low[...] = sum(
        jnp.where(owner_lane == j, terms[j * ADAPTER_RANK : (j + 1) * ADAPTER_RANK], 0.0)
        for j in range(4)
    )


def attend(place, table, prefix, pages, own, back, kv_own, kv_back, k_pool, v_pool, q_gain, k_gain,
           cosine, sine, chosen_own, chosen_back):
    rows, q_width = own.shape
    kv_width = k_pool.shape[1]
    keys = k_pool.shape[0] + rows
    return pl.pallas_call(
        attention_kernel,
        in_specs=[in_smem()] * 4 + [in_vmem()] * 12,
        out_specs=[in_vmem()] * 3,
        out_shape=[
            jax.ShapeDtypeStruct((rows, q_width), jnp.bfloat16),
            jax.ShapeDtypeStruct((rows, 2 * kv_width), jnp.bfloat16),
            jax.ShapeDtypeStruct((ADAPTER_RANK, rows), jnp.float32),
        ],
        scratch_shapes=[
            pltpu.VMEM(own.shape, jnp.bfloat16),
            pltpu.VMEM(kv_own.shape, jnp.bfloat16),
            pltpu.VMEM((keys, HEAD_SIZE), jnp.bfloat16),
            pltpu.VMEM((keys, HEAD_SIZE), jnp.bfloat16),
            pltpu.VMEM((rows, keys), jnp.int32),
            pltpu.VMEM((4 * ADAPTER_RANK, chosen_own.shape[2]), jnp.bfloat16),
        ],
        compiler_params=kernel_params(56),
        cost_estimate=cost(4 * rows * keys * q_width, 6 * rows * q_width, rows * keys * (q_width // HEAD_SIZE)),
        name="attend",
    )(place, table, prefix, pages, own, back, kv_own, kv_back, k_pool, v_pool, q_gain, k_gain,
      cosine, sine, chosen_own, chosen_back)


def columns_kernel(count, place, attended, *refs):
    sources, rest = refs[: 4 * count], refs[4 * count :]
    low = rest[0] if len(rest) > 2 * BLOCKS + 4 else None
    outs, made, (rows_held, held, sems, out_sems) = rest[-2 * BLOCKS - 4 : -BLOCKS - 4], rest[-BLOCKS - 4 : -4], rest[-4:]
    rows = attended.shape[0]
    at_end = place[6] == 1

    def copies(chunk, end, k):
        pair = sources[4 * chunk + (0 if end else 2) :][:2]
        return [
            pltpu.make_async_copy(
                pair[c].at[place[1] ^ k], held.at[chunk, c, k], sems.at[chunk, k, c]
            )
            for c in range(2)
        ]

    given = pltpu.make_async_copy(attended, rows_held, sems.at[count, 0, 0])
    given.start()
    for end in (True, False):

        @pl.when(at_end if end else jnp.logical_not(at_end))
        def _(end=end):
            for k in (3, 2, 1, 0):
                for chunk in range(count):
                    for copy in copies(chunk, end, k):
                        copy.start()

    given.wait()
    sent = []
    for k in (3, 2, 1, 0):
        for chunk in range(count):
            for copy in copies(chunk, False, k):
                copy.wait()
        w = jnp.concatenate([held[chunk, c, k] for chunk in range(count) for c in range(2)], axis=1)
        made[k][:rows] = dot(rows_held[...], w).astype(jnp.bfloat16)
        if low is not None:
            made[k][rows:, :rows] = low[...].astype(jnp.bfloat16)
            made[k][rows:, rows:] = jnp.zeros(
                (low.shape[0], made[k].shape[1] - rows), jnp.bfloat16
            )
        sent.append(pltpu.make_async_copy(made[k], outs[k], out_sems.at[k]))
        sent[-1].start()
    for copy in sent:
        copy.wait()


def project_columns(place, attended, chunks, low=None, mebibytes=56):
    more = [] if low is None else [low]
    rows = attended.shape[0] + (0 if low is None else low.shape[0])
    depth = chunks[0][0].shape[1]
    width = WIDE * len(chunks)
    return pl.pallas_call(
        functools.partial(columns_kernel, len(chunks)),
        in_specs=[in_smem()]
        + [pl.BlockSpec(memory_space=pl.ANY)] * (1 + 4 * len(chunks))
        + [in_vmem()] * len(more),
        out_specs=[pl.BlockSpec(memory_space=pl.ANY)] * BLOCKS,
        out_shape=[jax.ShapeDtypeStruct((rows, width), jnp.bfloat16)] * BLOCKS,
        scratch_shapes=[pltpu.VMEM((rows, width), jnp.bfloat16)] * BLOCKS
        + [
            pltpu.VMEM(attended.shape, jnp.bfloat16),
            pltpu.VMEM((len(chunks), 2, BLOCKS, depth, HEAD_SIZE), jnp.bfloat16),
            pltpu.SemaphoreType.DMA((len(chunks) + 1, BLOCKS, 2)),
            pltpu.SemaphoreType.DMA((BLOCKS,)),
        ],
        compiler_params=kernel_params(mebibytes),
        cost_estimate=cost(
            2 * rows * depth * BLOCKS * width,
            2 * (rows * depth + depth * BLOCKS * width + rows * BLOCKS * width),
        ),
        name="project_columns",
    )(place, attended, *[w for chunk in chunks for w in chunk], *more)


def sum_kernel(place, table, chosen_own, chosen_back, *refs):
    parts, (out, up) = refs[:12], refs[12:]
    rank, rows = ADAPTER_RANK, out.shape[0]

    @pl.when(place[6] == 1)
    def _():
        up[...] = chosen_back[:, rank:, :].reshape(up.shape)

    @pl.when(place[6] == 0)
    def _():
        up[...] = chosen_own[:, rank:, :].reshape(up.shape)

    low = sum(v[rows:, :rows].astype(jnp.float32) for v in parts[:4])
    low = low.astype(jnp.bfloat16).astype(jnp.float32)
    owner = request_of_rows(table, (1, rows), 1)
    wide = jnp.concatenate([jnp.where(owner == j, low, 0.0) for j in range(4)], axis=0)
    spread = wide.T.astype(jnp.bfloat16)
    core = place[0]
    for i in range(PLANES):
        first, at = (0, i * WIDE) if i < 2 else (4 * (i - 1), 0)
        total = sum(v[:rows, at : at + WIDE].astype(jnp.float32) for v in parts[first : first + 4])
        for c, mine in ((core, total[:, :HEAD_SIZE]), (1 - core, total[:, HEAD_SIZE:])):
            begin = pl.multiple_of((2 * place[7 + i] + c) * HEAD_SIZE, HEAD_SIZE)
            columns = pl.ds(begin, HEAD_SIZE)
            out[:, columns] = (
                mine + jnp.dot(spread, up[:, columns], preferred_element_type=jnp.float32)
            ).astype(jnp.bfloat16)


def sum_columns(place, table, chosen_own, chosen_back, parts):
    rows = parts[-1].shape[0]
    width = chosen_own.shape[2]
    return pl.pallas_call(
        sum_kernel,
        in_specs=[in_smem()] * 2 + [in_vmem()] * 14,
        out_specs=in_vmem(),
        out_shape=jax.ShapeDtypeStruct((rows, width), jnp.bfloat16),
        scratch_shapes=[pltpu.VMEM((4 * ADAPTER_RANK, width), jnp.bfloat16)],
        compiler_params=kernel_params(56),
        cost_estimate=cost(2 * rows * width * (8 + 4 * ADAPTER_RANK), 12 * rows * width, 0),
        name="sum_columns",
    )(place, table, chosen_own, chosen_back, *parts)


def shards_by_plane(
    hidden_input,
    input_norm_gain,
    query_norm_gain,
    key_norm_gain,
    query_weight,
    key_value_weight,
    output_weight,
    adapter_down_qkv,
    adapter_down_output,
    adapter_up_query,
    adapter_up_key_value,
    adapter_up_output,
    pool,
    lengths,
    cached_prefix_pages,
    prefix_page_table,
    adapter_of_request,
    adapter_storage,
):
    request_index = lax.axis_index("req")
    plane, core = request_index // 2, request_index % 2
    block = lax.axis_index("mlp")
    at_end = (plane == 0) | (plane == PLANES - 1)
    near = plane ^ 1
    inner = [core, block, plane, near, 3 - plane, 3 - near]
    other = jnp.where(at_end, jnp.where(plane == 0, 2, 1), 3 - plane)
    place = jnp.stack(
        inner + [at_end.astype(jnp.int32)]
        + [plane, near, other, 6 - plane - near - other]
        + [sum(i * (p == block ^ k).astype(jnp.int32) for i, p in enumerate(inner[2:])) for k in range(BLOCKS)]
    ).astype(jnp.int32)
    row_count, block_width = hidden_input.shape
    key_value_width = KEY_VALUE_HEADS // BLOCKS * HEAD_SIZE
    key_value_begin = block * key_value_width

    half_rows = row_count // 2
    table = jnp.concatenate([lengths[0], adapter_of_request[0, :, 0]])
    q_2 = along(query_weight, MIDDLE)
    end_hidden = along(hidden_input, INWARD)
    own_1, own_2 = swap_blocks(hidden_input, 1), swap_blocks(hidden_input, 2)
    kv_0 = lax.dynamic_slice_in_dim(key_value_weight, key_value_begin, key_value_width, 2)
    up_kv = lax.dynamic_slice_in_dim(adapter_up_key_value, key_value_begin, key_value_width, 3)
    rest_0 = pack_rows(
        table,
        kv_0.reshape(-1, 2 * key_value_width),
        adapter_down_qkv,
        adapter_up_query,
        up_kv.reshape(up_kv.shape[0], ADAPTER_RANK, 2 * key_value_width),
        adapter_down_output,
        adapter_up_output,
    )
    _, _, token_positions, _ = row_tables(
        lengths[0], cached_prefix_pages[0], prefix_page_table[0], row_count
    )
    half_width = HEAD_SIZE // 2
    inverse_freq = jnp.exp(
        jnp.arange(half_width, dtype=jnp.float32) * (-2.0 / HEAD_SIZE) * math.log(rope_base)
    )
    angles = token_positions.astype(jnp.float32)[:, None] * inverse_freq[None, :]
    cosine, sine = jnp.cos(angles), jnp.sin(angles)
    cosine = jnp.concatenate([cosine, cosine], axis=1)
    sine = jnp.concatenate([-sine, sine], axis=1)
    cached = lax.dynamic_slice_in_dim(pool, key_value_begin, key_value_width, 2)
    k_pool, v_pool = cached[:, 0], cached[:, 1]
    wo_0 = jnp.transpose(output_weight, (1, 0, 2))

    to_1 = jnp.concatenate([end_hidden, own_2[half_rows:]], axis=0)
    to_2 = jnp.concatenate([end_hidden, own_1[:half_rows]], axis=0)
    rest_0, to_1, to_2, q_2, query_later, cosine, sine, k_pool, v_pool, wo_0 = gate(
        [rest_0, to_1, to_2, q_2, query_weight, cosine, sine, k_pool, v_pool, wo_0], []
    )
    rest_1 = along(rest_0, INWARD)
    rest_2 = along(rest_0, MIDDLE)
    from_1, from_2 = swap_blocks(to_1, 1), swap_blocks(to_2, 2)
    q_0x, q_2x, rest_0x = (along(v, CORES) for v in (query_later, q_2, rest_0))

    rest_1, rest_2, from_1, from_2, query_later = gate(
        [rest_1, rest_2, from_1, from_2, query_later], [q_0x, q_2x, rest_0x]
    )
    half_1, half_2 = from_1[:half_rows], from_2[half_rows:row_count]
    end_table = rest_1[7 * ADAPTER_RANK, :8].astype(jnp.int32)
    q_1 = along(query_later, INWARD)
    rest_3 = along(rest_1, MIDDLE)
    end_3, end_4 = swap_blocks(half_1, 2), swap_blocks(half_2, 1)

    gain = input_norm_gain.astype(jnp.float32).reshape(BLOCKS, block_width)
    own_pieces = [(hidden_input, 0), (own_1, 0), (own_2, 0), (from_2, 4), (from_1, 4)]
    end_pieces = [(end_hidden, 0), (from_1, 0), (from_2, 0), (end_3, 0), (end_4, 0)]
    x, own_done = norm_rows(place, gain, own_pieces, 0, None)
    x, end_done = norm_rows(place, gain, end_pieces, 1, x)
    q_1, rest_1, rest_2, rest_3, wo_0 = gate([q_1, rest_1, rest_2, rest_3, wo_0], [end_done])
    q_3 = along(q_1, MIDDLE)
    wo_1 = along(wo_0, NEAR)
    rest_1x, rest_2x, rest_3x = (along(v, CORES) for v in (rest_1, rest_2, rest_3))
    q_1x = along(q_1, CORES)

    packed = [rest_0, rest_1, rest_2, rest_3, rest_0x, rest_1x, rest_2x, rest_3x]
    low, chosen_own, chosen_end, up, up_kv = rank_terms(
        place, table, end_table, adapter_storage, x, packed, 2 * key_value_width
    )
    lows = [low] + to_blocks([low] * BLOCKS)
    chosen_back = along(chosen_end, OUTWARD)

    kv_own, kv_end = project(
        place,
        table,
        end_table,
        adapter_storage,
        x,
        [v for pair in zip(packed[:4], packed[4:]) for v in pair],
        lows,
        up_kv,
        False,
    )
    kv_back = along(kv_end, OUTWARD)
    q_3, wo_0, wo_1 = gate([q_3, wo_0, wo_1], [kv_own])
    q_3x = along(q_3, CORES)
    wo_mid1, wo_mid2 = along(wo_0, MIDDLE), along(wo_1, MIDDLE)
    raw_own, raw_end = project(
        place,
        table,
        end_table,
        adapter_storage,
        x,
        [query_weight, q_0x, q_1, q_1x, q_2, q_2x, q_3, q_3x],
        lows,
        up,
        True,
    )
    raw_end, kv_back, chosen_back = gate([raw_end, kv_back, chosen_back], [])
    raw_back = along(raw_end, OUTWARD)
    wo_0x, wo_1x = along(wo_0, CORES), along(wo_1, CORES)
    wo_mid1, raw_back = gate([wo_mid1, raw_back], [wo_0x, wo_1x])
    wo_out2 = along(wo_mid1, OUTWARD)

    attended, cache, low_out = attend(
        place,
        table,
        cached_prefix_pages[0],
        prefix_page_table[0].reshape(-1),
        raw_own,
        raw_back,
        kv_own,
        kv_back,
        k_pool,
        v_pool,
        query_norm_gain.astype(jnp.float32)[None, :],
        key_norm_gain.astype(jnp.float32)[None, :],
        cosine,
        sine,
        chosen_own,
        chosen_back,
    )
    new_cache = cache.reshape(row_count, 2, key_value_width)

    attended, wo_mid2 = gate([attended, wo_mid2], [])
    wo_out3 = along(wo_mid2, OUTWARD)
    near_parts = project_columns(
        place, attended, [(wo_0, wo_0x, wo_0, wo_0x), (wo_1, wo_1x, wo_1, wo_1x)], low_out
    )
    parts = [near_parts[0]] + to_blocks(near_parts)
    (wo_out2,) = gate([wo_out2], near_parts[:1])
    mid_parts = project_columns(
        place, attended, [(wo_out2, along(wo_out2, CORES), wo_mid1, along(wo_mid1, CORES))]
    )
    parts += [mid_parts[0]] + to_blocks(mid_parts)
    (wo_out3,) = gate([wo_out3], parts[:5], 1)
    last_parts = project_columns(
        place,
        attended,
        [(wo_out3, along(wo_out3, CORES), wo_mid2, along(wo_mid2, CORES))],
        mebibytes=12,
    )
    parts += [last_parts[0]] + to_blocks(last_parts)
    attention_update = sum_columns(place, table, chosen_own, chosen_back, parts)
    return (attention_update, new_cache)


def solution(mesh):
    return jax.shard_map(
        shards_by_plane if planes_fit(mesh) else shards,
        mesh=mesh,
        in_specs=(
            P("req", "mlp"),
            P(),
            P(),
            P(),
            P("req", "mlp"),
            P("req", None, None),
            P("mlp", None, "req"),
            P("req", None, "mlp"),
            P("req", None, "mlp"),
            P("req", None, "mlp"),
            P("req", None, None, None),
            P("req", None, "mlp"),
            P("req", None, None),
            P("req", None),
            P("req", None),
            P("req", None, None),
            P("req", None, None),
            P(),
        ),
        out_specs=(P("req", "mlp"), P("req", None, "mlp")),
        check_vma=False,
    )
```

```python
import functools
import math

import jax
import jax.numpy as jnp
from jax import lax
from jax.experimental import pallas as pl
from jax.experimental.pallas import tpu as pltpu
from jax.sharding import PartitionSpec as P

QUERY_HEADS = 32
KEY_VALUE_HEADS = 8
HEAD_SIZE = 128
ADAPTER_RANK = 16
PAGE = 64


epsilon = 1e-06
rope_base = 1000000.0


def root_mean_scale(values, gain_vec):
    mean_sq = jnp.mean(values * values, axis=-1, keepdims=True)
    return values * lax.rsqrt(mean_sq + epsilon) * gain_vec.astype(jnp.float32)


def rotary_embed(values, token_positions):
    half_width = values.shape[-1] // 2
    inverse_freq = jnp.exp(
        jnp.arange(half_width, dtype=jnp.float32) * (-2.0 / values.shape[-1]) * math.log(rope_base)
    )
    angles = token_positions.astype(jnp.float32)[:, None] * inverse_freq[None, :]
    cosine = jnp.cos(angles)[:, None, :]
    sine_part = jnp.sin(angles)[:, None, :]
    front = values[..., :half_width]
    back = values[..., half_width:]
    return jnp.concatenate(
        [front * cosine - back * sine_part, back * cosine + front * sine_part], axis=-1
    )


def row_tables(lengths_row, prefix_row, page_rows, row_count):
    ends_at = jnp.cumsum(lengths_row)
    starts_at = ends_at - lengths_row
    row_ids = jnp.arange(row_count, dtype=jnp.int32)
    owners = jnp.sum((row_ids[:, None] >= ends_at[None, :]).astype(jnp.int32), axis=1)
    group_members = owners[:, None] == jnp.arange(lengths_row.shape[0], dtype=jnp.int32)[None, :]
    offsets = PAGE * prefix_row[None, :] + row_ids[:, None] - starts_at[None, :]
    token_positions = jnp.sum(jnp.where(group_members, offsets, 0), axis=1)
    page_ids = jnp.arange(page_rows.shape[1], dtype=jnp.int32)
    listed = (page_rows[:, :, None] == page_ids[None, None, :]) & (
        page_ids[None, :, None] < prefix_row[:, None, None]
    )
    page_used = jnp.sum(listed.astype(jnp.float32), axis=1)
    return (owners, group_members, token_positions, page_used)


def apply_adapter(lowrank_inner, group_members, chosen_up):
    masked = lowrank_inner[:, None, :] * group_members.astype(lowrank_inner.dtype)[:, :, None]
    return jnp.einsum("gjr,jrc->gc", masked, chosen_up, preferred_element_type=jnp.float32)


def select_rows(terms, group_members):
    return jnp.sum(terms * group_members.astype(jnp.float32)[:, :, None], axis=1)


def shards(
    hidden_input,
    input_norm_gain,
    query_norm_gain,
    key_norm_gain,
    query_weight,
    key_value_weight,
    output_weight,
    adapter_down_qkv,
    adapter_down_output,
    adapter_up_query,
    adapter_up_key_value,
    adapter_up_output,
    pool,
    lengths,
    cached_prefix_pages,
    prefix_page_table,
    adapter_of_request,
    adapter_storage,
):
    feature_group_count = lax.axis_size("mlp")
    feature_group_index = lax.axis_index("mlp")
    whole = lax.all_gather(hidden_input, "mlp", axis=1, tiled=True)
    row_count, full_width = whole.shape
    normalized_input = root_mean_scale(whole.astype(jnp.float32), input_norm_gain).astype(
        jnp.bfloat16
    )
    owners, group_members, token_positions, page_used = row_tables(
        lengths[0], cached_prefix_pages[0], prefix_page_table[0], row_count
    )
    q_width = query_weight.shape[1]
    query_head_rows = q_width // HEAD_SIZE
    key_value_local = max(1, KEY_VALUE_HEADS // feature_group_count)
    key_value_width = key_value_local * HEAD_SIZE
    key_value_begin = (
        feature_group_index * query_head_rows // (QUERY_HEADS // KEY_VALUE_HEADS) * HEAD_SIZE
    )
    own_wkv = lax.dynamic_slice_in_dim(key_value_weight, key_value_begin, key_value_width, 2)
    request_key_value_up = lax.dynamic_slice_in_dim(
        adapter_up_key_value, key_value_begin, key_value_width, 3
    )
    gathered = (
        lax.all_gather(adapter_down_qkv, "req", axis=0, tiled=True),
        lax.all_gather(adapter_down_output, "req", axis=0, tiled=True),
        lax.all_gather(adapter_up_query, "req", axis=0, tiled=True),
        lax.all_gather(request_key_value_up, "req", axis=0, tiled=True),
        lax.all_gather(adapter_up_output, "req", axis=0, tiled=True),
    )
    slot_indices = jnp.take(adapter_storage, adapter_of_request[0, :, 0], axis=0)
    chosen_down = jnp.take(gathered[0], slot_indices, axis=0)
    output_down = jnp.take(gathered[1], slot_indices, axis=0)
    query_up_part = jnp.take(gathered[2], slot_indices, axis=0)
    key_value_up = jnp.take(gathered[3], slot_indices, axis=0)
    output_up = jnp.take(gathered[4], slot_indices, axis=0)
    feature_cols = full_width // feature_group_count
    own_normed = lax.dynamic_slice_in_dim(
        normalized_input, feature_group_index * feature_cols, feature_cols, 1
    )
    low_terms = jnp.einsum(
        "gd,jkd->gjk", own_normed, chosen_down, preferred_element_type=jnp.float32
    )
    lowrank_inner = lax.psum(select_rows(low_terms, group_members).astype(jnp.bfloat16), "mlp")
    q_part = lax.all_gather(query_weight, "req", axis=0, tiled=True)
    kv_part = lax.all_gather(own_wkv, "req", axis=0, tiled=True)
    query_width_total = jnp.dot(normalized_input, q_part, preferred_element_type=jnp.float32)
    kv_total = jnp.dot(
        normalized_input,
        kv_part.reshape(kv_part.shape[0], 2 * key_value_width),
        preferred_element_type=jnp.float32,
    )
    query_width_total, kv_total = (query_width_total, kv_total)
    query_plain = (
        query_width_total
        + apply_adapter(lowrank_inner[:, 0:ADAPTER_RANK], group_members, query_up_part)
    ).astype(jnp.bfloat16)
    key_lowrank_part = apply_adapter(
        lowrank_inner[:, ADAPTER_RANK : 2 * ADAPTER_RANK], group_members, key_value_up[:, :, 0]
    )
    value_lowrank_part = apply_adapter(
        lowrank_inner[:, 2 * ADAPTER_RANK : 3 * ADAPTER_RANK], group_members, key_value_up[:, :, 1]
    )
    key_value_plain = (
        kv_total.reshape(row_count, 2, key_value_width)
        + jnp.stack([key_lowrank_part, value_lowrank_part], axis=1)
    ).astype(jnp.bfloat16)
    cached = lax.dynamic_slice_in_dim(pool, key_value_begin, key_value_width, 2)
    pool_token_rows = cached.shape[0]
    query_rotated = rotary_embed(
        root_mean_scale(
            query_plain.astype(jnp.float32).reshape(row_count, query_head_rows, HEAD_SIZE),
            query_norm_gain,
        ),
        token_positions,
    ).astype(jnp.bfloat16)
    key_rotated = rotary_embed(
        root_mean_scale(
            key_value_plain[:, 0]
            .astype(jnp.float32)
            .reshape(row_count, key_value_local, HEAD_SIZE),
            key_norm_gain,
        ),
        token_positions,
    ).astype(jnp.bfloat16)
    cache_columns = KEY_VALUE_HEADS * HEAD_SIZE // feature_group_count
    own_offset = feature_group_index * cache_columns - key_value_begin
    local_cache = jnp.stack(
        [key_rotated.reshape(row_count, key_value_width), key_value_plain[:, 1]], axis=1
    )
    new_cache = lax.dynamic_slice_in_dim(local_cache, own_offset, cache_columns, 2)
    key_matrix = jnp.concatenate(
        [cached[:, 0].reshape(pool_token_rows, key_value_local, HEAD_SIZE), key_rotated], axis=0
    )
    value_matrix = jnp.concatenate(
        [
            cached[:, 1].reshape(pool_token_rows, key_value_local, HEAD_SIZE),
            key_value_plain[:, 1].reshape(row_count, key_value_local, HEAD_SIZE),
        ],
        axis=0,
    )
    pool_ok = jnp.dot(group_members.astype(jnp.float32), page_used, precision=lax.Precision.HIGHEST)
    pool_ok = jnp.repeat(pool_ok, PAGE, axis=1) > 0.5
    row_ids = jnp.arange(row_count, dtype=jnp.int32)
    causal = (owners[:, None] == owners[None, :]) & (row_ids[None, :] <= row_ids[:, None])
    allowed = jnp.concatenate([pool_ok, causal], axis=1)
    query_rows = query_rotated.reshape(
        row_count, key_value_local, query_head_rows // key_value_local, HEAD_SIZE
    )
    scores = jnp.einsum(
        "gkhd,skd->khgs", query_rows, key_matrix, preferred_element_type=jnp.float32
    ) / math.sqrt(HEAD_SIZE)
    exp_scores = jnp.where(allowed[None, None], jnp.exp(scores), 0.0)
    softmax = (exp_scores / jnp.sum(exp_scores, axis=-1, keepdims=True)).astype(jnp.bfloat16)
    attended = jnp.einsum(
        "khgs,skd->gkhd", softmax, value_matrix, preferred_element_type=jnp.float32
    )
    attended = attended.astype(jnp.bfloat16).reshape(row_count, q_width)
    out_terms = jnp.einsum("gc,jrc->gjr", attended, output_down, preferred_element_type=jnp.float32)
    lowrank_result = lax.psum(select_rows(out_terms, group_members), "mlp").astype(jnp.bfloat16)
    partial_value = jnp.einsum(
        "gc,cnk->gnk",
        attended,
        lax.all_gather(output_weight, "req", axis=2, tiled=True),
        preferred_element_type=jnp.float32,
    )
    summed_output = lax.psum_scatter(
        partial_value.reshape(row_count, full_width).astype(jnp.bfloat16),
        "mlp",
        scatter_dimension=1,
        tiled=True,
    ).astype(jnp.float32)
    attention_update = (
        summed_output + apply_adapter(lowrank_result, group_members, output_up)
    ).astype(jnp.bfloat16)
    return (attention_update, new_cache)


PLANES = 4
BLOCKS = 4
GROUPS = 2
HIDDEN = -1e30
WIDE = 256


def planes_fit(mesh):
    return mesh.shape["req"] == 2 * PLANES and mesh.shape["mlp"] == BLOCKS


def plane_pairs(pairs):
    return [(2 * a + core, 2 * b + core) for a, b in pairs for core in range(2)]


INWARD = plane_pairs([(0, 1), (3, 2)])
MIDDLE = plane_pairs([(1, 2), (2, 1)])
OUTWARD = plane_pairs([(1, 0), (2, 3)])
NEAR = plane_pairs([(0, 1), (1, 0), (2, 3), (3, 2)])
CORES = [(r, r ^ 1) for r in range(2 * PLANES)]


def along(value, pairs):
    return lax.ppermute(value, "req", pairs)


def swap_blocks(value, k):
    return lax.ppermute(value, "mlp", [(b, b ^ k) for b in range(BLOCKS)])


def to_blocks(pieces):
    return [
        lax.ppermute(piece, "mlp", [(b, b ^ k) for b in range(BLOCKS)])
        for k, piece in enumerate(pieces)
        if k > 0
    ]


def gate_kernel(*refs):
    del refs


def gate(values, earlier, mebibytes=60):
    return pl.pallas_call(
        gate_kernel,
        in_specs=[pl.BlockSpec(memory_space=pl.ANY)] * (len(values) + len(earlier)),
        out_specs=[pl.BlockSpec(memory_space=pl.ANY)] * len(values),
        out_shape=[jax.ShapeDtypeStruct(v.shape, v.dtype) for v in values],
        input_output_aliases={i: i for i in range(len(values))},
        compiler_params=kernel_params(mebibytes),
        name="gate",
    )(*values, *earlier)


def in_vmem():
    return pl.BlockSpec(memory_space=pltpu.VMEM)


def in_smem():
    return pl.BlockSpec(memory_space=pltpu.SMEM)


def cost(flops, bytes_accessed, transcendentals=0):
    return pl.CostEstimate(
        flops=flops, bytes_accessed=bytes_accessed, transcendentals=transcendentals
    )


def kernel_params(mebibytes):
    return pltpu.CompilerParams(vmem_limit_bytes=mebibytes * 1024 * 1024)


def request_of_rows(table, shape, axis):
    row = lax.broadcasted_iota(jnp.int32, shape, axis)
    end, owner = table[0], jnp.zeros(shape, jnp.int32)
    for j in range(1, 4):
        owner = jnp.where(row >= end, j, owner)
        end = end + table[j]
    return owner


def slots_of_rows(table, storage, row_count):
    owner = request_of_rows(table, (1, row_count), 1)
    slots = jnp.zeros((1, row_count), jnp.int32) + storage[table[4]]
    for j in range(1, 4):
        slots = jnp.where(owner == j, storage[table[4 + j]], slots)
    return slots


def slot_list(place):
    core = place[0]
    return [4 * place[2 + i] + 2 * c + s for c in (core, 1 - core) for i in range(4) for s in range(2)]


def dot(a, b):
    return jnp.dot(a, b, preferred_element_type=jnp.float32)


def core_columns(c, half):
    return pl.ds(pl.multiple_of(c * half, half), half)


def norm_kernel(place, gain, p0, p1, p2, p3, p4, *refs):
    out, done = refs[-2:]
    pieces = [p[...].astype(jnp.float32) for p in (p0, p1, p2)]
    late = pl.program_id(0) >= pl.num_programs(0) // 2
    pieces.append(jnp.where(late, p4[...], p3[...]).astype(jnp.float32))
    total = sum(jnp.sum(v * v, axis=1, keepdims=True) for v in pieces)
    half = pieces[0].shape[1] // 2
    scale = lax.rsqrt(total / (BLOCKS * 2 * half) + epsilon)
    core = place[0]
    for k, v in enumerate(pieces):
        normed = (v * scale * gain[pl.ds(place[1] ^ k, 1), :]).astype(jnp.bfloat16)
        first = 2 * place[11 + k]
        out[:, core_columns(first + core, half)] = normed[:, :half]
        out[:, core_columns(first + 1 - core, half)] = normed[:, half:]
    done[...] = jnp.zeros(done.shape, jnp.float32)


def norm_rows(place, gain, pieces, group, given):
    tiles, width = 4, gain.shape[1]
    rows = pieces[0][0].shape[0]
    tile = rows // tiles
    more = [] if given is None else [given]
    index = [lambda i: i] * 3
    index += [lambda i: jnp.minimum(i, tiles // 2 - 1), lambda i: jnp.maximum(i - tiles // 2, 0)]
    return pl.pallas_call(
        norm_kernel,
        grid_spec=pltpu.PrefetchScalarGridSpec(
            num_scalar_prefetch=1,
            grid=(tiles,),
            in_specs=[pl.BlockSpec((BLOCKS, width), lambda i, place: (0, 0))]
            + [
                pl.BlockSpec((tile, width), lambda i, place, f=f, at=at: (f + at(i), 0))
                for (_, f), at in zip(pieces, index)
            ]
            + [pl.BlockSpec(memory_space=pl.ANY)] * len(more),
            out_specs=[
                pl.BlockSpec((tile, BLOCKS * width), lambda i, place: (tiles * group + i, 0)),
                pl.BlockSpec((8, 128), lambda i, place: (0, 0)),
            ],
        ),
        out_shape=[
            jax.ShapeDtypeStruct((GROUPS * rows, BLOCKS * width), jnp.bfloat16),
            jax.ShapeDtypeStruct((8, 128), jnp.float32),
        ],
        input_output_aliases={7: 0} if more else {},
        compiler_params=kernel_params(56),
        cost_estimate=cost(16 * rows * width, 4 * BLOCKS * rows * width),
        name="norm_rows",
    )(place, gain, *[p for p, _ in pieces], *more)


SLOT_ROWS = 128


def pack_kernel(table, kv, down_qkv, up_query, up_kv, down_out, up_out, out):
    depth, kv_columns = kv.shape
    rank = ADAPTER_RANK
    out[2 * SLOT_ROWS :, :kv_columns] = kv[: depth // 2]
    out[2 * SLOT_ROWS :, kv_columns:] = kv[depth // 2 :]
    for s in range(2):
        first = s * SLOT_ROWS
        out[first : first + 3 * rank] = down_qkv[s]
        out[first + 3 * rank : first + 4 * rank] = up_query[s]
        out[first + 4 * rank : first + 5 * rank, :kv_columns] = up_kv[s]
        out[first + 4 * rank : first + 5 * rank, kv_columns:] = jnp.zeros(
            (rank, out.shape[1] - kv_columns), jnp.bfloat16
        )
        out[first + 5 * rank : first + 6 * rank] = down_out[s]
        out[first + 6 * rank : first + 7 * rank] = up_out[s]
    shape = (rank, out.shape[1])
    lane = lax.broadcasted_iota(jnp.int32, shape, 1)
    numbers = jnp.zeros(shape, jnp.float32)
    for i in range(8):
        numbers = jnp.where(lane == i, table[i].astype(jnp.float32), numbers)
    for s in range(2):
        out[s * SLOT_ROWS + 7 * rank : (s + 1) * SLOT_ROWS] = numbers.astype(jnp.bfloat16)


def pack_rows(table, kv, *adapters):
    width = adapters[0].shape[2]
    return pl.pallas_call(
        pack_kernel,
        in_specs=[in_smem()] + [in_vmem()] * 6,
        out_specs=in_vmem(),
        out_shape=jax.ShapeDtypeStruct((2 * SLOT_ROWS + kv.shape[0] // 2, width), jnp.bfloat16),
        compiler_params=kernel_params(56),
        cost_estimate=cost(0, 4 * width * (2 * SLOT_ROWS + kv.shape[0] // 2), 0),
        name="pack_rows",
    )(table, kv, *adapters)


def rank_kernel(place, own_table, end_table, storage, x, *refs):
    packed, (low, chosen_own, chosen_end, up, up_kv, down) = refs[:8], refs[8:]
    slots = slot_list(place)
    rank, rows, q_width = ADAPTER_RANK, x.shape[0] // GROUPS, x.shape[1]
    kv_columns, half, core = up_kv.shape[1], q_width // 2, place[0]
    for t, ref in enumerate(packed):
        for s in range(2):
            i, first = 2 * t + s, s * SLOT_ROWS
            for c, columns in ((core, slice(0, half)), (1 - core, slice(half, q_width))):
                down[3 * rank * i : 3 * rank * (i + 1), columns] = ref[
                    first : first + 3 * rank, core_columns(c, half)
                ]
            up[rank * i : rank * (i + 1), :] = ref[first + 3 * rank : first + 4 * rank, :]
            up_kv[rank * i : rank * (i + 1), :] = ref[
                first + 4 * rank : first + 5 * rank, :kv_columns
            ]
    for g, (table, chosen) in enumerate(((own_table, chosen_own), (end_table, chosen_end))):
        terms = lax.dot_general(
            down[...],
            x[g * rows : (g + 1) * rows, :],
            (((1,), (1,)), ((), ())),
            preferred_element_type=jnp.float32,
        )
        row_slots = slots_of_rows(table, storage, rows)
        total = jnp.zeros((3 * rank, rows), jnp.float32)
        for i, slot in enumerate(slots):
            total += jnp.where(row_slots == slot, terms[3 * rank * i : 3 * rank * (i + 1)], 0.0)
        low[:, g * rows : (g + 1) * rows] = total.astype(jnp.bfloat16)
        for j in range(4):
            wanted = storage[table[4 + j]]
            for i, slot in enumerate(slots):

                @pl.when(wanted == slot)
                def _(j=j, i=i, chosen=chosen):
                    first = (i % 2) * SLOT_ROWS
                    chosen[j] = packed[i // 2][first + 5 * rank : first + 7 * rank, :]


def rank_terms(place, own_table, end_table, storage, x, packed, kv_columns):
    rows, width = x.shape[0], x.shape[1] // BLOCKS
    chosen = jax.ShapeDtypeStruct((4, 2 * ADAPTER_RANK, width), jnp.bfloat16)
    up = jax.ShapeDtypeStruct((16 * ADAPTER_RANK, width), jnp.bfloat16)
    up_kv = jax.ShapeDtypeStruct((16 * ADAPTER_RANK, kv_columns), jnp.bfloat16)
    low = jax.ShapeDtypeStruct((3 * ADAPTER_RANK, rows), jnp.bfloat16)
    slots = pl.BlockSpec((2 * SLOT_ROWS, width), lambda i, place: (0, 0))
    whole = lambda shape: pl.BlockSpec(shape, lambda i, place: (0,) * len(shape))
    return pl.pallas_call(
        rank_kernel,
        grid_spec=pltpu.PrefetchScalarGridSpec(
            num_scalar_prefetch=1,
            grid=(1,),
            in_specs=[in_smem()] * 3
            + [pl.BlockSpec((rows, width), lambda i, place: (0, place[11]))]
            + [slots] * 8,
            out_specs=[whole(v.shape) for v in (low, chosen, chosen, up, up_kv)],
            scratch_shapes=[pltpu.VMEM((16 * 3 * ADAPTER_RANK, width), jnp.bfloat16)],
        ),
        out_shape=[low, chosen, chosen, up, up_kv],
        compiler_params=kernel_params(56),
        cost_estimate=cost(
            2 * 16 * 3 * ADAPTER_RANK * rows * width, 2 * width * (rows + 18 * SLOT_ROWS + 256)
        ),
        name="rank_terms",
    )(place, own_table, end_table, storage, x, *packed)


def spread_ranks(place, tables, storage, lows, part, spread):
    rank = ADAPTER_RANK
    rows = spread.shape[0] // GROUPS
    slots = slot_list(place)
    low = sum(v[part * rank : (part + 1) * rank].astype(jnp.float32) for v in lows)
    low = low.astype(jnp.bfloat16).astype(jnp.float32)
    for g, table in enumerate(tables):
        row_slots = slots_of_rows(table, storage, rows)
        mine = low[:, g * rows : (g + 1) * rows]
        wide = jnp.concatenate([jnp.where(row_slots == s, mine, 0.0) for s in slots], axis=0)
        spread[g * rows : (g + 1) * rows, :] = wide.T.astype(jnp.bfloat16)


def project_kernel(is_q, place, own_table, end_table, storage, x, *refs):
    sources, lows, up = refs[:8], refs[8:12], refs[12]
    own, end, spread, held, x_held, sems = refs[-6:]
    rows, width = own.shape[0], x.shape[1] // BLOCKS
    depth = held.shape[0] // 8

    def copies(chunk):
        block = slice(chunk * width, (chunk + 1) * width)
        first = 0 if is_q else 2 * SLOT_ROWS
        return [pltpu.make_async_copy(x.at[:, block], x_held.at[:, block], sems.at[chunk, 2])] + [
            pltpu.make_async_copy(
                sources[2 * chunk + c].at[first:, :],
                held.at[(2 * chunk + c) * depth : (2 * chunk + c + 1) * depth, :],
                sems.at[chunk, c],
            )
            for c in range(2)
        ]

    for chunk in range(BLOCKS):
        for copy in copies(chunk):
            copy.start()
    tables = (own_table, end_table)
    total = None
    if is_q:
        spread_ranks(place, tables, storage, lows, 0, spread)
        low = dot(spread[...], up[...])
    else:
        low = []
        for part in range(2):
            spread_ranks(place, tables, storage, lows, 1 + part, spread)
            low.append(dot(spread[...], up[:, part * WIDE : (part + 1) * WIDE]))
        low = jnp.concatenate(low, axis=1)
    for chunk in range(BLOCKS):
        for copy in copies(chunk):
            copy.wait()
        w = held[2 * chunk * depth : 2 * (chunk + 1) * depth, :]
        if not is_q:
            columns = own.shape[1]
            w = jnp.concatenate(
                [
                    w[c * depth : (c + 1) * depth, h * columns : (h + 1) * columns]
                    for c in range(2)
                    for h in range(2)
                ],
                axis=0,
            )
        term = dot(x_held[:, chunk * width : (chunk + 1) * width], w)
        total = low + term if total is None else total + term
    total = total.astype(jnp.bfloat16)
    own[...] = total[:rows]
    end[:rows] = total[rows:]
    if not is_q:
        chosen_end = refs[13]
        count, each, _ = chosen_end.shape
        for h in range(width // columns):
            for j in range(count):
                first = rows + (count * h + j) * each
                end[first : first + each] = chosen_end[j, :, h * columns : (h + 1) * columns]


def project(place, own_table, end_table, storage, x, sources, lows, up, is_q, chosen_end=None):
    rows, width = x.shape[0], x.shape[1] // BLOCKS
    columns = up.shape[1]
    more = [] if is_q else [chosen_end]
    extra = 0 if is_q else chosen_end.size // columns
    anywhere = pl.BlockSpec(memory_space=pl.ANY)
    return pl.pallas_call(
        functools.partial(project_kernel, is_q),
        in_specs=[in_smem()] * 4 + [anywhere] * 9 + [in_vmem()] * (5 + len(more)),
        out_specs=[in_vmem()] * 2,
        out_shape=[
            jax.ShapeDtypeStruct((rows // GROUPS, columns), jnp.bfloat16),
            jax.ShapeDtypeStruct((rows // GROUPS + extra, columns), jnp.bfloat16),
        ],
        scratch_shapes=[
            pltpu.VMEM((rows, 16 * ADAPTER_RANK), jnp.bfloat16),
            pltpu.VMEM(((8 if is_q else 4) * sources[0].shape[0], width), jnp.bfloat16),
            pltpu.VMEM(x.shape, jnp.bfloat16),
            pltpu.SemaphoreType.DMA((BLOCKS, 3)),
        ],
        compiler_params=kernel_params(56),
        cost_estimate=cost(
            2 * rows * (BLOCKS * width + 256) * columns,
            2 * BLOCKS * width * (rows + columns) + 2 * rows * columns,
        ),
        name="project_query" if is_q else "project_key_value",
    )(place, own_table, end_table, storage, x, *sources, *lows, up, *more)


def take_adapters(out, at_end, chosen_own, kv_back, rows, first):
    rank = ADAPTER_RANK
    count, each, width = chosen_own.shape
    columns = kv_back.shape[1]

    @pl.when(jnp.logical_not(at_end))
    def _():
        for j in range(count):
            out[rank * j : rank * (j + 1), :] = chosen_own[j, first : first + rank, :]

    @pl.when(at_end)
    def _():
        for h in range(width // columns):
            for j in range(count):
                start = rows + (count * h + j) * each + first
                out[rank * j : rank * (j + 1), h * columns : (h + 1) * columns] = kv_back[
                    start : start + rank, :
                ]


def attention_kernel(
    place, table, prefix, pages, own, back, kv_own, kv_back, k_pool, v_pool, q_gain, k_gain,
    cosine, sine, chosen_own, out, cache, low, raw, raw_kv, keys, values, allowed, down,
):
    rows, pool_rows = own.shape[0], k_pool.shape[0]
    page_count = pool_rows // PAGE

    @pl.when(place[6] == 1)
    def _():
        raw[...] = back[...]
        raw_kv[...] = kv_back[:rows]

    @pl.when(place[6] == 0)
    def _():
        raw[...] = own[...]
        raw_kv[...] = kv_own[...]

    take_adapters(down, place[6] == 1, chosen_own, kv_back, rows, 0)

    owner = request_of_rows(table, (rows, 1), 0)
    page = lax.broadcasted_iota(jnp.int32, (1, pool_rows), 1) // PAGE
    seen = jnp.zeros((rows, pool_rows), jnp.int32)
    for j in range(4):
        mine = jnp.zeros((1, pool_rows), jnp.int32)
        for i in range(page_count):
            mine = jnp.where((page == pages[8 * j + i]) & (i < prefix[j]), 1, mine)
        seen = jnp.where(owner == j, mine, seen)
    allowed[:, :pool_rows] = jnp.where(seen > 0, 0.0, HIDDEN)
    row = lax.broadcasted_iota(jnp.int32, (rows, rows), 0)
    column = lax.broadcasted_iota(jnp.int32, (rows, rows), 1)
    same = owner == request_of_rows(table, (1, rows), 1)
    allowed[:, pool_rows:] = jnp.where(same & (column <= row), 0.0, HIDDEN)

    def turned(value, gain):
        value = value.astype(jnp.float32)
        mean_sq = jnp.mean(value * value, axis=1, keepdims=True)
        value = value * lax.rsqrt(mean_sq + epsilon) * gain[...]
        other = pltpu.roll(value, HEAD_SIZE // 2, 1)
        return (value * cosine[...] + other * sine[...]).astype(jnp.bfloat16)

    kv_heads = k_pool.shape[1] // HEAD_SIZE
    q_width = out.shape[1]
    per_key = q_width // HEAD_SIZE // kv_heads
    kv_width = kv_heads * HEAD_SIZE
    cache[:, kv_width:] = raw_kv[:, kv_width:]
    for h in range(kv_heads):
        head = slice(h * HEAD_SIZE, (h + 1) * HEAD_SIZE)
        keys[:pool_rows] = k_pool[:, head]
        values[:pool_rows] = v_pool[:, head]
        k_new = turned(raw_kv[:, head], k_gain)
        keys[pool_rows:] = k_new
        cache[:, head] = k_new
        values[pool_rows:] = raw_kv[:, kv_width + h * HEAD_SIZE : kv_width + (h + 1) * HEAD_SIZE]
        for g in range(per_key):
            place_q = slice((h * per_key + g) * HEAD_SIZE, (h * per_key + g + 1) * HEAD_SIZE)
            query = turned(raw[:, place_q], q_gain)
            scores = lax.dot_general(
                query, keys[...], (((1,), (1,)), ((), ())), preferred_element_type=jnp.float32
            )
            grown = jnp.exp(scores * (1.0 / math.sqrt(HEAD_SIZE)) + allowed[...])
            weights = (grown * (1.0 / jnp.sum(grown, axis=1, keepdims=True))).astype(jnp.bfloat16)
            out[:, place_q] = jnp.dot(
                weights, values[...], preferred_element_type=jnp.float32
            ).astype(jnp.bfloat16)
    terms = lax.dot_general(
        down[...], out[...], (((1,), (1,)), ((), ())), preferred_element_type=jnp.float32
    )
    owner_lane = request_of_rows(table, (1, rows), 1)
    low[...] = sum(
        jnp.where(owner_lane == j, terms[j * ADAPTER_RANK : (j + 1) * ADAPTER_RANK], 0.0)
        for j in range(4)
    )


def attend(place, table, prefix, pages, own, back, kv_own, kv_back, k_pool, v_pool, q_gain, k_gain,
           cosine, sine, chosen_own):
    rows, q_width = own.shape
    kv_width = k_pool.shape[1]
    keys = k_pool.shape[0] + rows
    return pl.pallas_call(
        attention_kernel,
        in_specs=[in_smem()] * 4 + [in_vmem()] * 11,
        out_specs=[in_vmem()] * 3,
        out_shape=[
            jax.ShapeDtypeStruct((rows, q_width), jnp.bfloat16),
            jax.ShapeDtypeStruct((rows, 2 * kv_width), jnp.bfloat16),
            jax.ShapeDtypeStruct((ADAPTER_RANK, rows), jnp.float32),
        ],
        scratch_shapes=[
            pltpu.VMEM(own.shape, jnp.bfloat16),
            pltpu.VMEM(kv_own.shape, jnp.bfloat16),
            pltpu.VMEM((keys, HEAD_SIZE), jnp.bfloat16),
            pltpu.VMEM((keys, HEAD_SIZE), jnp.bfloat16),
            pltpu.VMEM((rows, keys), jnp.float32),
            pltpu.VMEM((4 * ADAPTER_RANK, chosen_own.shape[2]), jnp.bfloat16),
        ],
        compiler_params=kernel_params(56),
        cost_estimate=cost(4 * rows * keys * q_width, 6 * rows * q_width, rows * keys * (q_width // HEAD_SIZE)),
        name="attend",
    )(place, table, prefix, pages, own, back, kv_own, kv_back, k_pool, v_pool, q_gain, k_gain,
      cosine, sine, chosen_own)


def columns_kernel(count, place, attended, *refs):
    sources, rest = refs[: 4 * count], refs[4 * count :]
    low = rest[0] if len(rest) > 2 * BLOCKS + 4 else None
    outs, made, (rows_held, held, sems, out_sems) = rest[-2 * BLOCKS - 4 : -BLOCKS - 4], rest[-BLOCKS - 4 : -4], rest[-4:]
    rows = attended.shape[0]
    at_end = place[6] == 1

    def copies(chunk, end, k):
        pair = sources[4 * chunk + (0 if end else 2) :][:2]
        return [
            pltpu.make_async_copy(
                pair[c].at[place[1] ^ k], held.at[chunk, c, k], sems.at[chunk, k, c]
            )
            for c in range(2)
        ]

    given = pltpu.make_async_copy(attended, rows_held, sems.at[count, 0, 0])
    given.start()
    for end in (True, False):

        @pl.when(at_end if end else jnp.logical_not(at_end))
        def _(end=end):
            for k in (3, 2, 1, 0):
                for chunk in range(count):
                    for copy in copies(chunk, end, k):
                        copy.start()

    given.wait()
    sent = []
    for k in (3, 2, 1, 0):
        for chunk in range(count):
            for copy in copies(chunk, False, k):
                copy.wait()
        w = jnp.concatenate([held[chunk, c, k] for chunk in range(count) for c in range(2)], axis=1)
        made[k][:rows] = dot(rows_held[...], w).astype(jnp.bfloat16)
        if low is not None:
            made[k][rows:, :rows] = low[...].astype(jnp.bfloat16)
            made[k][rows:, rows:] = jnp.zeros(
                (low.shape[0], made[k].shape[1] - rows), jnp.bfloat16
            )
        sent.append(pltpu.make_async_copy(made[k], outs[k], out_sems.at[k]))
        sent[-1].start()
    for copy in sent:
        copy.wait()


def project_columns(place, attended, chunks, low=None, mebibytes=56):
    more = [] if low is None else [low]
    rows = attended.shape[0] + (0 if low is None else low.shape[0])
    depth = chunks[0][0].shape[1]
    width = WIDE * len(chunks)
    return pl.pallas_call(
        functools.partial(columns_kernel, len(chunks)),
        in_specs=[in_smem()]
        + [pl.BlockSpec(memory_space=pl.ANY)] * (1 + 4 * len(chunks))
        + [in_vmem()] * len(more),
        out_specs=[pl.BlockSpec(memory_space=pl.ANY)] * BLOCKS,
        out_shape=[jax.ShapeDtypeStruct((rows, width), jnp.bfloat16)] * BLOCKS,
        scratch_shapes=[pltpu.VMEM((rows, width), jnp.bfloat16)] * BLOCKS
        + [
            pltpu.VMEM(attended.shape, jnp.bfloat16),
            pltpu.VMEM((len(chunks), 2, BLOCKS, depth, HEAD_SIZE), jnp.bfloat16),
            pltpu.SemaphoreType.DMA((len(chunks) + 1, BLOCKS, 2)),
            pltpu.SemaphoreType.DMA((BLOCKS,)),
        ],
        compiler_params=kernel_params(mebibytes),
        cost_estimate=cost(
            2 * rows * depth * BLOCKS * width,
            2 * (rows * depth + depth * BLOCKS * width + rows * BLOCKS * width),
        ),
        name="project_columns",
    )(place, attended, *[w for chunk in chunks for w in chunk], *more)


def sum_kernel(place, table, chosen_own, kv_back, *refs):
    parts, (out, last, up) = refs[:8], refs[8:]
    rank, rows = ADAPTER_RANK, out.shape[0]
    take_adapters(up, place[6] == 1, chosen_own, kv_back, rows, rank)
    low = sum(v[rows:, :rows].astype(jnp.float32) for v in parts[:4])
    low = low.astype(jnp.bfloat16).astype(jnp.float32)
    owner = request_of_rows(table, (1, rows), 1)
    wide = jnp.concatenate([jnp.where(owner == j, low, 0.0) for j in range(4)], axis=0)
    spread = wide.T.astype(jnp.bfloat16)
    core = place[0]
    for i in range(PLANES):
        for h, c in enumerate((core, 1 - core)):
            begin = pl.multiple_of((2 * place[7 + i] + c) * HEAD_SIZE, HEAD_SIZE)
            total = dot(spread, up[:, pl.ds(begin, HEAD_SIZE)])
            if i == PLANES - 1:
                last[:, h * HEAD_SIZE : (h + 1) * HEAD_SIZE] = total
                out[:, pl.ds(begin, HEAD_SIZE)] = total.astype(jnp.bfloat16)
                continue
            first, at = (0, i * WIDE + h * HEAD_SIZE) if i < 2 else (4, h * HEAD_SIZE)
            for v in parts[first : first + 4]:
                total = total + v[:rows, at : at + HEAD_SIZE].astype(jnp.float32)
            out[:, pl.ds(begin, HEAD_SIZE)] = total.astype(jnp.bfloat16)


def sum_columns(place, table, chosen_own, kv_back, parts):
    rows = parts[-1].shape[0]
    width = chosen_own.shape[2]
    return pl.pallas_call(
        sum_kernel,
        in_specs=[in_smem()] * 2 + [in_vmem()] * 10,
        out_specs=[in_vmem()] * 2,
        out_shape=[
            jax.ShapeDtypeStruct((rows, width), jnp.bfloat16),
            jax.ShapeDtypeStruct((rows, WIDE), jnp.float32),
        ],
        scratch_shapes=[pltpu.VMEM((4 * ADAPTER_RANK, width), jnp.bfloat16)],
        compiler_params=kernel_params(56),
        cost_estimate=cost(2 * rows * width * (8 + 4 * ADAPTER_RANK), 12 * rows * width),
        name="sum_columns",
    )(place, table, chosen_own, kv_back, *parts)


def last_columns_kernel(place, given, p0, p1, p2, p3, whole, out):
    del place, whole
    total = given[...] + sum(v[...].astype(jnp.float32) for v in (p0, p1, p2, p3))
    out[...] = total.astype(jnp.bfloat16)


def last_columns(place, given, parts, whole):
    rows = given.shape[0]
    tile = pl.BlockSpec((rows, HEAD_SIZE), lambda i, place: (0, i))
    return pl.pallas_call(
        last_columns_kernel,
        grid_spec=pltpu.PrefetchScalarGridSpec(
            num_scalar_prefetch=1,
            grid=(2,),
            in_specs=[tile] * 5 + [pl.BlockSpec(memory_space=pl.ANY)],
            out_specs=pl.BlockSpec(
                (rows, HEAD_SIZE), lambda i, place: (0, 2 * place[10] + (place[0] ^ i))
            ),
        ),
        out_shape=jax.ShapeDtypeStruct(whole.shape, whole.dtype),
        input_output_aliases={6: 0},
        compiler_params=kernel_params(12),
        cost_estimate=cost(8 * rows * WIDE, 16 * rows * WIDE),
        name="last_columns",
    )(place, given, *parts, whole)


def shards_by_plane(
    hidden_input,
    input_norm_gain,
    query_norm_gain,
    key_norm_gain,
    query_weight,
    key_value_weight,
    output_weight,
    adapter_down_qkv,
    adapter_down_output,
    adapter_up_query,
    adapter_up_key_value,
    adapter_up_output,
    pool,
    lengths,
    cached_prefix_pages,
    prefix_page_table,
    adapter_of_request,
    adapter_storage,
):
    request_index = lax.axis_index("req")
    plane, core = request_index // 2, request_index % 2
    block = lax.axis_index("mlp")
    at_end = (plane == 0) | (plane == PLANES - 1)
    near = plane ^ 1
    inner = [core, block, plane, near, 3 - plane, 3 - near]
    other = jnp.where(at_end, jnp.where(plane == 0, 2, 1), 3 - plane)
    place = jnp.stack(
        inner + [at_end.astype(jnp.int32)]
        + [plane, near, other, 6 - plane - near - other]
        + [sum(i * (p == block ^ k).astype(jnp.int32) for i, p in enumerate(inner[2:])) for k in range(BLOCKS)]
    ).astype(jnp.int32)
    row_count, block_width = hidden_input.shape
    key_value_width = KEY_VALUE_HEADS // BLOCKS * HEAD_SIZE
    key_value_begin = block * key_value_width

    half_rows = row_count // 2
    table = jnp.concatenate([lengths[0], adapter_of_request[0, :, 0]])
    q_2 = along(query_weight, MIDDLE)
    end_hidden = along(hidden_input, INWARD)
    own_1, own_2 = swap_blocks(hidden_input, 1), swap_blocks(hidden_input, 2)
    kv_0 = lax.dynamic_slice_in_dim(key_value_weight, key_value_begin, key_value_width, 2)
    up_kv = lax.dynamic_slice_in_dim(adapter_up_key_value, key_value_begin, key_value_width, 3)
    rest_0 = pack_rows(
        table,
        kv_0.reshape(-1, 2 * key_value_width),
        adapter_down_qkv,
        adapter_up_query,
        up_kv.reshape(up_kv.shape[0], ADAPTER_RANK, 2 * key_value_width),
        adapter_down_output,
        adapter_up_output,
    )
    _, _, token_positions, _ = row_tables(
        lengths[0], cached_prefix_pages[0], prefix_page_table[0], row_count
    )
    half_width = HEAD_SIZE // 2
    inverse_freq = jnp.exp(
        jnp.arange(half_width, dtype=jnp.float32) * (-2.0 / HEAD_SIZE) * math.log(rope_base)
    )
    angles = token_positions.astype(jnp.float32)[:, None] * inverse_freq[None, :]
    cosine, sine = jnp.cos(angles), jnp.sin(angles)
    cosine = jnp.concatenate([cosine, cosine], axis=1)
    sine = jnp.concatenate([-sine, sine], axis=1)
    cached = lax.dynamic_slice_in_dim(pool, key_value_begin, key_value_width, 2)
    k_pool, v_pool = cached[:, 0], cached[:, 1]
    wo_0 = jnp.transpose(output_weight, (1, 0, 2))

    to_1 = jnp.concatenate([end_hidden, own_2[half_rows:]], axis=0)
    to_2 = jnp.concatenate([end_hidden, own_1[:half_rows]], axis=0)
    rest_0, to_1, to_2, q_2, query_later, cosine, sine, k_pool, v_pool, wo_0 = gate(
        [rest_0, to_1, to_2, q_2, query_weight, cosine, sine, k_pool, v_pool, wo_0], []
    )
    rest_1 = along(rest_0, INWARD)
    rest_2 = along(rest_0, MIDDLE)
    from_1, from_2 = swap_blocks(to_1, 1), swap_blocks(to_2, 2)
    q_0x, q_2x, rest_0x = (along(v, CORES) for v in (query_later, q_2, rest_0))

    rest_1, rest_2, from_1, from_2, query_later = gate(
        [rest_1, rest_2, from_1, from_2, query_later], [q_0x, q_2x, rest_0x]
    )
    half_1, half_2 = from_1[:half_rows], from_2[half_rows:row_count]
    end_table = rest_1[7 * ADAPTER_RANK, :8].astype(jnp.int32)
    q_1 = along(query_later, INWARD)
    rest_3 = along(rest_1, MIDDLE)
    end_3, end_4 = swap_blocks(half_1, 2), swap_blocks(half_2, 1)

    gain = input_norm_gain.astype(jnp.float32).reshape(BLOCKS, block_width)
    own_pieces = [(hidden_input, 0), (own_1, 0), (own_2, 0), (from_2, 4), (from_1, 4)]
    end_pieces = [(end_hidden, 0), (from_1, 0), (from_2, 0), (end_3, 0), (end_4, 0)]
    x, own_done = norm_rows(place, gain, own_pieces, 0, None)
    x, end_done = norm_rows(place, gain, end_pieces, 1, x)
    q_1, rest_1, rest_2, rest_3, wo_0 = gate([q_1, rest_1, rest_2, rest_3, wo_0], [end_done])
    q_3 = along(q_1, MIDDLE)
    wo_1 = along(wo_0, NEAR)
    rest_1x, rest_2x, rest_3x = (along(v, CORES) for v in (rest_1, rest_2, rest_3))
    q_1x = along(q_1, CORES)

    packed = [rest_0, rest_1, rest_2, rest_3, rest_0x, rest_1x, rest_2x, rest_3x]
    low, chosen_own, chosen_end, up, up_kv = rank_terms(
        place, table, end_table, adapter_storage, x, packed, 2 * key_value_width
    )
    lows = [low] + to_blocks([low] * BLOCKS)

    kv_own, kv_end = project(
        place,
        table,
        end_table,
        adapter_storage,
        x,
        [v for pair in zip(packed[:4], packed[4:]) for v in pair],
        lows,
        up_kv,
        False,
        chosen_end,
    )
    kv_back = along(kv_end, OUTWARD)
    q_3, wo_0, wo_1 = gate([q_3, wo_0, wo_1], [kv_own])
    q_3x = along(q_3, CORES)
    wo_mid1, wo_mid2 = along(wo_0, MIDDLE), along(wo_1, MIDDLE)
    raw_own, raw_end = project(
        place,
        table,
        end_table,
        adapter_storage,
        x,
        [query_weight, q_0x, q_1, q_1x, q_2, q_2x, q_3, q_3x],
        lows,
        up,
        True,
    )
    raw_end, kv_back = gate([raw_end, kv_back], [])
    raw_back = along(raw_end, OUTWARD)
    wo_0x, wo_1x = along(wo_0, CORES), along(wo_1, CORES)
    wo_mid1, raw_back = gate([wo_mid1, raw_back], [wo_0x, wo_1x])
    wo_out2 = along(wo_mid1, OUTWARD)

    attended, cache, low_out = attend(
        place,
        table,
        cached_prefix_pages[0],
        prefix_page_table[0].reshape(-1),
        raw_own,
        raw_back,
        kv_own,
        kv_back,
        k_pool,
        v_pool,
        query_norm_gain.astype(jnp.float32)[None, :],
        key_norm_gain.astype(jnp.float32)[None, :],
        cosine,
        sine,
        chosen_own,
    )
    new_cache = cache.reshape(row_count, 2, key_value_width)

    attended, wo_mid2 = gate([attended, wo_mid2], [])
    wo_out3 = along(wo_mid2, OUTWARD)
    near_parts = project_columns(
        place, attended, [(wo_0, wo_0x, wo_0, wo_0x), (wo_1, wo_1x, wo_1, wo_1x)], low_out
    )
    parts = [near_parts[0]] + to_blocks(near_parts)
    (wo_out2,) = gate([wo_out2], near_parts[:1])
    mid_parts = project_columns(
        place, attended, [(wo_out2, along(wo_out2, CORES), wo_mid1, along(wo_mid1, CORES))]
    )
    parts += [mid_parts[0]] + to_blocks(mid_parts)
    (wo_out3,) = gate([wo_out3], parts[:5], 1)
    last_parts = project_columns(
        place,
        attended,
        [(wo_out3, along(wo_out3, CORES), wo_mid2, along(wo_mid2, CORES))],
        mebibytes=12,
    )
    parts += [last_parts[0]] + to_blocks(last_parts)
    whole, given = sum_columns(place, table, chosen_own, kv_back, parts[:8])
    attention_update = last_columns(place, given, parts[8:], whole)
    return (attention_update, new_cache)


def solution(mesh):
    return jax.shard_map(
        shards_by_plane if planes_fit(mesh) else shards,
        mesh=mesh,
        in_specs=(
            P("req", "mlp"),
            P(),
            P(),
            P(),
            P("req", "mlp"),
            P("req", None, None),
            P("mlp", None, "req"),
            P("req", None, "mlp"),
            P("req", None, "mlp"),
            P("req", None, "mlp"),
            P("req", None, None, None),
            P("req", None, "mlp"),
            P("req", None, None),
            P("req", None),
            P("req", None),
            P("req", None, None),
            P("req", None, None),
            P(),
        ),
        out_specs=(P("req", "mlp"), P("req", None, "mlp")),
        check_vma=False,
    )
```

```python
import functools
import math

import jax
import jax.numpy as jnp
from jax import lax
from jax.experimental import pallas as pl
from jax.experimental.pallas import tpu as pltpu
from jax.sharding import PartitionSpec as P

QUERY_HEADS = 32
KEY_VALUE_HEADS = 8
HEAD_SIZE = 128
ADAPTER_RANK = 16
PAGE = 64


epsilon = 1e-06
rope_base = 1000000.0


def root_mean_scale(values, gain_vec):
    mean_sq = jnp.mean(values * values, axis=-1, keepdims=True)
    return values * lax.rsqrt(mean_sq + epsilon) * gain_vec.astype(jnp.float32)


def rotary_embed(values, token_positions):
    half_width = values.shape[-1] // 2
    inverse_freq = jnp.exp(
        jnp.arange(half_width, dtype=jnp.float32) * (-2.0 / values.shape[-1]) * math.log(rope_base)
    )
    angles = token_positions.astype(jnp.float32)[:, None] * inverse_freq[None, :]
    cosine = jnp.cos(angles)[:, None, :]
    sine_part = jnp.sin(angles)[:, None, :]
    front = values[..., :half_width]
    back = values[..., half_width:]
    return jnp.concatenate(
        [front * cosine - back * sine_part, back * cosine + front * sine_part], axis=-1
    )


def row_tables(lengths_row, prefix_row, page_rows, row_count):
    ends_at = jnp.cumsum(lengths_row)
    starts_at = ends_at - lengths_row
    row_ids = jnp.arange(row_count, dtype=jnp.int32)
    owners = jnp.sum((row_ids[:, None] >= ends_at[None, :]).astype(jnp.int32), axis=1)
    group_members = owners[:, None] == jnp.arange(lengths_row.shape[0], dtype=jnp.int32)[None, :]
    offsets = PAGE * prefix_row[None, :] + row_ids[:, None] - starts_at[None, :]
    token_positions = jnp.sum(jnp.where(group_members, offsets, 0), axis=1)
    page_ids = jnp.arange(page_rows.shape[1], dtype=jnp.int32)
    listed = (page_rows[:, :, None] == page_ids[None, None, :]) & (
        page_ids[None, :, None] < prefix_row[:, None, None]
    )
    page_used = jnp.sum(listed.astype(jnp.float32), axis=1)
    return (owners, group_members, token_positions, page_used)


def apply_adapter(lowrank_inner, group_members, chosen_up):
    masked = lowrank_inner[:, None, :] * group_members.astype(lowrank_inner.dtype)[:, :, None]
    return jnp.einsum("gjr,jrc->gc", masked, chosen_up, preferred_element_type=jnp.float32)


def select_rows(terms, group_members):
    return jnp.sum(terms * group_members.astype(jnp.float32)[:, :, None], axis=1)


def shards(
    hidden_input,
    input_norm_gain,
    query_norm_gain,
    key_norm_gain,
    query_weight,
    key_value_weight,
    output_weight,
    adapter_down_qkv,
    adapter_down_output,
    adapter_up_query,
    adapter_up_key_value,
    adapter_up_output,
    pool,
    lengths,
    cached_prefix_pages,
    prefix_page_table,
    adapter_of_request,
    adapter_storage,
):
    feature_group_count = lax.axis_size("mlp")
    feature_group_index = lax.axis_index("mlp")
    whole = lax.all_gather(hidden_input, "mlp", axis=1, tiled=True)
    row_count, full_width = whole.shape
    normalized_input = root_mean_scale(whole.astype(jnp.float32), input_norm_gain).astype(
        jnp.bfloat16
    )
    owners, group_members, token_positions, page_used = row_tables(
        lengths[0], cached_prefix_pages[0], prefix_page_table[0], row_count
    )
    q_width = query_weight.shape[1]
    query_head_rows = q_width // HEAD_SIZE
    key_value_local = max(1, KEY_VALUE_HEADS // feature_group_count)
    key_value_width = key_value_local * HEAD_SIZE
    key_value_begin = (
        feature_group_index * query_head_rows // (QUERY_HEADS // KEY_VALUE_HEADS) * HEAD_SIZE
    )
    own_wkv = lax.dynamic_slice_in_dim(key_value_weight, key_value_begin, key_value_width, 2)
    request_key_value_up = lax.dynamic_slice_in_dim(
        adapter_up_key_value, key_value_begin, key_value_width, 3
    )
    gathered = (
        lax.all_gather(adapter_down_qkv, "req", axis=0, tiled=True),
        lax.all_gather(adapter_down_output, "req", axis=0, tiled=True),
        lax.all_gather(adapter_up_query, "req", axis=0, tiled=True),
        lax.all_gather(request_key_value_up, "req", axis=0, tiled=True),
        lax.all_gather(adapter_up_output, "req", axis=0, tiled=True),
    )
    slot_indices = jnp.take(adapter_storage, adapter_of_request[0, :, 0], axis=0)
    chosen_down = jnp.take(gathered[0], slot_indices, axis=0)
    output_down = jnp.take(gathered[1], slot_indices, axis=0)
    query_up_part = jnp.take(gathered[2], slot_indices, axis=0)
    key_value_up = jnp.take(gathered[3], slot_indices, axis=0)
    output_up = jnp.take(gathered[4], slot_indices, axis=0)
    feature_cols = full_width // feature_group_count
    own_normed = lax.dynamic_slice_in_dim(
        normalized_input, feature_group_index * feature_cols, feature_cols, 1
    )
    low_terms = jnp.einsum(
        "gd,jkd->gjk", own_normed, chosen_down, preferred_element_type=jnp.float32
    )
    lowrank_inner = lax.psum(select_rows(low_terms, group_members).astype(jnp.bfloat16), "mlp")
    q_part = lax.all_gather(query_weight, "req", axis=0, tiled=True)
    kv_part = lax.all_gather(own_wkv, "req", axis=0, tiled=True)
    query_width_total = jnp.dot(normalized_input, q_part, preferred_element_type=jnp.float32)
    kv_total = jnp.dot(
        normalized_input,
        kv_part.reshape(kv_part.shape[0], 2 * key_value_width),
        preferred_element_type=jnp.float32,
    )
    query_width_total, kv_total = (query_width_total, kv_total)
    query_plain = (
        query_width_total
        + apply_adapter(lowrank_inner[:, 0:ADAPTER_RANK], group_members, query_up_part)
    ).astype(jnp.bfloat16)
    key_lowrank_part = apply_adapter(
        lowrank_inner[:, ADAPTER_RANK : 2 * ADAPTER_RANK], group_members, key_value_up[:, :, 0]
    )
    value_lowrank_part = apply_adapter(
        lowrank_inner[:, 2 * ADAPTER_RANK : 3 * ADAPTER_RANK], group_members, key_value_up[:, :, 1]
    )
    key_value_plain = (
        kv_total.reshape(row_count, 2, key_value_width)
        + jnp.stack([key_lowrank_part, value_lowrank_part], axis=1)
    ).astype(jnp.bfloat16)
    cached = lax.dynamic_slice_in_dim(pool, key_value_begin, key_value_width, 2)
    pool_token_rows = cached.shape[0]
    query_rotated = rotary_embed(
        root_mean_scale(
            query_plain.astype(jnp.float32).reshape(row_count, query_head_rows, HEAD_SIZE),
            query_norm_gain,
        ),
        token_positions,
    ).astype(jnp.bfloat16)
    key_rotated = rotary_embed(
        root_mean_scale(
            key_value_plain[:, 0]
            .astype(jnp.float32)
            .reshape(row_count, key_value_local, HEAD_SIZE),
            key_norm_gain,
        ),
        token_positions,
    ).astype(jnp.bfloat16)
    cache_columns = KEY_VALUE_HEADS * HEAD_SIZE // feature_group_count
    own_offset = feature_group_index * cache_columns - key_value_begin
    local_cache = jnp.stack(
        [key_rotated.reshape(row_count, key_value_width), key_value_plain[:, 1]], axis=1
    )
    new_cache = lax.dynamic_slice_in_dim(local_cache, own_offset, cache_columns, 2)
    key_matrix = jnp.concatenate(
        [cached[:, 0].reshape(pool_token_rows, key_value_local, HEAD_SIZE), key_rotated], axis=0
    )
    value_matrix = jnp.concatenate(
        [
            cached[:, 1].reshape(pool_token_rows, key_value_local, HEAD_SIZE),
            key_value_plain[:, 1].reshape(row_count, key_value_local, HEAD_SIZE),
        ],
        axis=0,
    )
    pool_ok = jnp.dot(group_members.astype(jnp.float32), page_used, precision=lax.Precision.HIGHEST)
    pool_ok = jnp.repeat(pool_ok, PAGE, axis=1) > 0.5
    row_ids = jnp.arange(row_count, dtype=jnp.int32)
    causal = (owners[:, None] == owners[None, :]) & (row_ids[None, :] <= row_ids[:, None])
    allowed = jnp.concatenate([pool_ok, causal], axis=1)
    query_rows = query_rotated.reshape(
        row_count, key_value_local, query_head_rows // key_value_local, HEAD_SIZE
    )
    scores = jnp.einsum(
        "gkhd,skd->khgs", query_rows, key_matrix, preferred_element_type=jnp.float32
    ) / math.sqrt(HEAD_SIZE)
    exp_scores = jnp.where(allowed[None, None], jnp.exp(scores), 0.0)
    softmax = (exp_scores / jnp.sum(exp_scores, axis=-1, keepdims=True)).astype(jnp.bfloat16)
    attended = jnp.einsum(
        "khgs,skd->gkhd", softmax, value_matrix, preferred_element_type=jnp.float32
    )
    attended = attended.astype(jnp.bfloat16).reshape(row_count, q_width)
    out_terms = jnp.einsum("gc,jrc->gjr", attended, output_down, preferred_element_type=jnp.float32)
    lowrank_result = lax.psum(select_rows(out_terms, group_members), "mlp").astype(jnp.bfloat16)
    partial_value = jnp.einsum(
        "gc,cnk->gnk",
        attended,
        lax.all_gather(output_weight, "req", axis=2, tiled=True),
        preferred_element_type=jnp.float32,
    )
    summed_output = lax.psum_scatter(
        partial_value.reshape(row_count, full_width).astype(jnp.bfloat16),
        "mlp",
        scatter_dimension=1,
        tiled=True,
    ).astype(jnp.float32)
    attention_update = (
        summed_output + apply_adapter(lowrank_result, group_members, output_up)
    ).astype(jnp.bfloat16)
    return (attention_update, new_cache)


PLANES = 4
BLOCKS = 4
GROUPS = 2
HIDDEN = -1e30
WIDE = 256


def planes_fit(mesh):
    return mesh.shape["req"] == 2 * PLANES and mesh.shape["mlp"] == BLOCKS


def plane_pairs(pairs):
    return [(2 * a + core, 2 * b + core) for a, b in pairs for core in range(2)]


INWARD = plane_pairs([(0, 1), (3, 2)])
MIDDLE = plane_pairs([(1, 2), (2, 1)])
OUTWARD = plane_pairs([(1, 0), (2, 3)])
NEAR = plane_pairs([(0, 1), (1, 0), (2, 3), (3, 2)])
CORES = [(r, r ^ 1) for r in range(2 * PLANES)]


def along(value, pairs):
    return lax.ppermute(value, "req", pairs)


def swap_blocks(value, k):
    return lax.ppermute(value, "mlp", [(b, b ^ k) for b in range(BLOCKS)])


def to_blocks(pieces):
    return [
        lax.ppermute(piece, "mlp", [(b, b ^ k) for b in range(BLOCKS)])
        for k, piece in enumerate(pieces)
        if k > 0
    ]


def gate_kernel(*refs):
    del refs


def gate(values, earlier, mebibytes=1):
    return pl.pallas_call(
        gate_kernel,
        in_specs=[pl.BlockSpec(memory_space=pl.ANY)] * (len(values) + len(earlier)),
        out_specs=[pl.BlockSpec(memory_space=pl.ANY)] * len(values),
        out_shape=[jax.ShapeDtypeStruct(v.shape, v.dtype) for v in values],
        input_output_aliases={i: i for i in range(len(values))},
        compiler_params=kernel_params(mebibytes),
        name="gate",
    )(*values, *earlier)


def in_vmem():
    return pl.BlockSpec(memory_space=pltpu.VMEM)


def in_smem():
    return pl.BlockSpec(memory_space=pltpu.SMEM)


def cost(flops, bytes_accessed, transcendentals=0):
    return pl.CostEstimate(
        flops=flops, bytes_accessed=bytes_accessed, transcendentals=transcendentals
    )


def kernel_params(mebibytes):
    return pltpu.CompilerParams(vmem_limit_bytes=mebibytes * 1024 * 1024)


def request_of_rows(table, shape, axis):
    row = lax.broadcasted_iota(jnp.int32, shape, axis)
    end, owner = table[0], jnp.zeros(shape, jnp.int32)
    for j in range(1, 4):
        owner = jnp.where(row >= end, j, owner)
        end = end + table[j]
    return owner


def slots_of_rows(table, storage, row_count):
    owner = request_of_rows(table, (1, row_count), 1)
    slots = jnp.zeros((1, row_count), jnp.int32) + storage[table[4]]
    for j in range(1, 4):
        slots = jnp.where(owner == j, storage[table[4 + j]], slots)
    return slots


def slot_list(place):
    core = place[0]
    return [4 * place[2 + i] + 2 * c + s for c in (core, 1 - core) for i in range(4) for s in range(2)]


def dot(a, b):
    return jnp.dot(a, b, preferred_element_type=jnp.float32)


def core_columns(c, half):
    return pl.ds(pl.multiple_of(c * half, half), half)


def norm_kernel(place, gain, p0, p1, p2, p3, p4, *refs):
    out, done = refs[-2:]
    pieces = [p[...].astype(jnp.float32) for p in (p0, p1, p2)]
    late = pl.program_id(0) >= pl.num_programs(0) // 2
    pieces.append(jnp.where(late, p4[...], p3[...]).astype(jnp.float32))
    total = sum(jnp.sum(v * v, axis=1, keepdims=True) for v in pieces)
    half = pieces[0].shape[1] // 2
    scale = lax.rsqrt(total / (BLOCKS * 2 * half) + epsilon)
    core = place[0]
    for k, v in enumerate(pieces):
        normed = (v * scale * gain[pl.ds(place[1] ^ k, 1), :]).astype(jnp.bfloat16)
        first = 2 * place[11 + k]
        out[:, core_columns(first + core, half)] = normed[:, :half]
        out[:, core_columns(first + 1 - core, half)] = normed[:, half:]
    done[...] = jnp.zeros(done.shape, jnp.float32)


def norm_rows(place, gain, pieces, group, given):
    tiles, width = 4, gain.shape[1]
    rows = pieces[0][0].shape[0]
    tile = rows // tiles
    more = [] if given is None else [given]
    index = [lambda i: i] * 3
    index += [lambda i: jnp.minimum(i, tiles // 2 - 1), lambda i: jnp.maximum(i - tiles // 2, 0)]
    return pl.pallas_call(
        norm_kernel,
        grid_spec=pltpu.PrefetchScalarGridSpec(
            num_scalar_prefetch=1,
            grid=(tiles,),
            in_specs=[pl.BlockSpec((BLOCKS, width), lambda i, place: (0, 0))]
            + [
                pl.BlockSpec((tile, width), lambda i, place, f=f, at=at: (f + at(i), 0))
                for (_, f), at in zip(pieces, index)
            ]
            + [pl.BlockSpec(memory_space=pl.ANY)] * len(more),
            out_specs=[
                pl.BlockSpec((tile, BLOCKS * width), lambda i, place: (tiles * group + i, 0)),
                pl.BlockSpec((8, 128), lambda i, place: (0, 0)),
            ],
        ),
        out_shape=[
            jax.ShapeDtypeStruct((GROUPS * rows, BLOCKS * width), jnp.bfloat16),
            jax.ShapeDtypeStruct((8, 128), jnp.float32),
        ],
        input_output_aliases={7: 0} if more else {},
        compiler_params=kernel_params(56),
        cost_estimate=cost(16 * rows * width, 4 * BLOCKS * rows * width),
        name="norm_rows",
    )(place, gain, *[p for p, _ in pieces], *more)


SLOT_ROWS = 128


def pack_kernel(table, kv, down_qkv, up_query, up_kv, down_out, up_out, out):
    depth, kv_columns = kv.shape
    rank = ADAPTER_RANK
    out[2 * SLOT_ROWS :, :kv_columns] = kv[: depth // 2]
    out[2 * SLOT_ROWS :, kv_columns:] = kv[depth // 2 :]
    for s in range(2):
        first = s * SLOT_ROWS
        out[first : first + 3 * rank] = down_qkv[s]
        out[first + 3 * rank : first + 4 * rank] = up_query[s]
        out[first + 4 * rank : first + 5 * rank, :kv_columns] = up_kv[s]
        out[first + 4 * rank : first + 5 * rank, kv_columns:] = jnp.zeros(
            (rank, out.shape[1] - kv_columns), jnp.bfloat16
        )
        out[first + 5 * rank : first + 6 * rank] = down_out[s]
        out[first + 6 * rank : first + 7 * rank] = up_out[s]
    shape = (rank, out.shape[1])
    lane = lax.broadcasted_iota(jnp.int32, shape, 1)
    numbers = jnp.zeros(shape, jnp.float32)
    for i in range(8):
        numbers = jnp.where(lane == i, table[i].astype(jnp.float32), numbers)
    for s in range(2):
        out[s * SLOT_ROWS + 7 * rank : (s + 1) * SLOT_ROWS] = numbers.astype(jnp.bfloat16)


def pack_rows(table, kv, *adapters):
    width = adapters[0].shape[2]
    return pl.pallas_call(
        pack_kernel,
        in_specs=[in_smem()] + [in_vmem()] * 6,
        out_specs=in_vmem(),
        out_shape=jax.ShapeDtypeStruct((2 * SLOT_ROWS + kv.shape[0] // 2, width), jnp.bfloat16),
        compiler_params=kernel_params(56),
        cost_estimate=cost(0, 4 * width * (2 * SLOT_ROWS + kv.shape[0] // 2), 0),
        name="pack_rows",
    )(table, kv, *adapters)


def rank_kernel(place, own_table, end_table, storage, x, *refs):
    packed, (low, chosen_own, chosen_end, up, up_kv, down) = refs[:8], refs[8:]
    slots = slot_list(place)
    rank, rows, q_width = ADAPTER_RANK, x.shape[0] // GROUPS, x.shape[1]
    kv_columns, half, core = up_kv.shape[1], q_width // 2, place[0]
    for t, ref in enumerate(packed):
        for s in range(2):
            i, first = 2 * t + s, s * SLOT_ROWS
            for c, columns in ((core, slice(0, half)), (1 - core, slice(half, q_width))):
                down[3 * rank * i : 3 * rank * (i + 1), columns] = ref[
                    first : first + 3 * rank, core_columns(c, half)
                ]
            up[rank * i : rank * (i + 1), :] = ref[first + 3 * rank : first + 4 * rank, :]
            up_kv[rank * i : rank * (i + 1), :] = ref[
                first + 4 * rank : first + 5 * rank, :kv_columns
            ]
    for g, (table, chosen) in enumerate(((own_table, chosen_own), (end_table, chosen_end))):
        terms = lax.dot_general(
            down[...],
            x[g * rows : (g + 1) * rows, :],
            (((1,), (1,)), ((), ())),
            preferred_element_type=jnp.float32,
        )
        row_slots = slots_of_rows(table, storage, rows)
        total = jnp.zeros((3 * rank, rows), jnp.float32)
        for i, slot in enumerate(slots):
            total += jnp.where(row_slots == slot, terms[3 * rank * i : 3 * rank * (i + 1)], 0.0)
        low[:, g * rows : (g + 1) * rows] = total.astype(jnp.bfloat16)
        for j in range(4):
            wanted = storage[table[4 + j]]
            for i, slot in enumerate(slots):

                @pl.when(wanted == slot)
                def _(j=j, i=i, chosen=chosen):
                    first = (i % 2) * SLOT_ROWS
                    chosen[j] = packed[i // 2][first + 5 * rank : first + 7 * rank, :]


def rank_terms(place, own_table, end_table, storage, x, packed, kv_columns):
    rows, width = x.shape[0], x.shape[1] // BLOCKS
    chosen = jax.ShapeDtypeStruct((4, 2 * ADAPTER_RANK, width), jnp.bfloat16)
    up = jax.ShapeDtypeStruct((16 * ADAPTER_RANK, width), jnp.bfloat16)
    up_kv = jax.ShapeDtypeStruct((16 * ADAPTER_RANK, kv_columns), jnp.bfloat16)
    low = jax.ShapeDtypeStruct((3 * ADAPTER_RANK, rows), jnp.bfloat16)
    slots = pl.BlockSpec((2 * SLOT_ROWS, width), lambda i, place: (0, 0))
    whole = lambda shape: pl.BlockSpec(shape, lambda i, place: (0,) * len(shape))
    return pl.pallas_call(
        rank_kernel,
        grid_spec=pltpu.PrefetchScalarGridSpec(
            num_scalar_prefetch=1,
            grid=(1,),
            in_specs=[in_smem()] * 3
            + [pl.BlockSpec((rows, width), lambda i, place: (0, place[11]))]
            + [slots] * 8,
            out_specs=[whole(v.shape) for v in (low, chosen, chosen, up, up_kv)],
            scratch_shapes=[pltpu.VMEM((16 * 3 * ADAPTER_RANK, width), jnp.bfloat16)],
        ),
        out_shape=[low, chosen, chosen, up, up_kv],
        compiler_params=kernel_params(56),
        cost_estimate=cost(
            2 * 16 * 3 * ADAPTER_RANK * rows * width, 2 * width * (rows + 18 * SLOT_ROWS + 256)
        ),
        name="rank_terms",
    )(place, own_table, end_table, storage, x, *packed)


def spread_ranks(place, tables, storage, lows, part, spread):
    rank = ADAPTER_RANK
    rows = spread.shape[0] // GROUPS
    slots = slot_list(place)
    low = sum(v[part * rank : (part + 1) * rank].astype(jnp.float32) for v in lows)
    low = low.astype(jnp.bfloat16).astype(jnp.float32)
    for g, table in enumerate(tables):
        row_slots = slots_of_rows(table, storage, rows)
        mine = low[:, g * rows : (g + 1) * rows]
        wide = jnp.concatenate([jnp.where(row_slots == s, mine, 0.0) for s in slots], axis=0)
        spread[g * rows : (g + 1) * rows, :] = wide.T.astype(jnp.bfloat16)


def project_kernel(is_q, place, own_table, end_table, storage, x, *refs):
    sources, lows, up = refs[:8], refs[8:12], refs[12]
    own, end, spread, held, x_held, sems = refs[-6:]
    rows, width = own.shape[0], x.shape[1] // BLOCKS
    depth = held.shape[0] // 8

    def copies(chunk):
        block = slice(chunk * width, (chunk + 1) * width)
        first = 0 if is_q else 2 * SLOT_ROWS
        return [pltpu.make_async_copy(x.at[:, block], x_held.at[:, block], sems.at[chunk, 2])] + [
            pltpu.make_async_copy(
                sources[2 * chunk + c].at[first:, :],
                held.at[(2 * chunk + c) * depth : (2 * chunk + c + 1) * depth, :],
                sems.at[chunk, c],
            )
            for c in range(2)
        ]

    for chunk in range(BLOCKS):
        for copy in copies(chunk):
            copy.start()
    tables = (own_table, end_table)
    total = None
    if is_q:
        spread_ranks(place, tables, storage, lows, 0, spread)
        low = dot(spread[...], up[...])
    else:
        low = []
        for part in range(2):
            spread_ranks(place, tables, storage, lows, 1 + part, spread)
            low.append(dot(spread[...], up[:, part * WIDE : (part + 1) * WIDE]))
        low = jnp.concatenate(low, axis=1)
    for chunk in range(BLOCKS):
        for copy in copies(chunk):
            copy.wait()
        w = held[2 * chunk * depth : 2 * (chunk + 1) * depth, :]
        if not is_q:
            columns = own.shape[1]
            w = jnp.concatenate(
                [
                    w[c * depth : (c + 1) * depth, h * columns : (h + 1) * columns]
                    for c in range(2)
                    for h in range(2)
                ],
                axis=0,
            )
        term = dot(x_held[:, chunk * width : (chunk + 1) * width], w)
        total = low + term if total is None else total + term
    total = total.astype(jnp.bfloat16)
    own[...] = total[:rows]
    end[:rows] = total[rows:]
    if not is_q:
        chosen_end = refs[13]
        count, each, _ = chosen_end.shape
        for h in range(width // columns):
            for j in range(count):
                first = rows + (count * h + j) * each
                end[first : first + each] = chosen_end[j, :, h * columns : (h + 1) * columns]


def project(place, own_table, end_table, storage, x, sources, lows, up, is_q, chosen_end=None):
    rows, width = x.shape[0], x.shape[1] // BLOCKS
    columns = up.shape[1]
    more = [] if is_q else [chosen_end]
    extra = 0 if is_q else chosen_end.size // columns
    anywhere = pl.BlockSpec(memory_space=pl.ANY)
    return pl.pallas_call(
        functools.partial(project_kernel, is_q),
        in_specs=[in_smem()] * 4 + [anywhere] * 9 + [in_vmem()] * (5 + len(more)),
        out_specs=[in_vmem()] * 2,
        out_shape=[
            jax.ShapeDtypeStruct((rows // GROUPS, columns), jnp.bfloat16),
            jax.ShapeDtypeStruct((rows // GROUPS + extra, columns), jnp.bfloat16),
        ],
        scratch_shapes=[
            pltpu.VMEM((rows, 16 * ADAPTER_RANK), jnp.bfloat16),
            pltpu.VMEM(((8 if is_q else 4) * sources[0].shape[0], width), jnp.bfloat16),
            pltpu.VMEM(x.shape, jnp.bfloat16),
            pltpu.SemaphoreType.DMA((BLOCKS, 3)),
        ],
        compiler_params=kernel_params(56),
        cost_estimate=cost(
            2 * rows * (BLOCKS * width + 256) * columns,
            2 * BLOCKS * width * (rows + columns) + 2 * rows * columns,
        ),
        name="project_query" if is_q else "project_key_value",
    )(place, own_table, end_table, storage, x, *sources, *lows, up, *more)


def take_adapters(out, at_end, chosen_own, kv_back, rows, first):
    rank = ADAPTER_RANK
    count, each, width = chosen_own.shape
    columns = kv_back.shape[1]

    @pl.when(jnp.logical_not(at_end))
    def _():
        for j in range(count):
            out[rank * j : rank * (j + 1), :] = chosen_own[j, first : first + rank, :]

    @pl.when(at_end)
    def _():
        for h in range(width // columns):
            for j in range(count):
                start = rows + (count * h + j) * each + first
                out[rank * j : rank * (j + 1), h * columns : (h + 1) * columns] = kv_back[
                    start : start + rank, :
                ]


def attention_kernel(
    place, table, prefix, pages, own, back, kv_own, kv_back, k_pool, v_pool, q_gain, k_gain,
    cosine, sine, chosen_own, out, cache, low, raw, raw_kv, keys, values, allowed, down,
):
    rows, pool_rows = own.shape[0], k_pool.shape[0]
    page_count = pool_rows // PAGE

    @pl.when(place[6] == 1)
    def _():
        raw[...] = back[...]
        raw_kv[...] = kv_back[:rows]

    @pl.when(place[6] == 0)
    def _():
        raw[...] = own[...]
        raw_kv[...] = kv_own[...]

    take_adapters(down, place[6] == 1, chosen_own, kv_back, rows, 0)

    owner = request_of_rows(table, (rows, 1), 0)
    page = lax.broadcasted_iota(jnp.int32, (1, pool_rows), 1) // PAGE
    seen = jnp.zeros((rows, pool_rows), jnp.int32)
    for j in range(4):
        mine = jnp.zeros((1, pool_rows), jnp.int32)
        for i in range(page_count):
            mine = jnp.where((page == pages[8 * j + i]) & (i < prefix[j]), 1, mine)
        seen = jnp.where(owner == j, mine, seen)
    allowed[:, :pool_rows] = jnp.where(seen > 0, 0.0, HIDDEN)
    row = lax.broadcasted_iota(jnp.int32, (rows, rows), 0)
    column = lax.broadcasted_iota(jnp.int32, (rows, rows), 1)
    same = owner == request_of_rows(table, (1, rows), 1)
    allowed[:, pool_rows:] = jnp.where(same & (column <= row), 0.0, HIDDEN)

    def turned(value, gain):
        value = value.astype(jnp.float32)
        mean_sq = jnp.mean(value * value, axis=1, keepdims=True)
        value = value * lax.rsqrt(mean_sq + epsilon) * gain[...]
        other = pltpu.roll(value, HEAD_SIZE // 2, 1)
        return (value * cosine[...] + other * sine[...]).astype(jnp.bfloat16)

    kv_heads = k_pool.shape[1] // HEAD_SIZE
    q_width = out.shape[1]
    per_key = q_width // HEAD_SIZE // kv_heads
    kv_width = kv_heads * HEAD_SIZE
    cache[:, kv_width:] = raw_kv[:, kv_width:]
    for h in range(kv_heads):
        head = slice(h * HEAD_SIZE, (h + 1) * HEAD_SIZE)
        keys[:pool_rows] = k_pool[:, head]
        values[:pool_rows] = v_pool[:, head]
        k_new = turned(raw_kv[:, head], k_gain)
        keys[pool_rows:] = k_new
        cache[:, head] = k_new
        values[pool_rows:] = raw_kv[:, kv_width + h * HEAD_SIZE : kv_width + (h + 1) * HEAD_SIZE]
        for g in range(per_key):
            place_q = slice((h * per_key + g) * HEAD_SIZE, (h * per_key + g + 1) * HEAD_SIZE)
            query = turned(raw[:, place_q], q_gain)
            scores = lax.dot_general(
                query, keys[...], (((1,), (1,)), ((), ())), preferred_element_type=jnp.float32
            )
            grown = jnp.exp(scores * (1.0 / math.sqrt(HEAD_SIZE)) + allowed[...])
            weights = (grown * (1.0 / jnp.sum(grown, axis=1, keepdims=True))).astype(jnp.bfloat16)
            out[:, place_q] = jnp.dot(
                weights, values[...], preferred_element_type=jnp.float32
            ).astype(jnp.bfloat16)
    terms = lax.dot_general(
        down[...], out[...], (((1,), (1,)), ((), ())), preferred_element_type=jnp.float32
    )
    owner_lane = request_of_rows(table, (1, rows), 1)
    low[...] = sum(
        jnp.where(owner_lane == j, terms[j * ADAPTER_RANK : (j + 1) * ADAPTER_RANK], 0.0)
        for j in range(4)
    )


def attend(place, table, prefix, pages, own, back, kv_own, kv_back, k_pool, v_pool, q_gain, k_gain,
           cosine, sine, chosen_own):
    rows, q_width = own.shape
    kv_width = k_pool.shape[1]
    keys = k_pool.shape[0] + rows
    return pl.pallas_call(
        attention_kernel,
        in_specs=[in_smem()] * 4 + [in_vmem()] * 11,
        out_specs=[in_vmem()] * 3,
        out_shape=[
            jax.ShapeDtypeStruct((rows, q_width), jnp.bfloat16),
            jax.ShapeDtypeStruct((rows, 2 * kv_width), jnp.bfloat16),
            jax.ShapeDtypeStruct((ADAPTER_RANK, rows), jnp.float32),
        ],
        scratch_shapes=[
            pltpu.VMEM(own.shape, jnp.bfloat16),
            pltpu.VMEM(kv_own.shape, jnp.bfloat16),
            pltpu.VMEM((keys, HEAD_SIZE), jnp.bfloat16),
            pltpu.VMEM((keys, HEAD_SIZE), jnp.bfloat16),
            pltpu.VMEM((rows, keys), jnp.float32),
            pltpu.VMEM((4 * ADAPTER_RANK, chosen_own.shape[2]), jnp.bfloat16),
        ],
        compiler_params=kernel_params(56),
        cost_estimate=cost(4 * rows * keys * q_width, 6 * rows * q_width, rows * keys * (q_width // HEAD_SIZE)),
        name="attend",
    )(place, table, prefix, pages, own, back, kv_own, kv_back, k_pool, v_pool, q_gain, k_gain,
      cosine, sine, chosen_own)


def columns_kernel(count, place, attended, *refs):
    sources, rest = refs[: 4 * count], refs[4 * count :]
    low = rest[0] if len(rest) > 2 * BLOCKS + 4 else None
    outs, made, (rows_held, held, sems, out_sems) = rest[-2 * BLOCKS - 4 : -BLOCKS - 4], rest[-BLOCKS - 4 : -4], rest[-4:]
    rows = attended.shape[0]
    at_end = place[6] == 1

    def copies(chunk, end, k):
        pair = sources[4 * chunk + (0 if end else 2) :][:2]
        return [
            pltpu.make_async_copy(
                pair[c].at[place[1] ^ k], held.at[chunk, c, k], sems.at[chunk, k, c]
            )
            for c in range(2)
        ]

    given = pltpu.make_async_copy(attended, rows_held, sems.at[count, 0, 0])
    given.start()
    for end in (True, False):

        @pl.when(at_end if end else jnp.logical_not(at_end))
        def _(end=end):
            for k in (3, 2, 1, 0):
                for chunk in range(count):
                    for copy in copies(chunk, end, k):
                        copy.start()

    given.wait()
    sent = []
    for k in (3, 2, 1, 0):
        for chunk in range(count):
            for copy in copies(chunk, False, k):
                copy.wait()
        w = jnp.concatenate([held[chunk, c, k] for chunk in range(count) for c in range(2)], axis=1)
        made[k][:rows] = dot(rows_held[...], w).astype(jnp.bfloat16)
        if low is not None:
            made[k][rows:, :rows] = low[...].astype(jnp.bfloat16)
            made[k][rows:, rows:] = jnp.zeros(
                (low.shape[0], made[k].shape[1] - rows), jnp.bfloat16
            )
        sent.append(pltpu.make_async_copy(made[k], outs[k], out_sems.at[k]))
        sent[-1].start()
    for copy in sent:
        copy.wait()


def project_columns(place, attended, chunks, low=None, mebibytes=56):
    more = [] if low is None else [low]
    rows = attended.shape[0] + (0 if low is None else low.shape[0])
    depth = chunks[0][0].shape[1]
    width = WIDE * len(chunks)
    return pl.pallas_call(
        functools.partial(columns_kernel, len(chunks)),
        in_specs=[in_smem()]
        + [pl.BlockSpec(memory_space=pl.ANY)] * (1 + 4 * len(chunks))
        + [in_vmem()] * len(more),
        out_specs=[pl.BlockSpec(memory_space=pl.ANY)] * BLOCKS,
        out_shape=[jax.ShapeDtypeStruct((rows, width), jnp.bfloat16)] * BLOCKS,
        scratch_shapes=[pltpu.VMEM((rows, width), jnp.bfloat16)] * BLOCKS
        + [
            pltpu.VMEM(attended.shape, jnp.bfloat16),
            pltpu.VMEM((len(chunks), 2, BLOCKS, depth, HEAD_SIZE), jnp.bfloat16),
            pltpu.SemaphoreType.DMA((len(chunks) + 1, BLOCKS, 2)),
            pltpu.SemaphoreType.DMA((BLOCKS,)),
        ],
        compiler_params=kernel_params(mebibytes),
        cost_estimate=cost(
            2 * rows * depth * BLOCKS * width,
            2 * (rows * depth + depth * BLOCKS * width + rows * BLOCKS * width),
        ),
        name="project_columns",
    )(place, attended, *[w for chunk in chunks for w in chunk], *more)


def sum_kernel(place, table, chosen_own, kv_back, *refs):
    parts, (out, last, up) = refs[:8], refs[8:]
    rank, rows = ADAPTER_RANK, out.shape[0]
    take_adapters(up, place[6] == 1, chosen_own, kv_back, rows, rank)
    low = sum(v[rows:, :rows].astype(jnp.float32) for v in parts[:4])
    low = low.astype(jnp.bfloat16).astype(jnp.float32)
    owner = request_of_rows(table, (1, rows), 1)
    wide = jnp.concatenate([jnp.where(owner == j, low, 0.0) for j in range(4)], axis=0)
    spread = wide.T.astype(jnp.bfloat16)
    core = place[0]
    for i in range(PLANES):
        for h, c in enumerate((core, 1 - core)):
            begin = pl.multiple_of((2 * place[7 + i] + c) * HEAD_SIZE, HEAD_SIZE)
            total = dot(spread, up[:, pl.ds(begin, HEAD_SIZE)])
            if i == PLANES - 1:
                last[:, h * HEAD_SIZE : (h + 1) * HEAD_SIZE] = total
                out[:, pl.ds(begin, HEAD_SIZE)] = total.astype(jnp.bfloat16)
                continue
            first, at = (0, i * WIDE + h * HEAD_SIZE) if i < 2 else (4, h * HEAD_SIZE)
            for v in parts[first : first + 4]:
                total = total + v[:rows, at : at + HEAD_SIZE].astype(jnp.float32)
            out[:, pl.ds(begin, HEAD_SIZE)] = total.astype(jnp.bfloat16)


def sum_columns(place, table, chosen_own, kv_back, parts):
    rows = parts[-1].shape[0]
    width = chosen_own.shape[2]
    return pl.pallas_call(
        sum_kernel,
        in_specs=[in_smem()] * 2 + [in_vmem()] * 10,
        out_specs=[in_vmem()] * 2,
        out_shape=[
            jax.ShapeDtypeStruct((rows, width), jnp.bfloat16),
            jax.ShapeDtypeStruct((rows, WIDE), jnp.float32),
        ],
        scratch_shapes=[pltpu.VMEM((4 * ADAPTER_RANK, width), jnp.bfloat16)],
        compiler_params=kernel_params(56),
        cost_estimate=cost(2 * rows * width * (8 + 4 * ADAPTER_RANK), 12 * rows * width),
        name="sum_columns",
    )(place, table, chosen_own, kv_back, *parts)


def last_columns_kernel(place, given, p0, p1, p2, p3, whole, out):
    del place, whole
    total = given[...] + sum(v[...].astype(jnp.float32) for v in (p0, p1, p2, p3))
    out[...] = total.astype(jnp.bfloat16)


def last_columns(place, given, parts, whole):
    rows = given.shape[0]
    tile = pl.BlockSpec((rows, HEAD_SIZE), lambda i, place: (0, i))
    return pl.pallas_call(
        last_columns_kernel,
        grid_spec=pltpu.PrefetchScalarGridSpec(
            num_scalar_prefetch=1,
            grid=(2,),
            in_specs=[tile] * 5 + [pl.BlockSpec(memory_space=pl.ANY)],
            out_specs=pl.BlockSpec(
                (rows, HEAD_SIZE), lambda i, place: (0, 2 * place[10] + (place[0] ^ i))
            ),
        ),
        out_shape=jax.ShapeDtypeStruct(whole.shape, whole.dtype),
        input_output_aliases={6: 0},
        compiler_params=kernel_params(12),
        cost_estimate=cost(8 * rows * WIDE, 16 * rows * WIDE),
        name="last_columns",
    )(place, given, *parts, whole)


def shards_by_plane(
    hidden_input,
    input_norm_gain,
    query_norm_gain,
    key_norm_gain,
    query_weight,
    key_value_weight,
    output_weight,
    adapter_down_qkv,
    adapter_down_output,
    adapter_up_query,
    adapter_up_key_value,
    adapter_up_output,
    pool,
    lengths,
    cached_prefix_pages,
    prefix_page_table,
    adapter_of_request,
    adapter_storage,
):
    request_index = lax.axis_index("req")
    plane, core = request_index // 2, request_index % 2
    block = lax.axis_index("mlp")
    at_end = (plane == 0) | (plane == PLANES - 1)
    near = plane ^ 1
    inner = [core, block, plane, near, 3 - plane, 3 - near]
    other = jnp.where(at_end, jnp.where(plane == 0, 2, 1), 3 - plane)
    place = jnp.stack(
        inner + [at_end.astype(jnp.int32)]
        + [plane, near, other, 6 - plane - near - other]
        + [sum(i * (p == block ^ k).astype(jnp.int32) for i, p in enumerate(inner[2:])) for k in range(BLOCKS)]
    ).astype(jnp.int32)
    row_count, block_width = hidden_input.shape
    key_value_width = KEY_VALUE_HEADS // BLOCKS * HEAD_SIZE
    key_value_begin = block * key_value_width

    half_rows = row_count // 2
    table = jnp.concatenate([lengths[0], adapter_of_request[0, :, 0]])
    q_2 = along(query_weight, MIDDLE)
    end_hidden = along(hidden_input, INWARD)
    own_1, own_2 = swap_blocks(hidden_input, 1), swap_blocks(hidden_input, 2)
    kv_0 = lax.dynamic_slice_in_dim(key_value_weight, key_value_begin, key_value_width, 2)
    up_kv = lax.dynamic_slice_in_dim(adapter_up_key_value, key_value_begin, key_value_width, 3)
    rest_0 = pack_rows(
        table,
        kv_0.reshape(-1, 2 * key_value_width),
        adapter_down_qkv,
        adapter_up_query,
        up_kv.reshape(up_kv.shape[0], ADAPTER_RANK, 2 * key_value_width),
        adapter_down_output,
        adapter_up_output,
    )
    _, _, token_positions, _ = row_tables(
        lengths[0], cached_prefix_pages[0], prefix_page_table[0], row_count
    )
    half_width = HEAD_SIZE // 2
    inverse_freq = jnp.exp(
        jnp.arange(half_width, dtype=jnp.float32) * (-2.0 / HEAD_SIZE) * math.log(rope_base)
    )
    angles = token_positions.astype(jnp.float32)[:, None] * inverse_freq[None, :]
    cosine, sine = jnp.cos(angles), jnp.sin(angles)
    cosine = jnp.concatenate([cosine, cosine], axis=1)
    sine = jnp.concatenate([-sine, sine], axis=1)
    cached = lax.dynamic_slice_in_dim(pool, key_value_begin, key_value_width, 2)
    k_pool, v_pool = cached[:, 0], cached[:, 1]
    wo_0 = jnp.transpose(output_weight, (1, 0, 2))

    to_1 = jnp.concatenate([end_hidden, own_2[half_rows:]], axis=0)
    to_2 = jnp.concatenate([end_hidden, own_1[:half_rows]], axis=0)
    rest_0, to_1, to_2, q_2, query_later, cosine, sine, k_pool, v_pool, wo_0 = gate(
        [rest_0, to_1, to_2, q_2, query_weight, cosine, sine, k_pool, v_pool, wo_0], []
    )
    rest_1 = along(rest_0, INWARD)
    rest_2 = along(rest_0, MIDDLE)
    from_1, from_2 = swap_blocks(to_1, 1), swap_blocks(to_2, 2)
    q_0x, q_2x, rest_0x = (along(v, CORES) for v in (query_later, q_2, rest_0))

    rest_1, rest_2, from_1, from_2, query_later = gate(
        [rest_1, rest_2, from_1, from_2, query_later], [q_0x, q_2x, rest_0x]
    )
    half_1, half_2 = from_1[:half_rows], from_2[half_rows:row_count]
    end_table = rest_1[7 * ADAPTER_RANK, :8].astype(jnp.int32)
    q_1 = along(query_later, INWARD)
    rest_3 = along(rest_1, MIDDLE)
    end_3, end_4 = swap_blocks(half_1, 2), swap_blocks(half_2, 1)

    gain = input_norm_gain.astype(jnp.float32).reshape(BLOCKS, block_width)
    own_pieces = [(hidden_input, 0), (own_1, 0), (own_2, 0), (from_2, 4), (from_1, 4)]
    end_pieces = [(end_hidden, 0), (from_1, 0), (from_2, 0), (end_3, 0), (end_4, 0)]
    x, own_done = norm_rows(place, gain, own_pieces, 0, None)
    x, end_done = norm_rows(place, gain, end_pieces, 1, x)
    q_1, rest_1, rest_2, rest_3, wo_0 = gate([q_1, rest_1, rest_2, rest_3, wo_0], [end_done])
    q_3 = along(q_1, MIDDLE)
    wo_1 = along(wo_0, NEAR)
    rest_1x, rest_2x, rest_3x = (along(v, CORES) for v in (rest_1, rest_2, rest_3))
    q_1x = along(q_1, CORES)

    packed = [rest_0, rest_1, rest_2, rest_3, rest_0x, rest_1x, rest_2x, rest_3x]
    low, chosen_own, chosen_end, up, up_kv = rank_terms(
        place, table, end_table, adapter_storage, x, packed, 2 * key_value_width
    )
    lows = [low] + to_blocks([low] * BLOCKS)

    kv_own, kv_end = project(
        place,
        table,
        end_table,
        adapter_storage,
        x,
        [v for pair in zip(packed[:4], packed[4:]) for v in pair],
        lows,
        up_kv,
        False,
        chosen_end,
    )
    kv_back = along(kv_end, OUTWARD)
    q_3, wo_0, wo_1 = gate([q_3, wo_0, wo_1], [kv_own])
    q_3x = along(q_3, CORES)
    wo_mid1, wo_mid2 = along(wo_0, MIDDLE), along(wo_1, MIDDLE)
    raw_own, raw_end = project(
        place,
        table,
        end_table,
        adapter_storage,
        x,
        [query_weight, q_0x, q_1, q_1x, q_2, q_2x, q_3, q_3x],
        lows,
        up,
        True,
    )
    raw_end, kv_back = gate([raw_end, kv_back], [])
    raw_back = along(raw_end, OUTWARD)
    wo_0x, wo_1x = along(wo_0, CORES), along(wo_1, CORES)
    wo_mid1, raw_back = gate([wo_mid1, raw_back], [wo_0x, wo_1x])
    wo_out2 = along(wo_mid1, OUTWARD)

    attended, cache, low_out = attend(
        place,
        table,
        cached_prefix_pages[0],
        prefix_page_table[0].reshape(-1),
        raw_own,
        raw_back,
        kv_own,
        kv_back,
        k_pool,
        v_pool,
        query_norm_gain.astype(jnp.float32)[None, :],
        key_norm_gain.astype(jnp.float32)[None, :],
        cosine,
        sine,
        chosen_own,
    )
    new_cache = cache.reshape(row_count, 2, key_value_width)

    attended, wo_mid2 = gate([attended, wo_mid2], [])
    wo_out3 = along(wo_mid2, OUTWARD)
    near_parts = project_columns(
        place, attended, [(wo_0, wo_0x, wo_0, wo_0x), (wo_1, wo_1x, wo_1, wo_1x)], low_out
    )
    parts = [near_parts[0]] + to_blocks(near_parts)
    (wo_out2,) = gate([wo_out2], near_parts[:1])
    mid_parts = project_columns(
        place, attended, [(wo_out2, along(wo_out2, CORES), wo_mid1, along(wo_mid1, CORES))]
    )
    parts += [mid_parts[0]] + to_blocks(mid_parts)
    (wo_out3,) = gate([wo_out3], parts[:5], 1)
    last_parts = project_columns(
        place,
        attended,
        [(wo_out3, along(wo_out3, CORES), wo_mid2, along(wo_mid2, CORES))],
        mebibytes=12,
    )
    parts += [last_parts[0]] + to_blocks(last_parts)
    whole, given = sum_columns(place, table, chosen_own, kv_back, parts[:8])
    attention_update = last_columns(place, given, parts[8:], whole)
    return (attention_update, new_cache)


def solution(mesh):
    return jax.shard_map(
        shards_by_plane if planes_fit(mesh) else shards,
        mesh=mesh,
        in_specs=(
            P("req", "mlp"),
            P(),
            P(),
            P(),
            P("req", "mlp"),
            P("req", None, None),
            P("mlp", None, "req"),
            P("req", None, "mlp"),
            P("req", None, "mlp"),
            P("req", None, "mlp"),
            P("req", None, None, None),
            P("req", None, "mlp"),
            P("req", None, None),
            P("req", None),
            P("req", None),
            P("req", None, None),
            P("req", None, None),
            P(),
        ),
        out_specs=(P("req", "mlp"), P("req", None, "mlp")),
        check_vma=False,
    )
```
